32 devices in a mesh: tmpl: 4 (over y, x), freq: 8 (over z, core).
Axes of the slice: x: 2, y: 2, z: 4, core: 2. Of those that a mesh axis runs over, the one named last changes fastest.
Arguments:
- strain: float32 [64, 524288], P('tmpl', 'freq'), may hold values from -6 to 6
- psd: float32 [512, 512], P(None, 'freq'), may hold values from 0.1 to 10
- templates: bfloat16 [1024, 2, 512, 512], P('tmpl', None, 'freq'), may hold values from -0.0234375 to 0.0234375
- cutoffs: int32 [1024], P('tmpl'), may hold values from 1 to 512, as said below
- lags: int32 [16], replicated, may hold values from 0 to 524287
Outputs:
- intersections: float32 [64, 32, 1024], P('freq', None, 'tmpl')
The draws below stay inside these ranges and needn't reach their ends.
Inputs may be any that keep to these rules, and one draw needn't show every extreme that they name: `cutoffs`: the cutoff counts do not increase along the template index.
All inputs are finite; a program needn't handle non-finite values.
Results may differ from the reference program's by a relative error of at most 0.004.
Values may be sent and summed in bfloat16 or wider, within the bound.
No kernel may reach another device: no remote copies, remote signals or barrier semaphores. Data moves between devices by JAX's collectives and lax.ppermute only.
A program may use at most 192 MiB of HBM per device.

```python
import math
import jax
import jax.numpy as jnp
from jax import lax

A = 512
B = 1024
LEN = 524288
NB = 512
LAGS = 16
SEG = 64
TMPL = 1024


def draw_cutoffs(key, part):
    key_one = jax.random.fold_in(key, 11)
    key_two = jax.random.fold_in(key, 23)
    first_draw = jax.random.randint(key_one, (TMPL,), 1, NB + 1)
    second_draw = jax.random.randint(key_two, (TMPL,), 1, NB + 1)
    lowest = jnp.minimum(first_draw, second_draw)
    ordered = -jnp.sort(-lowest)
    ordered = ordered.at[0].set(NB).at[TMPL - 1].set(1)
    return ordered.astype(jnp.int32)


def plant(array, own_key, low, top_value):
    longest = array.shape.index(max(array.shape))
    spots = []
    for shift in (0, 1):
        where = [jax.random.randint(jax.random.fold_in(own_key, axis), (), 0, length) for axis, length in enumerate(array.shape)]
        where[longest] = (where[longest] + shift) % array.shape[longest]
        spots.append(tuple(where))
    return array.at[spots[0]].set(low).at[spots[1]].set(top_value)


def steps_of(own_key, shape, shards, smallest, top_value):
    def one(dim, parts):
        draws = jax.random.uniform(jax.random.fold_in(jax.random.fold_in(own_key, 6), dim), (parts,), jnp.float32, smallest / len(shards), top_value / len(shards))
        return jnp.repeat(jnp.exp(draws), shape[dim] // parts).reshape((-1,) + (1,) * (len(shape) - dim - 1))

    factor_of = one(*shards[0])
    for cut in shards[1:]:
        factor_of = factor_of * one(*cut)
    return factor_of


def noise(key, shape, width, limit, cuts=(), held_as=jnp.bfloat16):
    drawn = jax.random.normal(key, shape, jnp.float32) * width
    if len(cuts) > 0:
        drawn = steps_of(key, shape, cuts, -0.22, 0.18) * drawn
    return jnp.clip(drawn, min=-limit, max=limit).astype(held_as)


def setup_inputs(seed: int = 0) -> dict:
    seeds = jax.random.split(jax.random.key(seed), 6)
    return {
        "strain": noise(seeds[0], (SEG, LEN), 1.0, 6.0, ((0, 4), (1, 8)), jnp.float32),
        "psd": jnp.clip(jnp.exp(math.log(10.0) - 4.6051702 * jax.random.uniform(seeds[1], (NB, A), jnp.float32) ** steps_of(seeds[1], (NB, A), ((1, 8),), -0.2, 0.2)), 0.1, 10.0),
        "templates": noise(seeds[2], (TMPL, 2, NB, A), (NB * A // 4) ** -0.5, 0.0234375, ((0, 4), (2, 8))),
        "cutoffs": draw_cutoffs(jax.random.fold_in(seeds[5], 71), 0),
        "lags": plant(jax.random.randint(seeds[4], (LAGS,), 0, LEN), jax.random.fold_in(seeds[4], 1), 0, LEN - 1).astype(jnp.int32),
    }


two_pi = 2.0 * math.pi

def reference(strain, psd, templates, cutoffs, lags):
    spectrum = jnp.fft.rfft(strain, axis=1)[:, :LEN // 2]
    amplitude = jnp.sqrt(LEN * psd).reshape(1, NB * A)
    real_part = (jnp.real(spectrum) / amplitude).reshape(SEG, NB, A)
    imag_part = (jnp.imag(spectrum) / amplitude).reshape(SEG, NB, A)
    whitened = jnp.stack([real_part, imag_part], axis=1).astype(jnp.bfloat16)
    per_span = min(8, NB)
    span_total = NB // per_span
    position = jnp.arange(A, dtype=jnp.int32)

    def one_span(running, span_idx):
        offset = (span_idx * per_span).astype(jnp.int32)
        block_ids = offset + jnp.arange(per_span, dtype=jnp.int32)
        data_part = lax.dynamic_slice_in_dim(whitened, offset, per_span, 2).astype(jnp.float32)
        tmpl_part = lax.dynamic_slice_in_dim(templates, offset, per_span, 2)
        phase_int = (A * (lags[:, None] * block_ids[None, :] % B))[:, :, None] + (lags[:, None] * position[None, :] % LEN)[:, None, :]
        phase_angle = (phase_int % LEN).astype(jnp.float32) * (two_pi / LEN)
        lag_cos = jnp.cos(phase_angle)[None]
        lag_sin = jnp.sin(phase_angle)[None]
        data_real = data_part[:, 0][:, None]
        data_imag = data_part[:, 1][:, None]
        real_q = (data_real * lag_cos - data_imag * lag_sin).astype(jnp.bfloat16)
        imag_q = (data_real * lag_sin + data_imag * lag_cos).astype(jnp.bfloat16)
        real_rows = jnp.stack([real_q, imag_q], axis=2)
        imag_rows = jnp.stack([imag_q, -real_q], axis=2)
        lhs_rows = jnp.stack([real_rows, imag_rows], axis=1).reshape(SEG * 2 * LAGS, 2 * per_span * A).astype(jnp.float32)
        keep_mask = (block_ids[None, :] < cutoffs[:, None]).astype(jnp.bfloat16)
        masked = (tmpl_part * keep_mask[:, None, :, None]).reshape(TMPL, 2 * per_span * A).astype(jnp.float32)
        running = running + jnp.dot(lhs_rows, masked.T, precision=lax.Precision.HIGHEST)
        return (running, None)
    start_sum = jnp.zeros((SEG * 2 * LAGS, TMPL), jnp.float32)
    running, unused = lax.scan(one_span, start_sum, jnp.arange(span_total, dtype=jnp.int32))
    return running.reshape(SEG, 2 * LAGS, TMPL)
```

```python
import math

import jax
import jax.numpy as jnp
import ml_dtypes
import numpy as np
from jax import lax
from jax.experimental import pallas as pl
from jax.experimental.pallas import tpu as pltpu
from jax.sharding import PartitionSpec as P

A = 512
B = 1024
LEN = 524288
NB = 512
HALF = A // 2

STRAIN_SCALE = 8192.0
COEF_SCALE = 16.0

two_pi = 2.0 * math.pi


def cos_sin_table(row_ids, col_ids, modulus):
    product = row_ids[:, None] * col_ids[None, :] % modulus
    phase_angle = product.astype(jnp.float32) * (two_pi / modulus)
    return (jnp.cos(phase_angle), jnp.sin(phase_angle))


def split_const(table):
    high = table.astype(ml_dtypes.bfloat16)
    low = (table - high.astype(np.float64)).astype(ml_dtypes.bfloat16)
    return high, low


def first_table():
    angle = two_pi * (np.outer(np.arange(HALF), np.arange(A)) % A) / A
    table = np.concatenate([np.cos(angle), -np.sin(angle)], axis=0)
    table[HALF] = 1.0 - 2.0 * (np.arange(A) % 2)
    return split_const(table)


def second_tables():
    angle = two_pi * (np.outer(np.arange(528), np.arange(B)) % B) / B
    return split_const(np.cos(angle)) + split_const(np.sin(angle))


def twist_tables():
    angle = two_pi * np.outer(np.arange(HALF), np.arange(B)) / LEN
    edge = two_pi * HALF * np.arange(B)[None, :] / LEN
    return (
        np.cos(angle).astype(np.float32),
        np.sin(angle).astype(np.float32),
        np.cos(edge).astype(np.float32),
        np.sin(edge).astype(np.float32),
    )


def mirror_table():
    table = np.zeros((HALF, HALF), np.float32)
    table[0, 0] = 1.0
    table[np.arange(1, HALF), HALF - np.arange(1, HALF)] = 1.0
    return table


def split_parts(value):
    high = value.astype(jnp.bfloat16)
    low = (value - high.astype(jnp.float32)).astype(jnp.bfloat16)
    return high, low


def dot_nn(lhs, rhs):
    return lax.dot_general(lhs, rhs, (((1,), (0,)), ((), ())), preferred_element_type=jnp.float32)


def dot_nt(lhs, rhs):
    return lax.dot_general(lhs, rhs, (((1,), (1,)), ((), ())), preferred_element_type=jnp.float32)


def first_kernel(x_ref, high_ref, low_ref, out_ref):
    parts = x_ref.shape[0]
    pair = x_ref.shape[1]
    columns = []
    for s in range(pair):
        columns.append(jnp.concatenate([x_ref[f, s] for f in range(parts)], axis=0))
    value = jnp.concatenate(columns, axis=1)
    high, low = split_parts(value)
    result = dot_nn(high_ref[...], high) + dot_nn(high_ref[...], low) + dot_nn(low_ref[...], high)
    width = x_ref.shape[3]
    for s in range(pair):
        out_ref[s] = result[:, s * width : (s + 1) * width]


def first_section(received, tables):
    parts, segs, rows, width = received.shape
    pair = 2
    return pl.pallas_call(
        first_kernel,
        grid=(segs // pair,),
        in_specs=[
            pl.BlockSpec((parts, pair, rows, width), lambda i: (0, i, 0, 0)),
            pl.BlockSpec((A, A), lambda i: (0, 0)),
            pl.BlockSpec((A, A), lambda i: (0, 0)),
        ],
        out_specs=pl.BlockSpec((pair, A, width), lambda i: (i, 0, 0)),
        out_shape=jax.ShapeDtypeStruct((segs, A, width), jnp.float32),
        compiler_params=pltpu.CompilerParams(vmem_limit_bytes=40 * 2**20),
        cost_estimate=pl.CostEstimate(
            flops=2 * 3 * segs * A * A * width, bytes_accessed=segs * A * width * 8, transcendentals=0
        ),
        name="first_section",
    )(received, *tables)


def second_kernel(
    y_ref, tc_ref, ts_ref, ec_ref, es_ref, ch_ref, cl_ref, sh_ref, sl_ref, wa_ref, wm_ref, q_ref, out_ref
):
    parts = y_ref.shape[0]
    joined = jnp.concatenate([y_ref[f, 0] for f in range(parts)], axis=1)
    real_raw = joined[:HALF]
    imag_raw = joined[HALF:]
    row_ids = lax.broadcasted_iota(jnp.int32, (HALF, B), 0)
    imag_in = jnp.where(row_ids == 0, 0.0, imag_raw)
    twist_cos = tc_ref[...]
    twist_sin = ts_ref[...]
    real_u = real_raw * twist_cos + imag_in * twist_sin
    imag_u = imag_in * twist_cos - real_raw * twist_sin
    edge = imag_raw[0:1]
    edge_rows = jnp.where(
        lax.broadcasted_iota(jnp.int32, (16, B), 0) == 0,
        edge * ec_ref[...],
        jnp.where(lax.broadcasted_iota(jnp.int32, (16, B), 0) == 1, -edge * es_ref[...], 0.0),
    )
    u_high, u_low = split_parts(jnp.concatenate([real_u, imag_u], axis=0))
    e_high, e_low = split_parts(edge_rows)

    def three(high_ref, low_ref, high, low):
        return (
            dot_nt(high_ref[...], high) + dot_nt(high_ref[...], low) + dot_nt(low_ref[...], high)
        )

    by_cos = three(ch_ref, cl_ref, u_high, u_low)
    by_sin = three(sh_ref, sl_ref, u_high, u_low)
    edge_cos = three(ch_ref, cl_ref, e_high, e_low)[:NB]
    edge_sin = three(sh_ref, sl_ref, e_high, e_low)[:NB]
    white = wa_ref[...]
    real_out = ((by_cos[:NB, :HALF] + by_sin[:NB, HALF:]) * white).astype(jnp.bfloat16)
    imag_out = ((by_cos[:NB, HALF:] - by_sin[:NB, :HALF]) * white).astype(jnp.bfloat16)
    next_cos = by_cos[1 : NB + 1]
    next_sin = by_sin[1 : NB + 1]
    lane = lax.broadcasted_iota(jnp.int32, (NB, HALF), 1)
    real_edge = edge_cos[:, 0:1] + edge_sin[:, 1:2]
    imag_edge = edge_cos[:, 1:2] - edge_sin[:, 0:1]
    real_far = jnp.where(lane == 0, real_edge, next_cos[:, :HALF] - next_sin[:, HALF:])
    imag_far = jnp.where(lane == 0, imag_edge, -next_cos[:, HALF:] - next_sin[:, :HALF])
    white_far = wm_ref[...]
    order = q_ref[...]
    real_far = dot_nn((real_far * white_far).astype(jnp.bfloat16), order).astype(jnp.bfloat16)
    imag_far = dot_nn((imag_far * white_far).astype(jnp.bfloat16), order).astype(jnp.bfloat16)
    rows = NB // parts
    for f in range(parts):
        here = slice(f * rows, (f + 1) * rows)
        out_ref[f, 0, 0, :, :HALF] = real_out[here]
        out_ref[f, 0, 0, :, HALF:] = real_far[here]
        out_ref[f, 0, 1, :, :HALF] = imag_out[here]
        out_ref[f, 0, 1, :, HALF:] = imag_far[here]


def second_section(received, tables, white, white_far):
    parts, segs, rows, width = received.shape
    twists, seconds, order = tables

    def whole(array):
        return pl.BlockSpec(array.shape, lambda i: (0,) * array.ndim)

    fixed = (*twists, *seconds, white, white_far, order)
    return pl.pallas_call(
        second_kernel,
        grid=(segs,),
        in_specs=[pl.BlockSpec((parts, 1, rows, width), lambda i: (0, i, 0, 0))]
        + [whole(array) for array in fixed],
        out_specs=pl.BlockSpec((parts, 1, 2, NB // parts, A), lambda i: (0, i, 0, 0, 0)),
        out_shape=jax.ShapeDtypeStruct((parts, segs, 2, NB // parts, A), jnp.bfloat16),
        compiler_params=pltpu.CompilerParams(vmem_limit_bytes=60 * 2**20),
        cost_estimate=pl.CostEstimate(
            flops=2 * 6 * segs * 528 * B * A, bytes_accessed=segs * A * B * 6, transcendentals=0
        ),
        name="second_section",
    )(received, *fixed)


def lag_kernel(w_ref, t_ref, c_ref, s_ref, out_ref, acc_ref, p_ref, wf_ref):
    segs, _, blocks, _ = w_ref.shape
    quads = t_ref.shape[0]
    per_quad = blocks // quads
    lag_total = c_ref.shape[1]
    tmpl = out_ref.shape[2]
    step = pl.program_id(0)

    @pl.when(step == 0)
    def _():
        acc_ref[...] = jnp.zeros_like(acc_ref)

    unroll = 8

    @pl.loop(0, segs // unroll)
    def _(group):
        some = pl.ds(pl.multiple_of(group * unroll, unroll), unroll)
        for part in range(2):
            value = w_ref[some, part].astype(jnp.float32)
            wf_ref[part, :, some, :] = jnp.swapaxes(value, 0, 1)

    @pl.loop(0, quads)
    def _(quad):
        for jj in range(per_quad):
            block = quad * per_quad + jj
            for chunk in range(A // 128):
                lanes = slice(chunk * 128, (chunk + 1) * 128)
                lag_cos = c_ref[block, :, lanes]
                lag_sin = s_ref[block, :, lanes]
                out_lanes = slice(jj * A + chunk * 128, jj * A + (chunk + 1) * 128)

                @pl.loop(0, segs // unroll)
                def _(group):
                    some = pl.ds(pl.multiple_of(group * unroll, unroll), unroll)
                    reals = wf_ref[0, block, some, lanes]
                    imags = wf_ref[1, block, some, lanes]
                    for inner in range(unroll):
                        real = reals[inner : inner + 1]
                        imag = imags[inner : inner + 1]
                        first_row = (group * unroll + inner) * lag_total
                        rows = pl.ds(pl.multiple_of(first_row, lag_total), lag_total)
                        p_ref[0, rows, out_lanes] = (real * lag_cos - imag * lag_sin).astype(
                            jnp.bfloat16
                        )
                        p_ref[1, rows, out_lanes] = (real * lag_sin + imag * lag_cos).astype(
                            jnp.bfloat16
                        )

        for part in range(2):
            acc_ref[part] += dot_nt(p_ref[part], t_ref[quad])

    @pl.when(step == pl.num_programs(0) - 1)
    def _():
        shape = (segs, lag_total, tmpl)
        out_ref[:, :lag_total] = (acc_ref[0, :, :tmpl] + acc_ref[1, :, tmpl:]).reshape(shape)
        out_ref[:, lag_total:] = (acc_ref[1, :, :tmpl] - acc_ref[0, :, tmpl:]).reshape(shape)


def lag_products(data, laid, lag_cos, lag_sin):
    segs, _, blocks, _ = data.shape
    quads, tmpl2, depth = laid.shape
    per_quad = depth // A
    per_step = min(16, blocks)
    steps = blocks // per_step
    lag_total = lag_cos.shape[1]
    return pl.pallas_call(
        lag_kernel,
        grid=(steps,),
        in_specs=[
            pl.BlockSpec((segs, 2, per_step, A), lambda i: (0, 0, i, 0)),
            pl.BlockSpec((per_step // per_quad, tmpl2, depth), lambda i: (i, 0, 0)),
            pl.BlockSpec((per_step, lag_total, A), lambda i: (i, 0, 0)),
            pl.BlockSpec((per_step, lag_total, A), lambda i: (i, 0, 0)),
        ],
        out_specs=pl.BlockSpec((segs, 2 * lag_total, tmpl2 // 2), lambda i: (0, 0, 0)),
        out_shape=jax.ShapeDtypeStruct((segs, 2 * lag_total, tmpl2 // 2), jnp.float32),
        scratch_shapes=[
            pltpu.VMEM((2, segs * lag_total, tmpl2), jnp.float32),
            pltpu.VMEM((2, segs * lag_total, depth), jnp.bfloat16),
            pltpu.VMEM((2, per_step, segs, A), jnp.float32),
        ],
        compiler_params=pltpu.CompilerParams(vmem_limit_bytes=60 * 2**20),
        cost_estimate=pl.CostEstimate(
            flops=4 * segs * lag_total * tmpl2 * blocks * A,
            bytes_accessed=blocks * A * (tmpl2 * 2 + segs * 4),
            transcendentals=0,
        ),
        name="lag_products",
    )(data, laid, lag_cos, lag_sin)


def general_transform(strain, psd):
    freq_count = lax.axis_size("freq")
    freq_index = lax.axis_index("freq")
    seg_local = strain.shape[0]
    step_time = B // freq_count
    highest = lax.Precision.HIGHEST
    first_cos, first_sin = cos_sin_table(
        jnp.arange(A, dtype=jnp.int32), jnp.arange(A, dtype=jnp.int32), A
    )
    table = jnp.concatenate([first_cos, -first_sin], axis=0)
    time_ids = freq_index * step_time + jnp.arange(step_time, dtype=jnp.int32)
    twist_cos, twist_sin = cos_sin_table(jnp.arange(A, dtype=jnp.int32), time_ids, LEN)
    slab_blocks = strain.reshape(seg_local, A // freq_count, B)
    both_parts = jnp.einsum(
        "kn,snb->skb",
        table,
        lax.all_to_all(slab_blocks, "freq", split_axis=2, concat_axis=1, tiled=True),
        precision=highest,
    )
    real_part = both_parts[:, :A]
    imag_part = both_parts[:, A:]
    second_cos, second_sin = cos_sin_table(
        jnp.arange(B, dtype=jnp.int32), jnp.arange(NB, dtype=jnp.int32), B
    )
    rotation = jnp.concatenate(
        [
            jnp.concatenate([second_cos, -second_sin], axis=1),
            jnp.concatenate([second_sin, second_cos], axis=1),
        ],
        axis=0,
    )
    amplitude = jnp.sqrt(LEN * psd)
    real_in = lax.all_to_all(
        real_part * twist_cos + imag_part * twist_sin, "freq", split_axis=1, concat_axis=2, tiled=True
    )
    imag_in = lax.all_to_all(
        imag_part * twist_cos - real_part * twist_sin, "freq", split_axis=1, concat_axis=2, tiled=True
    )
    joined = jnp.concatenate([real_in, imag_in], axis=2)
    both_out = jnp.einsum("spc,cm->smp", joined, rotation, precision=highest)
    both_out = both_out.reshape(joined.shape[0], 2, NB, joined.shape[1])
    whitened = (both_out / amplitude).astype(jnp.bfloat16)
    return lax.all_to_all(whitened, "freq", split_axis=2, concat_axis=3, tiled=True)


def sliced_transform(strain, tables, white, white_far):
    freq_count = lax.axis_size("freq")
    seg_local = strain.shape[0]
    first, second = tables
    width = B // freq_count
    sent = (strain * STRAIN_SCALE).astype(jnp.float16)
    sent = sent.reshape(seg_local, A // freq_count, freq_count, width).transpose(2, 0, 1, 3)
    received = lax.all_to_all(sent, "freq", split_axis=0, concat_axis=0, tiled=True)
    received = received.astype(jnp.float32) * (1.0 / STRAIN_SCALE)
    coefs = first_section(received, first)
    sent = (coefs * COEF_SCALE).astype(jnp.float16).reshape(freq_count, seg_local // freq_count, A, width)
    received = lax.all_to_all(sent, "freq", split_axis=0, concat_axis=0, tiled=True)
    received = received.astype(jnp.float32) * (1.0 / COEF_SCALE)
    whitened = second_section(received, second, white, white_far)
    local_data = lax.all_to_all(whitened, "freq", split_axis=0, concat_axis=0, tiled=True)
    return local_data.reshape(seg_local, 2, NB // freq_count, A)


def on_device(strain, psd, templates, cutoffs, lags):
    freq_count = lax.axis_size("freq")
    freq_index = lax.axis_index("freq")
    seg_local = strain.shape[0]
    tmpl_local = templates.shape[0]
    blocks_here = templates.shape[2]
    lag_total = lags.shape[0]
    first_block = freq_index * blocks_here
    block_ids = first_block + jnp.arange(blocks_here, dtype=jnp.int32)

    per_quad = min(4, blocks_here)
    quads = blocks_here // per_quad
    keep = block_ids[None, :] < cutoffs[:, None]
    masked = jnp.where(keep[:, None, :, None], templates, jnp.bfloat16(0))
    laid = masked.reshape(tmpl_local, 2, quads, per_quad, A).transpose(2, 1, 0, 3, 4)
    laid = laid.reshape(quads, 2 * tmpl_local, per_quad * A)

    block_cos, block_sin = cos_sin_table(block_ids, lags % B, B)
    place = lags[:, None] * jnp.arange(A, dtype=jnp.int32)[None, :] % LEN
    place_angle = place.astype(jnp.float32) * (two_pi / LEN)
    place_cos = jnp.cos(place_angle)[None]
    place_sin = jnp.sin(place_angle)[None]
    block_cos = block_cos[:, :, None]
    block_sin = block_sin[:, :, None]
    lag_cos = block_cos * place_cos - block_sin * place_sin
    lag_sin = block_sin * place_cos + block_cos * place_sin

    sliced = seg_local % freq_count == 0 and (NB // freq_count) % 16 == 0 and B // freq_count == 128
    if not sliced:
        data = lax.all_gather(general_transform(strain, psd), "tmpl", axis=0, tiled=True)
        sums = lag_products(data, laid, lag_cos, lag_sin)
        return lax.psum_scatter(sums, "freq", scatter_dimension=0, tiled=True)

    order = mirror_table()
    psd_all = lax.all_gather(psd, "freq", axis=1, tiled=True)
    psd_far = jnp.dot(psd_all[:, HALF:], order.T, precision=lax.Precision.HIGHEST)
    white = lax.rsqrt(LEN * psd_all[:, :HALF])
    white_far = lax.rsqrt(LEN * psd_far)
    tables = (first_table(), (twist_tables(), second_tables(), order.astype(ml_dtypes.bfloat16)))

    group_total = seg_local // freq_count
    seg_out = seg_local * lax.axis_size("tmpl") // freq_count
    owners = seg_local // seg_out
    by_owner = strain.reshape(owners, group_total, seg_out // group_total, strain.shape[1])
    outputs = []
    for group in range(group_total):
        part = by_owner[:, group].reshape(seg_local // group_total, strain.shape[1])
        whitened = sliced_transform(part, tables, white, white_far)
        data = lax.all_gather(whitened, "tmpl", axis=0, tiled=True)
        sums = lag_products(data, laid, lag_cos, lag_sin)
        outputs.append(lax.psum_scatter(sums, "freq", scatter_dimension=0, tiled=True))
    return jnp.concatenate(outputs, axis=0)


def solution(mesh):
    placed = (P("tmpl", "freq"), P(None, "freq"), P("tmpl", None, "freq", None), P("tmpl"), P())
    return jax.shard_map(
        on_device, mesh=mesh, in_specs=placed, out_specs=P("freq", None, "tmpl"), check_vma=False
    )
```

```python
import math

import jax
import jax.numpy as jnp
import ml_dtypes
import numpy as np
from jax import lax
from jax.experimental import pallas as pl
from jax.experimental.pallas import tpu as pltpu
from jax.sharding import PartitionSpec as P

A = 512
B = 1024
LEN = 524288
NB = 512
HALF = A // 2

STRAIN_SCALE = 8192.0
COEF_SCALE = 16.0

two_pi = 2.0 * math.pi


def cos_sin_table(row_ids, col_ids, modulus):
    product = row_ids[:, None] * col_ids[None, :] % modulus
    phase_angle = product.astype(jnp.float32) * (two_pi / modulus)
    return (jnp.cos(phase_angle), jnp.sin(phase_angle))


def split_const(table):
    high = table.astype(ml_dtypes.bfloat16)
    low = (table - high.astype(np.float64)).astype(ml_dtypes.bfloat16)
    return high, low


def first_table():
    angle = two_pi * (np.outer(np.arange(HALF), np.arange(A)) % A) / A
    table = np.concatenate([np.cos(angle), -np.sin(angle)], axis=0)
    table[HALF] = 1.0 - 2.0 * (np.arange(A) % 2)
    return split_const(table)


def second_tables():
    angle = two_pi * (np.outer(np.arange(528), np.arange(B)) % B) / B
    return split_const(np.cos(angle)) + split_const(np.sin(angle))


def twist_tables():
    angle = two_pi * np.outer(np.arange(HALF), np.arange(B)) / LEN
    edge = two_pi * HALF * np.arange(B)[None, :] / LEN
    return (
        np.cos(angle).astype(np.float32),
        np.sin(angle).astype(np.float32),
        np.cos(edge).astype(np.float32),
        np.sin(edge).astype(np.float32),
    )


def mirror_table():
    table = np.zeros((HALF, HALF), np.float32)
    table[0, 0] = 1.0
    table[np.arange(1, HALF), HALF - np.arange(1, HALF)] = 1.0
    return table


def split_parts(value):
    high = value.astype(jnp.bfloat16)
    low = (value - high.astype(jnp.float32)).astype(jnp.bfloat16)
    return high, low


def dot_nn(lhs, rhs):
    return lax.dot_general(lhs, rhs, (((1,), (0,)), ((), ())), preferred_element_type=jnp.float32)


def dot_nt(lhs, rhs):
    return lax.dot_general(lhs, rhs, (((1,), (1,)), ((), ())), preferred_element_type=jnp.float32)


def first_kernel(x_ref, high_ref, low_ref, out_ref):
    parts = x_ref.shape[0]
    pair = x_ref.shape[1]
    columns = []
    for s in range(pair):
        columns.append(jnp.concatenate([x_ref[f, s] for f in range(parts)], axis=0))
    value = jnp.concatenate(columns, axis=1)
    high, low = split_parts(value)
    result = dot_nn(high_ref[...], high) + dot_nn(high_ref[...], low) + dot_nn(low_ref[...], high)
    width = x_ref.shape[3]
    for s in range(pair):
        out_ref[s] = result[:, s * width : (s + 1) * width]


def first_section(received, tables):
    parts, segs, rows, width = received.shape
    pair = 2
    return pl.pallas_call(
        first_kernel,
        grid=(segs // pair,),
        in_specs=[
            pl.BlockSpec((parts, pair, rows, width), lambda i: (0, i, 0, 0)),
            pl.BlockSpec((A, A), lambda i: (0, 0)),
            pl.BlockSpec((A, A), lambda i: (0, 0)),
        ],
        out_specs=pl.BlockSpec((pair, A, width), lambda i: (i, 0, 0)),
        out_shape=jax.ShapeDtypeStruct((segs, A, width), jnp.float32),
        compiler_params=pltpu.CompilerParams(vmem_limit_bytes=40 * 2**20),
        cost_estimate=pl.CostEstimate(
            flops=2 * 3 * segs * A * A * width, bytes_accessed=segs * A * width * 8, transcendentals=0
        ),
        name="first_section",
    )(received, *tables)


def second_kernel(
    y_ref, tc_ref, ts_ref, ec_ref, es_ref, ch_ref, cl_ref, sh_ref, sl_ref, wa_ref, wm_ref, q_ref, out_ref
):
    parts = y_ref.shape[0]
    joined = jnp.concatenate([y_ref[f, 0] for f in range(parts)], axis=1)
    real_raw = joined[:HALF]
    imag_raw = joined[HALF:]
    row_ids = lax.broadcasted_iota(jnp.int32, (HALF, B), 0)
    imag_in = jnp.where(row_ids == 0, 0.0, imag_raw)
    twist_cos = tc_ref[...]
    twist_sin = ts_ref[...]
    real_u = real_raw * twist_cos + imag_in * twist_sin
    imag_u = imag_in * twist_cos - real_raw * twist_sin
    edge = imag_raw[0:1]
    edge_rows = jnp.where(
        lax.broadcasted_iota(jnp.int32, (16, B), 0) == 0,
        edge * ec_ref[...],
        jnp.where(lax.broadcasted_iota(jnp.int32, (16, B), 0) == 1, -edge * es_ref[...], 0.0),
    )
    u_high, u_low = split_parts(jnp.concatenate([real_u, imag_u], axis=0))
    e_high, e_low = split_parts(edge_rows)

    def three(high_ref, low_ref, high, low):
        return (
            dot_nt(high_ref[...], high) + dot_nt(high_ref[...], low) + dot_nt(low_ref[...], high)
        )

    by_cos = three(ch_ref, cl_ref, u_high, u_low)
    by_sin = three(sh_ref, sl_ref, u_high, u_low)
    edge_cos = three(ch_ref, cl_ref, e_high, e_low)[:NB]
    edge_sin = three(sh_ref, sl_ref, e_high, e_low)[:NB]
    white = wa_ref[...]
    real_out = ((by_cos[:NB, :HALF] + by_sin[:NB, HALF:]) * white).astype(jnp.bfloat16)
    imag_out = ((by_cos[:NB, HALF:] - by_sin[:NB, :HALF]) * white).astype(jnp.bfloat16)
    next_cos = by_cos[1 : NB + 1]
    next_sin = by_sin[1 : NB + 1]
    lane = lax.broadcasted_iota(jnp.int32, (NB, HALF), 1)
    real_edge = edge_cos[:, 0:1] + edge_sin[:, 1:2]
    imag_edge = edge_cos[:, 1:2] - edge_sin[:, 0:1]
    real_far = jnp.where(lane == 0, real_edge, next_cos[:, :HALF] - next_sin[:, HALF:])
    imag_far = jnp.where(lane == 0, imag_edge, -next_cos[:, HALF:] - next_sin[:, :HALF])
    white_far = wm_ref[...]
    order = q_ref[...]
    real_far = dot_nn((real_far * white_far).astype(jnp.bfloat16), order).astype(jnp.bfloat16)
    imag_far = dot_nn((imag_far * white_far).astype(jnp.bfloat16), order).astype(jnp.bfloat16)
    rows = NB // parts
    for f in range(parts):
        here = slice(f * rows, (f + 1) * rows)
        out_ref[f, 0, 0, :, :HALF] = real_out[here]
        out_ref[f, 0, 0, :, HALF:] = real_far[here]
        out_ref[f, 0, 1, :, :HALF] = imag_out[here]
        out_ref[f, 0, 1, :, HALF:] = imag_far[here]


def second_section(received, tables, white, white_far):
    parts, segs, rows, width = received.shape
    twists, seconds, order = tables

    def whole(array):
        return pl.BlockSpec(array.shape, lambda i: (0,) * array.ndim)

    fixed = (*twists, *seconds, white, white_far, order)
    return pl.pallas_call(
        second_kernel,
        grid=(segs,),
        in_specs=[pl.BlockSpec((parts, 1, rows, width), lambda i: (0, i, 0, 0))]
        + [whole(array) for array in fixed],
        out_specs=pl.BlockSpec((parts, 1, 2, NB // parts, A), lambda i: (0, i, 0, 0, 0)),
        out_shape=jax.ShapeDtypeStruct((parts, segs, 2, NB // parts, A), jnp.bfloat16),
        compiler_params=pltpu.CompilerParams(vmem_limit_bytes=60 * 2**20),
        cost_estimate=pl.CostEstimate(
            flops=2 * 6 * segs * 528 * B * A, bytes_accessed=segs * A * B * 6, transcendentals=0
        ),
        name="second_section",
    )(received, *fixed)


def lag_kernel(w_ref, t_ref, c_ref, s_ref, out_ref, acc_ref, even_ref, odd_ref, wf_ref):
    segs, _, blocks, _ = w_ref.shape
    depth = t_ref.shape[2]
    per_quad = depth // A
    lag_total = c_ref.shape[1]
    tmpl = out_ref.shape[2]
    step = pl.program_id(0)
    last = pl.num_programs(0) - 1
    unroll = 8

    def make_rows(rows_ref, quad, jj):
        block = quad * per_quad + jj
        for chunk in range(A // 128):
            lanes = slice(chunk * 128, (chunk + 1) * 128)
            lag_cos = c_ref[block, :, lanes]
            lag_sin = s_ref[block, :, lanes]
            out_lanes = slice(jj * A + chunk * 128, jj * A + (chunk + 1) * 128)
            for group in range(segs // unroll):
                some = slice(group * unroll, (group + 1) * unroll)
                reals = wf_ref[0, block, some, lanes]
                imags = wf_ref[1, block, some, lanes]
                for inner in range(unroll):
                    real = reals[inner : inner + 1]
                    imag = imags[inner : inner + 1]
                    first_row = (group * unroll + inner) * lag_total
                    rows = slice(first_row, first_row + lag_total)
                    rows_ref[0, rows, out_lanes] = (real * lag_cos - imag * lag_sin).astype(jnp.bfloat16)
                    rows_ref[1, rows, out_lanes] = (real * lag_sin + imag * lag_cos).astype(jnp.bfloat16)

    @pl.when(step == 0)
    def _():
        acc_ref[...] = jnp.zeros_like(acc_ref)

        @pl.loop(0, segs // unroll)
        def _(group):
            some = pl.ds(pl.multiple_of(group * unroll, unroll), unroll)
            for part in range(2):
                for first in range(0, blocks, 8):
                    here = slice(first, first + 8)
                    value = w_ref[some, part, here].astype(jnp.float32)
                    wf_ref[part, here, some, :] = jnp.swapaxes(value, 0, 1)

        for jj in range(per_quad):
            make_rows(even_ref, 0, jj)

    def both(now_ref, next_ref):
        upcoming = jnp.minimum(step + 1, last)
        for jj in range(per_quad):
            make_rows(next_ref, upcoming, jj)
        for part in range(2):
            acc_ref[part] += dot_nt(now_ref[part], t_ref[0])

    @pl.when(step % 2 == 0)
    def _():
        both(even_ref, odd_ref)

    @pl.when(step % 2 == 1)
    def _():
        both(odd_ref, even_ref)

    @pl.when(step == last)
    def _():
        shape = (segs, lag_total, tmpl)
        out_ref[:, :lag_total] = (acc_ref[0, :, :tmpl] + acc_ref[1, :, tmpl:]).reshape(shape)
        out_ref[:, lag_total:] = (acc_ref[1, :, :tmpl] - acc_ref[0, :, tmpl:]).reshape(shape)


def lag_products(data, laid, lag_cos, lag_sin):
    segs, _, blocks, _ = data.shape
    quads, tmpl2, depth = laid.shape
    lag_total = lag_cos.shape[1]
    once = pl.Buffered(1)
    return pl.pallas_call(
        lag_kernel,
        grid=(quads,),
        in_specs=[
            pl.BlockSpec(data.shape, lambda i: (0, 0, 0, 0), pipeline_mode=once),
            pl.BlockSpec((1, tmpl2, depth), lambda i: (i, 0, 0)),
            pl.BlockSpec(lag_cos.shape, lambda i: (0, 0, 0), pipeline_mode=once),
            pl.BlockSpec(lag_sin.shape, lambda i: (0, 0, 0), pipeline_mode=once),
        ],
        out_specs=pl.BlockSpec((segs, 2 * lag_total, tmpl2 // 2), lambda i: (0, 0, 0)),
        out_shape=jax.ShapeDtypeStruct((segs, 2 * lag_total, tmpl2 // 2), jnp.float32),
        scratch_shapes=[
            pltpu.VMEM((2, segs * lag_total, tmpl2), jnp.float32),
            pltpu.VMEM((2, segs * lag_total, depth), jnp.bfloat16),
            pltpu.VMEM((2, segs * lag_total, depth), jnp.bfloat16),
            pltpu.VMEM((2, blocks, segs, A), jnp.float32),
        ],
        compiler_params=pltpu.CompilerParams(vmem_limit_bytes=60 * 2**20),
        cost_estimate=pl.CostEstimate(
            flops=4 * segs * lag_total * tmpl2 * blocks * A,
            bytes_accessed=blocks * A * (tmpl2 * 2 + segs * 4),
            transcendentals=0,
        ),
        name="lag_products",
    )(data, laid, lag_cos, lag_sin)


def layout_kernel(cut_ref, t_ref, *refs):
    out_ref = refs[-1]
    tmpl, _, rows, _ = t_ref.shape
    per_quad = out_ref.shape[3] // A
    first_row = pl.program_id(0) * rows + cut_ref[cut_ref.shape[0] - 1]
    first_tmpl = pl.program_id(1) * tmpl
    row_ids = lax.broadcasted_iota(jnp.int32, (rows, 128), 0) + first_row
    batch = 16

    @pl.loop(0, tmpl // batch)
    def _(group):
        some = pl.ds(pl.multiple_of(group * batch, batch), batch)
        keeps = [row_ids < cut_ref[first_tmpl + group * batch + n] for n in range(batch)]
        for part in range(2):
            for chunk in range(A // 128):
                lanes = slice(chunk * 128, (chunk + 1) * 128)
                value = t_ref[some, part, :, lanes].astype(jnp.float32)
                value = jnp.stack([jnp.where(keeps[n], value[n], 0.0) for n in range(batch)], axis=0)
                value = jnp.swapaxes(value, 0, 1).astype(jnp.bfloat16)
                for row in range(rows):
                    start = row % per_quad * A + chunk * 128
                    out_ref[row // per_quad, part, some, start : start + 128] = value[row]


def lay_out(templates, cuts, per_quad, piece, pieces, laid):
    tmpl, _, blocks, _ = templates.shape
    rows = min(16, blocks)
    steps = blocks // rows // pieces
    batch = min(64, tmpl)
    shape = (blocks // per_quad, 2, tmpl, per_quad * A)
    first = piece * steps
    info = jnp.concatenate([cuts, jnp.full((1,), first * rows, jnp.int32)])
    earlier = () if laid is None else (laid,)
    return pl.pallas_call(
        layout_kernel,
        grid=(steps, tmpl // batch),
        in_specs=[
            pl.BlockSpec(memory_space=pltpu.SMEM),
            pl.BlockSpec((batch, 2, rows, A), lambda i, j: (j, 0, i + first, 0)),
        ]
        + [pl.BlockSpec(memory_space=pl.ANY)] * len(earlier),
        out_specs=pl.BlockSpec(
            (rows // per_quad, 2, batch, per_quad * A), lambda i, j: (i + first, 0, j, 0)
        ),
        out_shape=jax.ShapeDtypeStruct(shape, jnp.bfloat16),
        input_output_aliases={2: 0} if earlier else {},
        compiler_params=pltpu.CompilerParams(vmem_limit_bytes=40 * 2**20),
        cost_estimate=pl.CostEstimate(
            flops=0, bytes_accessed=8 * tmpl * 2 * blocks * A // pieces, transcendentals=0
        ),
        name="lay_out",
    )(info, templates, *earlier)


def general_transform(strain, psd):
    freq_count = lax.axis_size("freq")
    freq_index = lax.axis_index("freq")
    seg_local = strain.shape[0]
    step_time = B // freq_count
    highest = lax.Precision.HIGHEST
    first_cos, first_sin = cos_sin_table(
        jnp.arange(A, dtype=jnp.int32), jnp.arange(A, dtype=jnp.int32), A
    )
    table = jnp.concatenate([first_cos, -first_sin], axis=0)
    time_ids = freq_index * step_time + jnp.arange(step_time, dtype=jnp.int32)
    twist_cos, twist_sin = cos_sin_table(jnp.arange(A, dtype=jnp.int32), time_ids, LEN)
    slab_blocks = strain.reshape(seg_local, A // freq_count, B)
    both_parts = jnp.einsum(
        "kn,snb->skb",
        table,
        lax.all_to_all(slab_blocks, "freq", split_axis=2, concat_axis=1, tiled=True),
        precision=highest,
    )
    real_part = both_parts[:, :A]
    imag_part = both_parts[:, A:]
    second_cos, second_sin = cos_sin_table(
        jnp.arange(B, dtype=jnp.int32), jnp.arange(NB, dtype=jnp.int32), B
    )
    rotation = jnp.concatenate(
        [
            jnp.concatenate([second_cos, -second_sin], axis=1),
            jnp.concatenate([second_sin, second_cos], axis=1),
        ],
        axis=0,
    )
    amplitude = jnp.sqrt(LEN * psd)
    real_in = lax.all_to_all(
        real_part * twist_cos + imag_part * twist_sin, "freq", split_axis=1, concat_axis=2, tiled=True
    )
    imag_in = lax.all_to_all(
        imag_part * twist_cos - real_part * twist_sin, "freq", split_axis=1, concat_axis=2, tiled=True
    )
    joined = jnp.concatenate([real_in, imag_in], axis=2)
    both_out = jnp.einsum("spc,cm->smp", joined, rotation, precision=highest)
    both_out = both_out.reshape(joined.shape[0], 2, NB, joined.shape[1])
    whitened = (both_out / amplitude).astype(jnp.bfloat16)
    return lax.all_to_all(whitened, "freq", split_axis=2, concat_axis=3, tiled=True)


def exchange(sent):
    return lax.all_to_all(sent, "freq", split_axis=0, concat_axis=0, tiled=True)


def pack_strain(strain, freq_count):
    seg_local = strain.shape[0]
    sent = (strain * STRAIN_SCALE).astype(jnp.float16)
    sent = sent.reshape(seg_local, A // freq_count, freq_count, B // freq_count)
    return sent.transpose(2, 0, 1, 3)


def pack_coefs(received, table):
    freq_count, seg_local, _, width = received.shape
    coefs = first_section(received.astype(jnp.float32) * (1.0 / STRAIN_SCALE), table)
    sent = (coefs * COEF_SCALE).astype(jnp.float16)
    return sent.reshape(freq_count, seg_local // freq_count, A, width)


def whiten(received, tables, white, white_far):
    return second_section(received.astype(jnp.float32) * (1.0 / COEF_SCALE), tables, white, white_far)


def on_device(strain, psd, templates, cutoffs, lags):
    freq_count = lax.axis_size("freq")
    freq_index = lax.axis_index("freq")
    seg_local = strain.shape[0]
    tmpl_local = templates.shape[0]
    blocks_here = templates.shape[2]
    first_block = freq_index * blocks_here
    block_ids = first_block + jnp.arange(blocks_here, dtype=jnp.int32)
    per_quad = min(4, blocks_here)
    quads = blocks_here // per_quad
    cuts = cutoffs - first_block
    tied = lax.optimization_barrier

    block_cos, block_sin = cos_sin_table(block_ids, lags % B, B)
    place = lags[:, None] * jnp.arange(A, dtype=jnp.int32)[None, :] % LEN
    place_angle = place.astype(jnp.float32) * (two_pi / LEN)
    place_cos = jnp.cos(place_angle)[None]
    place_sin = jnp.sin(place_angle)[None]
    block_cos = block_cos[:, :, None]
    block_sin = block_sin[:, :, None]
    lag_cos = block_cos * place_cos - block_sin * place_sin
    lag_sin = block_sin * place_cos + block_cos * place_sin

    sliced = seg_local == 2 * freq_count and (NB // freq_count) % 32 == 0 and B // freq_count == 128
    if not sliced:
        laid = lay_out(templates, cuts, per_quad, 0, 1, None)
        laid = laid.reshape(quads, 2 * tmpl_local, per_quad * A)
        data = lax.all_gather(general_transform(strain, psd), "tmpl", axis=0, tiled=True)
        half = data.shape[0] // 2
        sums = [lag_products(part, laid, lag_cos, lag_sin) for part in (data[:half], data[half:])]
        sums = jnp.concatenate(sums, axis=0)
        return lax.psum_scatter(sums, "freq", scatter_dimension=0, tiled=True)

    order = mirror_table()
    psd_all = lax.all_gather(psd, "freq", axis=1, tiled=True)
    psd_far = jnp.dot(psd_all[:, HALF:], order.T, precision=lax.Precision.HIGHEST)
    white = lax.rsqrt(LEN * psd_all[:, :HALF])
    white_far = lax.rsqrt(LEN * psd_far)
    first = first_table()
    second = (twist_tables(), second_tables(), order.astype(ml_dtypes.bfloat16))

    seg_out = seg_local * lax.axis_size("tmpl") // freq_count
    by_owner = strain.reshape(seg_local // seg_out, 2, seg_out // 2, strain.shape[1])
    strain_a, strain_b = (
        pack_strain(by_owner[:, group].reshape(seg_local // 2, strain.shape[1]), freq_count)
        for group in range(2)
    )
    time_a = exchange(strain_a)
    laid = lay_out(templates, cuts, per_quad, 0, 2, None)
    time_a, strain_b, laid = tied((time_a, strain_b, laid))
    time_b = exchange(strain_b)
    coefs_a = pack_coefs(time_a, first)
    laid = lay_out(templates, cuts, per_quad, 1, 2, laid)
    time_b, coefs_a, laid = tied((time_b, coefs_a, laid))
    parts_a = exchange(coefs_a)
    coefs_b = pack_coefs(time_b, first)
    parts_a, coefs_b, white, white_far, lag_cos, lag_sin = tied(
        (parts_a, coefs_b, white, white_far, lag_cos, lag_sin)
    )
    parts_b = exchange(coefs_b)
    white_a = whiten(parts_a, second, white, white_far)
    parts_b, white_a = tied((parts_b, white_a))
    data_a = exchange(white_a)
    white_b = whiten(parts_b, second, white, white_far)
    data_a, white_b = tied((data_a, white_b))
    data_b = exchange(white_b)
    laid = laid.reshape(quads, 2 * tmpl_local, per_quad * A)
    outputs = []
    for data in (data_a, data_b):
        data = data.reshape(seg_local // 2, 2, blocks_here, A)
        data = lax.all_gather(data, "tmpl", axis=0, tiled=True)
        sums = lag_products(data, laid, lag_cos, lag_sin)
        outputs.append(lax.psum_scatter(sums, "freq", scatter_dimension=0, tiled=True))
    return jnp.concatenate(outputs, axis=0)


def solution(mesh):
    placed = (P("tmpl", "freq"), P(None, "freq"), P("tmpl", None, "freq", None), P("tmpl"), P())
    return jax.shard_map(
        on_device, mesh=mesh, in_specs=placed, out_specs=P("freq", None, "tmpl"), check_vma=False
    )
```

```python
import math

import jax
import jax.numpy as jnp
import ml_dtypes
import numpy as np
from jax import lax
from jax.experimental import pallas as pl
from jax.experimental.pallas import tpu as pltpu
from jax.sharding import PartitionSpec as P

A = 512
B = 1024
LEN = 524288
NB = 512
HALF = A // 2

STRAIN_SCALE = 8192.0
COEF_SCALE = 16.0

two_pi = 2.0 * math.pi


def cos_sin_table(row_ids, col_ids, modulus):
    product = row_ids[:, None] * col_ids[None, :] % modulus
    phase_angle = product.astype(jnp.float32) * (two_pi / modulus)
    return (jnp.cos(phase_angle), jnp.sin(phase_angle))


def split_const(table):
    high = table.astype(ml_dtypes.bfloat16)
    low = (table - high.astype(np.float64)).astype(ml_dtypes.bfloat16)
    return high, low


def first_table():
    angle = two_pi * (np.outer(np.arange(HALF), np.arange(A)) % A) / A
    table = np.concatenate([np.cos(angle), -np.sin(angle)], axis=0)
    table[HALF] = 1.0 - 2.0 * (np.arange(A) % 2)
    return split_const(table)


def second_tables():
    angle = two_pi * (np.outer(np.arange(528), np.arange(B)) % B) / B
    return split_const(np.cos(angle)) + split_const(np.sin(angle))


def twist_tables():
    angle = two_pi * np.outer(np.arange(HALF), np.arange(B)) / LEN
    edge = two_pi * HALF * np.arange(B)[None, :] / LEN
    return (
        np.cos(angle).astype(np.float32),
        np.sin(angle).astype(np.float32),
        np.cos(edge).astype(np.float32),
        np.sin(edge).astype(np.float32),
    )


def mirror_table():
    table = np.zeros((HALF, HALF), np.float32)
    table[0, 0] = 1.0
    table[np.arange(1, HALF), HALF - np.arange(1, HALF)] = 1.0
    return table


def split_parts(value):
    high = value.astype(jnp.bfloat16)
    low = (value - high.astype(jnp.float32)).astype(jnp.bfloat16)
    return high, low


def dot_nn(lhs, rhs):
    return lax.dot_general(lhs, rhs, (((1,), (0,)), ((), ())), preferred_element_type=jnp.float32)


def dot_nt(lhs, rhs):
    return lax.dot_general(lhs, rhs, (((1,), (1,)), ((), ())), preferred_element_type=jnp.float32)


def first_kernel(x_ref, high_ref, low_ref, out_ref):
    parts = x_ref.shape[0]
    pair = x_ref.shape[1]
    columns = []
    for s in range(pair):
        columns.append(jnp.concatenate([x_ref[f, s] for f in range(parts)], axis=0))
    value = jnp.concatenate(columns, axis=1)
    high, low = split_parts(value)
    result = dot_nn(high_ref[...], high) + dot_nn(high_ref[...], low) + dot_nn(low_ref[...], high)
    width = x_ref.shape[3]
    for s in range(pair):
        out_ref[s] = result[:, s * width : (s + 1) * width]


def first_section(received, tables):
    parts, segs, rows, width = received.shape
    pair = 2
    return pl.pallas_call(
        first_kernel,
        grid=(segs // pair,),
        in_specs=[
            pl.BlockSpec((parts, pair, rows, width), lambda i: (0, i, 0, 0)),
            pl.BlockSpec((A, A), lambda i: (0, 0)),
            pl.BlockSpec((A, A), lambda i: (0, 0)),
        ],
        out_specs=pl.BlockSpec((pair, A, width), lambda i: (i, 0, 0)),
        out_shape=jax.ShapeDtypeStruct((segs, A, width), jnp.float32),
        compiler_params=pltpu.CompilerParams(vmem_limit_bytes=40 * 2**20),
        cost_estimate=pl.CostEstimate(
            flops=2 * 3 * segs * A * A * width, bytes_accessed=segs * A * width * 8, transcendentals=0
        ),
        name="first_section",
    )(received, *tables)


def second_kernel(
    y_ref, tc_ref, ts_ref, ec_ref, es_ref, ch_ref, cl_ref, sh_ref, sl_ref, wa_ref, wm_ref, q_ref, out_ref
):
    parts = y_ref.shape[0]
    joined = jnp.concatenate([y_ref[f, 0] for f in range(parts)], axis=1)
    real_raw = joined[:HALF]
    imag_raw = joined[HALF:]
    row_ids = lax.broadcasted_iota(jnp.int32, (HALF, B), 0)
    imag_in = jnp.where(row_ids == 0, 0.0, imag_raw)
    twist_cos = tc_ref[...]
    twist_sin = ts_ref[...]
    real_u = real_raw * twist_cos + imag_in * twist_sin
    imag_u = imag_in * twist_cos - real_raw * twist_sin
    edge = imag_raw[0:1]
    edge_rows = jnp.where(
        lax.broadcasted_iota(jnp.int32, (16, B), 0) == 0,
        edge * ec_ref[...],
        jnp.where(lax.broadcasted_iota(jnp.int32, (16, B), 0) == 1, -edge * es_ref[...], 0.0),
    )
    u_high, u_low = split_parts(jnp.concatenate([real_u, imag_u], axis=0))
    e_high, e_low = split_parts(edge_rows)

    def three(high_ref, low_ref, high, low):
        return (
            dot_nt(high_ref[...], high) + dot_nt(high_ref[...], low) + dot_nt(low_ref[...], high)
        )

    by_cos = three(ch_ref, cl_ref, u_high, u_low)
    by_sin = three(sh_ref, sl_ref, u_high, u_low)
    edge_cos = three(ch_ref, cl_ref, e_high, e_low)[:NB]
    edge_sin = three(sh_ref, sl_ref, e_high, e_low)[:NB]
    white = wa_ref[...]
    real_out = ((by_cos[:NB, :HALF] + by_sin[:NB, HALF:]) * white).astype(jnp.bfloat16)
    imag_out = ((by_cos[:NB, HALF:] - by_sin[:NB, :HALF]) * white).astype(jnp.bfloat16)
    next_cos = by_cos[1 : NB + 1]
    next_sin = by_sin[1 : NB + 1]
    lane = lax.broadcasted_iota(jnp.int32, (NB, HALF), 1)
    real_edge = edge_cos[:, 0:1] + edge_sin[:, 1:2]
    imag_edge = edge_cos[:, 1:2] - edge_sin[:, 0:1]
    real_far = jnp.where(lane == 0, real_edge, next_cos[:, :HALF] - next_sin[:, HALF:])
    imag_far = jnp.where(lane == 0, imag_edge, -next_cos[:, HALF:] - next_sin[:, :HALF])
    white_far = wm_ref[...]
    order = q_ref[...]
    real_far = dot_nn((real_far * white_far).astype(jnp.bfloat16), order).astype(jnp.bfloat16)
    imag_far = dot_nn((imag_far * white_far).astype(jnp.bfloat16), order).astype(jnp.bfloat16)
    rows = NB // parts
    for f in range(parts):
        here = slice(f * rows, (f + 1) * rows)
        out_ref[f, 0, 0, :, :HALF] = real_out[here]
        out_ref[f, 0, 0, :, HALF:] = real_far[here]
        out_ref[f, 0, 1, :, :HALF] = imag_out[here]
        out_ref[f, 0, 1, :, HALF:] = imag_far[here]


def second_section(received, tables, white, white_far):
    parts, segs, rows, width = received.shape
    twists, seconds, order = tables

    def whole(array):
        return pl.BlockSpec(array.shape, lambda i: (0,) * array.ndim)

    fixed = (*twists, *seconds, white, white_far, order)
    return pl.pallas_call(
        second_kernel,
        grid=(segs,),
        in_specs=[pl.BlockSpec((parts, 1, rows, width), lambda i: (0, i, 0, 0))]
        + [whole(array) for array in fixed],
        out_specs=pl.BlockSpec((parts, 1, 2, NB // parts, A), lambda i: (0, i, 0, 0, 0)),
        out_shape=jax.ShapeDtypeStruct((parts, segs, 2, NB // parts, A), jnp.bfloat16),
        compiler_params=pltpu.CompilerParams(vmem_limit_bytes=60 * 2**20),
        cost_estimate=pl.CostEstimate(
            flops=2 * 6 * segs * 528 * B * A, bytes_accessed=segs * A * B * 6, transcendentals=0
        ),
        name="second_section",
    )(received, *fixed)


def lag_kernel(w_ref, t_ref, c_ref, s_ref, out_ref, acc_ref, even_ref, odd_ref, wf_ref):
    segs, _, blocks, _ = w_ref.shape
    depth = t_ref.shape[2]
    per_quad = depth // A
    lag_total = c_ref.shape[1]
    tmpl = out_ref.shape[2]
    step = pl.program_id(0)
    last = pl.num_programs(0) - 1
    half = segs * lag_total
    unroll = 8

    def make_rows(rows_ref, quad, jj):
        block = quad * per_quad + jj
        for chunk in range(A // 128):
            lanes = slice(chunk * 128, (chunk + 1) * 128)
            lag_cos = c_ref[block, :, lanes]
            lag_sin = s_ref[block, :, lanes]
            out_lanes = slice(jj * A + chunk * 128, jj * A + (chunk + 1) * 128)
            for group in range(segs // unroll):
                some = slice(group * unroll, (group + 1) * unroll)
                reals = wf_ref[0, block, some, lanes]
                imags = wf_ref[1, block, some, lanes]
                for inner in range(unroll):
                    real = reals[inner : inner + 1]
                    imag = imags[inner : inner + 1]
                    first_row = (group * unroll + inner) * lag_total
                    rows = slice(first_row, first_row + lag_total)
                    rows_ref[rows, out_lanes] = (real * lag_cos - imag * lag_sin).astype(jnp.bfloat16)
                    rows = slice(half + first_row, half + first_row + lag_total)
                    rows_ref[rows, out_lanes] = (real * lag_sin + imag * lag_cos).astype(jnp.bfloat16)

    @pl.when(step == 0)
    def _():
        acc_ref[...] = jnp.zeros_like(acc_ref)

        @pl.loop(0, segs // unroll)
        def _(group):
            some = pl.ds(pl.multiple_of(group * unroll, unroll), unroll)
            for part in range(2):
                for first in range(0, blocks, 8):
                    here = slice(first, first + 8)
                    value = w_ref[some, part, here].astype(jnp.float32)
                    wf_ref[part, here, some, :] = jnp.swapaxes(value, 0, 1)

        for jj in range(per_quad):
            make_rows(even_ref, 0, jj)

    def both(now_ref, next_ref):
        upcoming = jnp.minimum(step + 1, last)
        cut = max(1, per_quad // 2)
        pieces = [(k, n) for k in range(per_quad // cut) for n in range(2)]
        for index, (k, n) in enumerate(pieces):
            for jj in range(per_quad):
                if jj * len(pieces) // per_quad == index:
                    make_rows(next_ref, upcoming, jj)
            deep = slice(k * cut * A, (k + 1) * cut * A)
            cols = slice(n * tmpl, (n + 1) * tmpl)
            acc_ref[:, cols] += dot_nt(now_ref[:, deep], t_ref[0, cols, deep])

    @pl.when(step % 2 == 0)
    def _():
        both(even_ref, odd_ref)

    @pl.when(step % 2 == 1)
    def _():
        both(odd_ref, even_ref)

    @pl.when(step == last)
    def _():
        shape = (segs, lag_total, tmpl)
        out_ref[:, :lag_total] = (acc_ref[:half, :tmpl] + acc_ref[half:, tmpl:]).reshape(shape)
        out_ref[:, lag_total:] = (acc_ref[half:, :tmpl] - acc_ref[:half, tmpl:]).reshape(shape)


def lag_products(data, laid, lag_cos, lag_sin):
    segs, _, blocks, _ = data.shape
    quads, tmpl2, depth = laid.shape
    lag_total = lag_cos.shape[1]
    once = pl.Buffered(1)
    return pl.pallas_call(
        lag_kernel,
        grid=(quads,),
        in_specs=[
            pl.BlockSpec(data.shape, lambda i: (0, 0, 0, 0), pipeline_mode=once),
            pl.BlockSpec((1, tmpl2, depth), lambda i: (i, 0, 0)),
            pl.BlockSpec(lag_cos.shape, lambda i: (0, 0, 0), pipeline_mode=once),
            pl.BlockSpec(lag_sin.shape, lambda i: (0, 0, 0), pipeline_mode=once),
        ],
        out_specs=pl.BlockSpec((segs, 2 * lag_total, tmpl2 // 2), lambda i: (0, 0, 0)),
        out_shape=jax.ShapeDtypeStruct((segs, 2 * lag_total, tmpl2 // 2), jnp.float32),
        scratch_shapes=[
            pltpu.VMEM((2 * segs * lag_total, tmpl2), jnp.float32),
            pltpu.VMEM((2 * segs * lag_total, depth), jnp.bfloat16),
            pltpu.VMEM((2 * segs * lag_total, depth), jnp.bfloat16),
            pltpu.VMEM((2, blocks, segs, A), jnp.float32),
        ],
        compiler_params=pltpu.CompilerParams(vmem_limit_bytes=60 * 2**20),
        cost_estimate=pl.CostEstimate(
            flops=4 * segs * lag_total * tmpl2 * blocks * A,
            bytes_accessed=blocks * A * (tmpl2 * 2 + segs * 4),
            transcendentals=0,
        ),
        name="lag_products",
    )(data, laid, lag_cos, lag_sin)


def layout_kernel(cut_ref, t_ref, *refs):
    out_ref = refs[-1]
    tmpl, _, rows, _ = t_ref.shape
    per_quad = out_ref.shape[3] // A
    first_row = pl.program_id(0) * rows + cut_ref[cut_ref.shape[0] - 1]
    first_tmpl = pl.program_id(1) * tmpl
    row_ids = lax.broadcasted_iota(jnp.int32, (rows, 128), 0) + first_row
    batch = 16

    @pl.loop(0, tmpl // batch)
    def _(group):
        some = pl.ds(pl.multiple_of(group * batch, batch), batch)
        keeps = [row_ids < cut_ref[first_tmpl + group * batch + n] for n in range(batch)]
        for part in range(2):
            for chunk in range(A // 128):
                lanes = slice(chunk * 128, (chunk + 1) * 128)
                value = t_ref[some, part, :, lanes].astype(jnp.float32)
                value = jnp.stack([jnp.where(keeps[n], value[n], 0.0) for n in range(batch)], axis=0)
                value = jnp.swapaxes(value, 0, 1).astype(jnp.bfloat16)
                for row in range(rows):
                    start = row % per_quad * A + chunk * 128
                    out_ref[row // per_quad, part, some, start : start + 128] = value[row]


def lay_out(templates, cuts, per_quad, piece, pieces, laid):
    tmpl, _, blocks, _ = templates.shape
    rows = min(16, blocks)
    steps = blocks // rows // pieces
    batch = min(64, tmpl)
    shape = (blocks // per_quad, 2, tmpl, per_quad * A)
    first = piece * steps
    info = jnp.concatenate([cuts, jnp.full((1,), first * rows, jnp.int32)])
    earlier = () if laid is None else (laid,)
    return pl.pallas_call(
        layout_kernel,
        grid=(steps, tmpl // batch),
        in_specs=[
            pl.BlockSpec(memory_space=pltpu.SMEM),
            pl.BlockSpec((batch, 2, rows, A), lambda i, j: (j, 0, i + first, 0)),
        ]
        + [pl.BlockSpec(memory_space=pl.ANY)] * len(earlier),
        out_specs=pl.BlockSpec(
            (rows // per_quad, 2, batch, per_quad * A), lambda i, j: (i + first, 0, j, 0)
        ),
        out_shape=jax.ShapeDtypeStruct(shape, jnp.bfloat16),
        input_output_aliases={2: 0} if earlier else {},
        compiler_params=pltpu.CompilerParams(vmem_limit_bytes=40 * 2**20),
        cost_estimate=pl.CostEstimate(
            flops=0, bytes_accessed=8 * tmpl * 2 * blocks * A // pieces, transcendentals=0
        ),
        name="lay_out",
    )(info, templates, *earlier)


def general_transform(strain, psd):
    freq_count = lax.axis_size("freq")
    freq_index = lax.axis_index("freq")
    seg_local = strain.shape[0]
    step_time = B // freq_count
    highest = lax.Precision.HIGHEST
    first_cos, first_sin = cos_sin_table(
        jnp.arange(A, dtype=jnp.int32), jnp.arange(A, dtype=jnp.int32), A
    )
    table = jnp.concatenate([first_cos, -first_sin], axis=0)
    time_ids = freq_index * step_time + jnp.arange(step_time, dtype=jnp.int32)
    twist_cos, twist_sin = cos_sin_table(jnp.arange(A, dtype=jnp.int32), time_ids, LEN)
    slab_blocks = strain.reshape(seg_local, A // freq_count, B)
    both_parts = jnp.einsum(
        "kn,snb->skb",
        table,
        lax.all_to_all(slab_blocks, "freq", split_axis=2, concat_axis=1, tiled=True),
        precision=highest,
    )
    real_part = both_parts[:, :A]
    imag_part = both_parts[:, A:]
    second_cos, second_sin = cos_sin_table(
        jnp.arange(B, dtype=jnp.int32), jnp.arange(NB, dtype=jnp.int32), B
    )
    rotation = jnp.concatenate(
        [
            jnp.concatenate([second_cos, -second_sin], axis=1),
            jnp.concatenate([second_sin, second_cos], axis=1),
        ],
        axis=0,
    )
    amplitude = jnp.sqrt(LEN * psd)
    real_in = lax.all_to_all(
        real_part * twist_cos + imag_part * twist_sin, "freq", split_axis=1, concat_axis=2, tiled=True
    )
    imag_in = lax.all_to_all(
        imag_part * twist_cos - real_part * twist_sin, "freq", split_axis=1, concat_axis=2, tiled=True
    )
    joined = jnp.concatenate([real_in, imag_in], axis=2)
    both_out = jnp.einsum("spc,cm->smp", joined, rotation, precision=highest)
    both_out = both_out.reshape(joined.shape[0], 2, NB, joined.shape[1])
    whitened = (both_out / amplitude).astype(jnp.bfloat16)
    return lax.all_to_all(whitened, "freq", split_axis=2, concat_axis=3, tiled=True)


def exchange(sent):
    return lax.all_to_all(sent, "freq", split_axis=0, concat_axis=0, tiled=True)


def pack_strain(strain, freq_count):
    seg_local = strain.shape[0]
    sent = (strain * STRAIN_SCALE).astype(jnp.float16)
    sent = sent.reshape(seg_local, A // freq_count, freq_count, B // freq_count)
    return sent.transpose(2, 0, 1, 3)


def pack_coefs(received, table):
    freq_count, seg_local, _, width = received.shape
    coefs = first_section(received.astype(jnp.float32) * (1.0 / STRAIN_SCALE), table)
    sent = (coefs * COEF_SCALE).astype(jnp.float16)
    return sent.reshape(freq_count, seg_local // freq_count, A, width)


def whiten(received, tables, white, white_far):
    return second_section(received.astype(jnp.float32) * (1.0 / COEF_SCALE), tables, white, white_far)


def on_device(strain, psd, templates, cutoffs, lags):
    freq_count = lax.axis_size("freq")
    freq_index = lax.axis_index("freq")
    seg_local = strain.shape[0]
    tmpl_local = templates.shape[0]
    blocks_here = templates.shape[2]
    first_block = freq_index * blocks_here
    block_ids = first_block + jnp.arange(blocks_here, dtype=jnp.int32)
    per_quad = min(4, blocks_here)
    quads = blocks_here // per_quad
    cuts = cutoffs - first_block
    tied = lax.optimization_barrier

    block_cos, block_sin = cos_sin_table(block_ids, lags % B, B)
    place = lags[:, None] * jnp.arange(A, dtype=jnp.int32)[None, :] % LEN
    place_angle = place.astype(jnp.float32) * (two_pi / LEN)
    place_cos = jnp.cos(place_angle)[None]
    place_sin = jnp.sin(place_angle)[None]
    block_cos = block_cos[:, :, None]
    block_sin = block_sin[:, :, None]
    lag_cos = block_cos * place_cos - block_sin * place_sin
    lag_sin = block_sin * place_cos + block_cos * place_sin

    sliced = seg_local == 2 * freq_count and (NB // freq_count) % 32 == 0 and B // freq_count == 128
    if not sliced:
        laid = lay_out(templates, cuts, per_quad, 0, 1, None)
        laid = laid.reshape(quads, 2 * tmpl_local, per_quad * A)
        data = lax.all_gather(general_transform(strain, psd), "tmpl", axis=0, tiled=True)
        half = data.shape[0] // 2
        sums = [lag_products(part, laid, lag_cos, lag_sin) for part in (data[:half], data[half:])]
        sums = jnp.concatenate(sums, axis=0)
        return lax.psum_scatter(sums, "freq", scatter_dimension=0, tiled=True)

    order = mirror_table()
    psd_all = lax.all_gather(psd, "freq", axis=1, tiled=True)
    psd_far = jnp.dot(psd_all[:, HALF:], order.T, precision=lax.Precision.HIGHEST)
    white = lax.rsqrt(LEN * psd_all[:, :HALF])
    white_far = lax.rsqrt(LEN * psd_far)
    first = first_table()
    second = (twist_tables(), second_tables(), order.astype(ml_dtypes.bfloat16))

    seg_out = seg_local * lax.axis_size("tmpl") // freq_count
    by_owner = strain.reshape(seg_local // seg_out, 2, seg_out // 2, strain.shape[1])
    strain_a, strain_b = (
        pack_strain(by_owner[:, group].reshape(seg_local // 2, strain.shape[1]), freq_count)
        for group in range(2)
    )
    time_a = exchange(strain_a)
    laid = lay_out(templates, cuts, per_quad, 0, 2, None)
    time_a, laid = tied((time_a, laid))
    coefs_a = pack_coefs(time_a, first)
    parts_a = exchange(coefs_a)
    laid = lay_out(templates, cuts, per_quad, 1, 2, laid)
    parts_a, strain_b, laid, white, white_far, lag_cos, lag_sin = tied(
        (parts_a, strain_b, laid, white, white_far, lag_cos, lag_sin)
    )
    time_b = exchange(strain_b)
    white_a = whiten(parts_a, second, white, white_far)
    time_b, white_a = tied((time_b, white_a))
    data_a = exchange(white_a)
    coefs_b = pack_coefs(time_b, first)
    data_a, coefs_b = tied((data_a, coefs_b))
    parts_b = exchange(coefs_b)
    data_a = data_a.reshape(seg_local // 2, 2, blocks_here, A)
    data_a = lax.all_gather(data_a, "tmpl", axis=0, tiled=True)
    white_b = whiten(parts_b, second, white, white_far)
    data_a = tied((data_a, white_b))[0]
    data_b = exchange(white_b).reshape(seg_local // 2, 2, blocks_here, A)
    data_b = lax.all_gather(data_b, "tmpl", axis=0, tiled=True)
    laid = laid.reshape(quads, 2 * tmpl_local, per_quad * A)
    outputs = []
    for data in (data_a, data_b):
        sums = lag_products(data, laid, lag_cos, lag_sin)
        outputs.append(lax.psum_scatter(sums, "freq", scatter_dimension=0, tiled=True))
    return jnp.concatenate(outputs, axis=0)


def solution(mesh):
    placed = (P("tmpl", "freq"), P(None, "freq"), P("tmpl", None, "freq", None), P("tmpl"), P())
    return jax.shard_map(
        on_device, mesh=mesh, in_specs=placed, out_specs=P("freq", None, "tmpl"), check_vma=False
    )
```

```python
import math

import jax
import jax.numpy as jnp
import ml_dtypes
import numpy as np
from jax import lax
from jax.experimental import pallas as pl
from jax.experimental.pallas import tpu as pltpu
from jax.sharding import PartitionSpec as P

A = 512
B = 1024
LEN = 524288
NB = 512
HALF = A // 2

STRAIN_SCALE = 8192.0
COEF_SCALE = 16.0

two_pi = 2.0 * math.pi


def cos_sin_table(row_ids, col_ids, modulus):
    product = row_ids[:, None] * col_ids[None, :] % modulus
    phase_angle = product.astype(jnp.float32) * (two_pi / modulus)
    return (jnp.cos(phase_angle), jnp.sin(phase_angle))


def split_const(table):
    high = table.astype(ml_dtypes.bfloat16)
    low = (table - high.astype(np.float64)).astype(ml_dtypes.bfloat16)
    return high, low


def first_table():
    angle = two_pi * (np.outer(np.arange(HALF), np.arange(A)) % A) / A
    table = np.concatenate([np.cos(angle), -np.sin(angle)], axis=0)
    table[HALF] = 1.0 - 2.0 * (np.arange(A) % 2)
    return split_const(table)


def second_tables():
    angle = two_pi * (np.outer(np.arange(528), np.arange(B)) % B) / B
    return split_const(np.cos(angle)) + split_const(np.sin(angle))


def twist_tables():
    angle = two_pi * np.outer(np.arange(HALF), np.arange(B)) / LEN
    edge = two_pi * HALF * np.arange(B)[None, :] / LEN
    return (
        np.cos(angle).astype(np.float32),
        np.sin(angle).astype(np.float32),
        np.cos(edge).astype(np.float32),
        np.sin(edge).astype(np.float32),
    )


def mirror_table():
    table = np.zeros((HALF, HALF), np.float32)
    table[0, 0] = 1.0
    table[np.arange(1, HALF), HALF - np.arange(1, HALF)] = 1.0
    return table


def split_parts(value):
    high = value.astype(jnp.bfloat16)
    low = (value - high.astype(jnp.float32)).astype(jnp.bfloat16)
    return high, low


def dot_nn(lhs, rhs):
    return lax.dot_general(lhs, rhs, (((1,), (0,)), ((), ())), preferred_element_type=jnp.float32)


def dot_nt(lhs, rhs):
    return lax.dot_general(lhs, rhs, (((1,), (1,)), ((), ())), preferred_element_type=jnp.float32)


def first_kernel(x_ref, high_ref, low_ref, out_ref):
    parts = x_ref.shape[0]
    pair = x_ref.shape[1]
    columns = []
    for s in range(pair):
        columns.append(jnp.concatenate([x_ref[f, s] for f in range(parts)], axis=0))
    value = jnp.concatenate(columns, axis=1)
    high, low = split_parts(value)
    result = dot_nn(high_ref[...], high) + dot_nn(high_ref[...], low) + dot_nn(low_ref[...], high)
    width = x_ref.shape[3]
    for s in range(pair):
        out_ref[s] = result[:, s * width : (s + 1) * width]


def first_section(received, tables):
    parts, segs, rows, width = received.shape
    pair = 2
    return pl.pallas_call(
        first_kernel,
        grid=(segs // pair,),
        in_specs=[
            pl.BlockSpec((parts, pair, rows, width), lambda i: (0, i, 0, 0)),
            pl.BlockSpec((A, A), lambda i: (0, 0)),
            pl.BlockSpec((A, A), lambda i: (0, 0)),
        ],
        out_specs=pl.BlockSpec((pair, A, width), lambda i: (i, 0, 0)),
        out_shape=jax.ShapeDtypeStruct((segs, A, width), jnp.float32),
        compiler_params=pltpu.CompilerParams(vmem_limit_bytes=40 * 2**20),
        cost_estimate=pl.CostEstimate(
            flops=2 * 3 * segs * A * A * width, bytes_accessed=segs * A * width * 8, transcendentals=0
        ),
        name="first_section",
    )(received, *tables)


def second_kernel(
    y_ref, tc_ref, ts_ref, ec_ref, es_ref, ch_ref, cl_ref, sh_ref, sl_ref, wa_ref, wm_ref, q_ref, out_ref
):
    parts = y_ref.shape[0]
    joined = jnp.concatenate([y_ref[f, 0] for f in range(parts)], axis=1)
    real_raw = joined[:HALF]
    imag_raw = joined[HALF:]
    row_ids = lax.broadcasted_iota(jnp.int32, (HALF, B), 0)
    imag_in = jnp.where(row_ids == 0, 0.0, imag_raw)
    twist_cos = tc_ref[...]
    twist_sin = ts_ref[...]
    real_u = real_raw * twist_cos + imag_in * twist_sin
    imag_u = imag_in * twist_cos - real_raw * twist_sin
    edge = imag_raw[0:1]
    edge_rows = jnp.where(
        lax.broadcasted_iota(jnp.int32, (16, B), 0) == 0,
        edge * ec_ref[...],
        jnp.where(lax.broadcasted_iota(jnp.int32, (16, B), 0) == 1, -edge * es_ref[...], 0.0),
    )
    u_high, u_low = split_parts(jnp.concatenate([real_u, imag_u], axis=0))
    e_high, e_low = split_parts(edge_rows)

    def three(high_ref, low_ref, high, low):
        return (
            dot_nt(high_ref[...], high) + dot_nt(high_ref[...], low) + dot_nt(low_ref[...], high)
        )

    by_cos = three(ch_ref, cl_ref, u_high, u_low)
    by_sin = three(sh_ref, sl_ref, u_high, u_low)
    edge_cos = three(ch_ref, cl_ref, e_high, e_low)[:NB]
    edge_sin = three(sh_ref, sl_ref, e_high, e_low)[:NB]
    white = wa_ref[...]
    real_out = ((by_cos[:NB, :HALF] + by_sin[:NB, HALF:]) * white).astype(jnp.bfloat16)
    imag_out = ((by_cos[:NB, HALF:] - by_sin[:NB, :HALF]) * white).astype(jnp.bfloat16)
    next_cos = by_cos[1 : NB + 1]
    next_sin = by_sin[1 : NB + 1]
    lane = lax.broadcasted_iota(jnp.int32, (NB, HALF), 1)
    real_edge = edge_cos[:, 0:1] + edge_sin[:, 1:2]
    imag_edge = edge_cos[:, 1:2] - edge_sin[:, 0:1]
    real_far = jnp.where(lane == 0, real_edge, next_cos[:, :HALF] - next_sin[:, HALF:])
    imag_far = jnp.where(lane == 0, imag_edge, -next_cos[:, HALF:] - next_sin[:, :HALF])
    white_far = wm_ref[...]
    order = q_ref[...]
    real_far = dot_nn((real_far * white_far).astype(jnp.bfloat16), order).astype(jnp.bfloat16)
    imag_far = dot_nn((imag_far * white_far).astype(jnp.bfloat16), order).astype(jnp.bfloat16)
    rows = NB // parts
    for f in range(parts):
        here = slice(f * rows, (f + 1) * rows)
        out_ref[f, 0, 0, :, :HALF] = real_out[here]
        out_ref[f, 0, 0, :, HALF:] = real_far[here]
        out_ref[f, 0, 1, :, :HALF] = imag_out[here]
        out_ref[f, 0, 1, :, HALF:] = imag_far[here]


def second_section(received, tables, white, white_far):
    parts, segs, rows, width = received.shape
    twists, seconds, order = tables

    def whole(array):
        return pl.BlockSpec(array.shape, lambda i: (0,) * array.ndim)

    fixed = (*twists, *seconds, white, white_far, order)
    return pl.pallas_call(
        second_kernel,
        grid=(segs,),
        in_specs=[pl.BlockSpec((parts, 1, rows, width), lambda i: (0, i, 0, 0))]
        + [whole(array) for array in fixed],
        out_specs=pl.BlockSpec((parts, 1, 2, NB // parts, A), lambda i: (0, i, 0, 0, 0)),
        out_shape=jax.ShapeDtypeStruct((parts, segs, 2, NB // parts, A), jnp.bfloat16),
        compiler_params=pltpu.CompilerParams(vmem_limit_bytes=60 * 2**20),
        cost_estimate=pl.CostEstimate(
            flops=2 * 6 * segs * 528 * B * A, bytes_accessed=segs * A * B * 6, transcendentals=0
        ),
        name="second_section",
    )(received, *fixed)


def lag_kernel(place_ref, a_ref, b_ref, x_ref, y_ref, t_ref, c_ref, s_ref, out_ref, acc_ref, even_ref, odd_ref):
    sources = (a_ref, b_ref, x_ref, y_ref)
    segs = a_ref.shape[1] // 2
    depth = t_ref.shape[2]
    per_quad = depth // A
    lag_total = c_ref.shape[1]
    tmpl = out_ref.shape[2]
    step = pl.program_id(0)
    last = pl.num_programs(0) - 1
    half = len(sources) * segs * lag_total

    def make_rows(rows_ref, jj):
        for chunk in range(A // 128):
            lanes = slice(chunk * 128, (chunk + 1) * 128)
            lag_cos = c_ref[jj, :, lanes]
            lag_sin = s_ref[jj, :, lanes]
            out_lanes = slice(jj * A + chunk * 128, jj * A + (chunk + 1) * 128)
            for index, source in enumerate(sources):
                value = source[jj, :, lanes].astype(jnp.float32)
                for s in range(segs):
                    real = value[s : s + 1]
                    imag = value[segs + s : segs + s + 1]
                    first_row = (index * segs + s) * lag_total
                    rows = slice(first_row, first_row + lag_total)
                    rows_ref[rows, out_lanes] = (real * lag_cos - imag * lag_sin).astype(jnp.bfloat16)
                    rows = slice(half + first_row, half + first_row + lag_total)
                    rows_ref[rows, out_lanes] = (real * lag_sin + imag * lag_cos).astype(jnp.bfloat16)

    def multiply(now_ref, next_ref):
        cut = max(1, per_quad // 2)
        pieces = [(k, n) for k in range(per_quad // cut) for n in range(2)]
        for index, (k, n) in enumerate(pieces):
            if next_ref is not None:
                for jj in range(per_quad):
                    if jj * len(pieces) // per_quad == index:
                        make_rows(next_ref, jj)
            deep = slice(k * cut * A, (k + 1) * cut * A)
            cols = slice(n * tmpl, (n + 1) * tmpl)
            acc_ref[:, cols] += dot_nt(now_ref[:, deep], t_ref[0, cols, deep])

    @pl.when(step == 0)
    def _():
        acc_ref[...] = jnp.zeros_like(acc_ref)
        for jj in range(per_quad):
            make_rows(even_ref, jj)

    @pl.when((step % 2 == 1) & (step < last))
    def _():
        multiply(even_ref, odd_ref)

    @pl.when((step % 2 == 0) & (step > 0) & (step < last))
    def _():
        multiply(odd_ref, even_ref)

    @pl.when(step == last)
    def _():
        multiply(odd_ref, None)
        shape = (segs, lag_total, tmpl)
        for index in range(len(sources)):
            low = slice(index * segs * lag_total, (index + 1) * segs * lag_total)
            high = slice(half + low.start, half + low.stop)
            place = pl.ds((place_ref[0] ^ index) * segs, segs)
            out_ref[place, :lag_total] = (acc_ref[low, :tmpl] + acc_ref[high, tmpl:]).reshape(shape)
            out_ref[place, lag_total:] = (acc_ref[high, :tmpl] - acc_ref[low, tmpl:]).reshape(shape)


def lag_products(sources, place, laid, lag_cos, lag_sin):
    blocks, rows, _ = sources[0].shape
    quads, tmpl2, depth = laid.shape
    per_quad = depth // A
    lag_total = lag_cos.shape[1]
    segs = len(sources) * rows // 2

    def ahead(i):
        return (jnp.minimum(i, quads - 1), 0, 0)

    return pl.pallas_call(
        lag_kernel,
        grid=(quads + 1,),
        in_specs=[pl.BlockSpec(memory_space=pltpu.SMEM)]
        + [pl.BlockSpec((per_quad, rows, A), ahead)] * len(sources)
        + [
            pl.BlockSpec((1, tmpl2, depth), lambda i: (jnp.maximum(i - 1, 0), 0, 0)),
            pl.BlockSpec((per_quad, lag_total, A), ahead),
            pl.BlockSpec((per_quad, lag_total, A), ahead),
        ],
        out_specs=pl.BlockSpec((segs, 2 * lag_total, tmpl2 // 2), lambda i: (0, 0, 0)),
        out_shape=jax.ShapeDtypeStruct((segs, 2 * lag_total, tmpl2 // 2), jnp.float32),
        scratch_shapes=[
            pltpu.VMEM((2 * segs * lag_total, tmpl2), jnp.float32),
            pltpu.VMEM((2 * segs * lag_total, depth), jnp.bfloat16),
            pltpu.VMEM((2 * segs * lag_total, depth), jnp.bfloat16),
        ],
        compiler_params=pltpu.CompilerParams(vmem_limit_bytes=60 * 2**20),
        cost_estimate=pl.CostEstimate(
            flops=4 * segs * lag_total * tmpl2 * blocks * A,
            bytes_accessed=blocks * A * (tmpl2 * 2 + segs * 4),
            transcendentals=0,
        ),
        name="lag_products",
    )(place, *sources, laid, lag_cos, lag_sin)


def block_rows(data):
    segs, parts, blocks, _ = data.shape
    return data.transpose(2, 1, 0, 3).reshape(blocks, parts * segs, A)


def spread(data):
    def swap(value, bit):
        return lax.ppermute(value, "tmpl", [(n, n ^ bit) for n in range(4)])

    middle = data.shape[0] // 2
    first = swap(data, 1)
    second = swap(data, 2)
    corner = jnp.concatenate([swap(first[:middle], 2), swap(second[middle:], 1)], axis=0)
    return data, first, second, corner


def layout_kernel(cut_ref, t_ref, *refs):
    out_ref = refs[-1]
    tmpl, _, rows, _ = t_ref.shape
    per_quad = out_ref.shape[3] // A
    first_row = pl.program_id(0) * rows + cut_ref[cut_ref.shape[0] - 1]
    first_tmpl = pl.program_id(1) * tmpl
    row_ids = lax.broadcasted_iota(jnp.int32, (rows, 128), 0) + first_row
    batch = 16

    @pl.loop(0, tmpl // batch)
    def _(group):
        some = pl.ds(pl.multiple_of(group * batch, batch), batch)
        keeps = [row_ids < cut_ref[first_tmpl + group * batch + n] for n in range(batch)]
        for part in range(2):
            for chunk in range(A // 128):
                lanes = slice(chunk * 128, (chunk + 1) * 128)
                value = t_ref[some, part, :, lanes].astype(jnp.float32)
                value = jnp.stack([jnp.where(keeps[n], value[n], 0.0) for n in range(batch)], axis=0)
                value = jnp.swapaxes(value, 0, 1).astype(jnp.bfloat16)
                for row in range(rows):
                    start = row % per_quad * A + chunk * 128
                    out_ref[row // per_quad, part, some, start : start + 128] = value[row]


def lay_out(templates, cuts, per_quad, piece, pieces, laid):
    tmpl, _, blocks, _ = templates.shape
    rows = min(16, blocks)
    steps = blocks // rows // pieces
    batch = min(64, tmpl)
    shape = (blocks // per_quad, 2, tmpl, per_quad * A)
    first = piece * steps
    info = jnp.concatenate([cuts, jnp.full((1,), first * rows, jnp.int32)])
    earlier = () if laid is None else (laid,)
    return pl.pallas_call(
        layout_kernel,
        grid=(steps, tmpl // batch),
        in_specs=[
            pl.BlockSpec(memory_space=pltpu.SMEM),
            pl.BlockSpec((batch, 2, rows, A), lambda i, j: (j, 0, i + first, 0)),
        ]
        + [pl.BlockSpec(memory_space=pl.ANY)] * len(earlier),
        out_specs=pl.BlockSpec(
            (rows // per_quad, 2, batch, per_quad * A), lambda i, j: (i + first, 0, j, 0)
        ),
        out_shape=jax.ShapeDtypeStruct(shape, jnp.bfloat16),
        input_output_aliases={2: 0} if earlier else {},
        compiler_params=pltpu.CompilerParams(vmem_limit_bytes=40 * 2**20),
        cost_estimate=pl.CostEstimate(
            flops=0, bytes_accessed=8 * tmpl * 2 * blocks * A // pieces, transcendentals=0
        ),
        name="lay_out",
    )(info, templates, *earlier)


def general_transform(strain, psd):
    freq_count = lax.axis_size("freq")
    freq_index = lax.axis_index("freq")
    seg_local = strain.shape[0]
    step_time = B // freq_count
    highest = lax.Precision.HIGHEST
    first_cos, first_sin = cos_sin_table(
        jnp.arange(A, dtype=jnp.int32), jnp.arange(A, dtype=jnp.int32), A
    )
    table = jnp.concatenate([first_cos, -first_sin], axis=0)
    time_ids = freq_index * step_time + jnp.arange(step_time, dtype=jnp.int32)
    twist_cos, twist_sin = cos_sin_table(jnp.arange(A, dtype=jnp.int32), time_ids, LEN)
    slab_blocks = strain.reshape(seg_local, A // freq_count, B)
    both_parts = jnp.einsum(
        "kn,snb->skb",
        table,
        lax.all_to_all(slab_blocks, "freq", split_axis=2, concat_axis=1, tiled=True),
        precision=highest,
    )
    real_part = both_parts[:, :A]
    imag_part = both_parts[:, A:]
    second_cos, second_sin = cos_sin_table(
        jnp.arange(B, dtype=jnp.int32), jnp.arange(NB, dtype=jnp.int32), B
    )
    rotation = jnp.concatenate(
        [
            jnp.concatenate([second_cos, -second_sin], axis=1),
            jnp.concatenate([second_sin, second_cos], axis=1),
        ],
        axis=0,
    )
    amplitude = jnp.sqrt(LEN * psd)
    real_in = lax.all_to_all(
        real_part * twist_cos + imag_part * twist_sin, "freq", split_axis=1, concat_axis=2, tiled=True
    )
    imag_in = lax.all_to_all(
        imag_part * twist_cos - real_part * twist_sin, "freq", split_axis=1, concat_axis=2, tiled=True
    )
    joined = jnp.concatenate([real_in, imag_in], axis=2)
    both_out = jnp.einsum("spc,cm->smp", joined, rotation, precision=highest)
    both_out = both_out.reshape(joined.shape[0], 2, NB, joined.shape[1])
    whitened = (both_out / amplitude).astype(jnp.bfloat16)
    return lax.all_to_all(whitened, "freq", split_axis=2, concat_axis=3, tiled=True)


def exchange(sent):
    return lax.all_to_all(sent, "freq", split_axis=0, concat_axis=0, tiled=True)


def pack_strain(strain, freq_count):
    seg_local = strain.shape[0]
    sent = (strain * STRAIN_SCALE).astype(jnp.float16)
    sent = sent.reshape(seg_local, A // freq_count, freq_count, B // freq_count)
    return sent.transpose(2, 0, 1, 3)


def pack_coefs(received, table):
    freq_count, seg_local, _, width = received.shape
    coefs = first_section(received.astype(jnp.float32) * (1.0 / STRAIN_SCALE), table)
    sent = (coefs * COEF_SCALE).astype(jnp.float16)
    return sent.reshape(freq_count, seg_local // freq_count, A, width)


def whiten(received, tables, white, white_far):
    return second_section(received.astype(jnp.float32) * (1.0 / COEF_SCALE), tables, white, white_far)


def on_device(strain, psd, templates, cutoffs, lags):
    freq_count = lax.axis_size("freq")
    freq_index = lax.axis_index("freq")
    seg_local = strain.shape[0]
    tmpl_local = templates.shape[0]
    blocks_here = templates.shape[2]
    first_block = freq_index * blocks_here
    block_ids = first_block + jnp.arange(blocks_here, dtype=jnp.int32)
    per_quad = min(4, blocks_here)
    quads = blocks_here // per_quad
    cuts = cutoffs - first_block
    tied = lax.optimization_barrier

    block_cos, block_sin = cos_sin_table(block_ids, lags % B, B)
    place = lags[:, None] * jnp.arange(A, dtype=jnp.int32)[None, :] % LEN
    place_angle = place.astype(jnp.float32) * (two_pi / LEN)
    place_cos = jnp.cos(place_angle)[None]
    place_sin = jnp.sin(place_angle)[None]
    block_cos = block_cos[:, :, None]
    block_sin = block_sin[:, :, None]
    lag_cos = block_cos * place_cos - block_sin * place_sin
    lag_sin = block_sin * place_cos + block_cos * place_sin

    sliced = (
        lax.axis_size("tmpl") == 4
        and seg_local == 2 * freq_count == 16
        and (NB // freq_count) % 32 == 0
        and B // freq_count == 128
    )
    if not sliced:
        laid = lay_out(templates, cuts, per_quad, 0, 1, None)
        laid = laid.reshape(quads, 2 * tmpl_local, per_quad * A)
        data = lax.all_gather(general_transform(strain, psd), "tmpl", axis=0, tiled=True)
        origin = jnp.zeros((1,), jnp.int32)
        sums = []
        for start in range(0, data.shape[0], 16):
            sources = [block_rows(data[n : n + 4]) for n in range(start, start + 16, 4)]
            sums.append(lag_products(sources, origin, laid, lag_cos, lag_sin))
        sums = jnp.concatenate(sums, axis=0)
        return lax.psum_scatter(sums, "freq", scatter_dimension=0, tiled=True)

    order = mirror_table()
    psd_all = lax.all_gather(psd, "freq", axis=1, tiled=True)
    psd_far = jnp.dot(psd_all[:, HALF:], order.T, precision=lax.Precision.HIGHEST)
    white = lax.rsqrt(LEN * psd_all[:, :HALF])
    white_far = lax.rsqrt(LEN * psd_far)
    first = first_table()
    second = (twist_tables(), second_tables(), order.astype(ml_dtypes.bfloat16))

    seg_out = seg_local * lax.axis_size("tmpl") // freq_count
    by_owner = strain.reshape(seg_local // seg_out, 2, seg_out // 2, strain.shape[1])
    strain_a, strain_b = (
        pack_strain(by_owner[:, group].reshape(seg_local // 2, strain.shape[1]), freq_count)
        for group in range(2)
    )
    time_a = exchange(strain_a)
    laid = lay_out(templates, cuts, per_quad, 0, 2, None)
    time_a, laid = tied((time_a, laid))
    coefs_a = pack_coefs(time_a, first)
    parts_a = exchange(coefs_a)
    laid = lay_out(templates, cuts, per_quad, 1, 2, laid)
    parts_a, strain_b, laid, white, white_far, lag_cos, lag_sin = tied(
        (parts_a, strain_b, laid, white, white_far, lag_cos, lag_sin)
    )
    time_b = exchange(strain_b)
    white_a = whiten(parts_a, second, white, white_far)
    time_b, white_a = tied((time_b, white_a))
    data_a = exchange(white_a)
    coefs_b = pack_coefs(time_b, first)
    data_a, coefs_b = tied((data_a, coefs_b))
    parts_b = exchange(coefs_b)
    laid = laid.reshape(quads, 2 * tmpl_local, per_quad * A)
    place = lax.axis_index("tmpl").astype(jnp.int32).reshape(1)

    def halves(data):
        data = data.reshape(2, 2, 2, 2, blocks_here, A)
        return [spread(block_rows(data[:, n].reshape(4, 2, blocks_here, A))) for n in range(2)]

    def collect(sums):
        return lax.psum_scatter(sums, "freq", scatter_dimension=0, tiled=True)

    first_a, second_a = halves(data_a)
    white_b = whiten(parts_b, second, white, white_far)
    first_a = tied((first_a, white_b))[0]
    data_b = exchange(white_b)
    sums_a = lag_products(first_a, place, laid, lag_cos, lag_sin)
    data_b, sums_a = tied((data_b, sums_a))
    first_b, second_b = halves(data_b)
    sums = [sums_a] + [
        lag_products(part, place, laid, lag_cos, lag_sin) for part in (second_a, first_b, second_b)
    ]
    outputs = [collect(part) for part in sums[:3]]
    shares = exchange(sums[3].reshape(freq_count, 2, 2 * lags.shape[0], tmpl_local))
    outputs.append(jnp.sum(shares, axis=0))
    return jnp.concatenate(outputs, axis=0)


def solution(mesh):
    placed = (P("tmpl", "freq"), P(None, "freq"), P("tmpl", None, "freq", None), P("tmpl"), P())
    return jax.shard_map(
        on_device, mesh=mesh, in_specs=placed, out_specs=P("freq", None, "tmpl"), check_vma=False
    )
```

```python
import math

import jax
import jax.numpy as jnp
import ml_dtypes
import numpy as np
from jax import lax
from jax.experimental import pallas as pl
from jax.experimental.pallas import tpu as pltpu
from jax.sharding import PartitionSpec as P

A = 512
B = 1024
LEN = 524288
NB = 512
HALF = A // 2

STRAIN_SCALE = 8192.0
COEF_SCALE = 16.0

two_pi = 2.0 * math.pi


def cos_sin_table(row_ids, col_ids, modulus):
    product = row_ids[:, None] * col_ids[None, :] % modulus
    phase_angle = product.astype(jnp.float32) * (two_pi / modulus)
    return (jnp.cos(phase_angle), jnp.sin(phase_angle))


def split_const(table):
    high = table.astype(ml_dtypes.bfloat16)
    low = (table - high.astype(np.float64)).astype(ml_dtypes.bfloat16)
    return high, low


def first_table():
    angle = two_pi * (np.outer(np.arange(HALF), np.arange(A)) % A) / A
    table = np.concatenate([np.cos(angle), -np.sin(angle)], axis=0)
    table[HALF] = 1.0 - 2.0 * (np.arange(A) % 2)
    return split_const(table)


def second_tables():
    angle = two_pi * (np.outer(np.arange(528), np.arange(B)) % B) / B
    return split_const(np.cos(angle)) + split_const(np.sin(angle))


def twist_tables():
    angle = two_pi * np.outer(np.arange(HALF), np.arange(B)) / LEN
    edge = two_pi * HALF * np.arange(B)[None, :] / LEN
    return (
        np.cos(angle).astype(np.float32),
        np.sin(angle).astype(np.float32),
        np.cos(edge).astype(np.float32),
        np.sin(edge).astype(np.float32),
    )


def mirror_table():
    table = np.zeros((HALF, HALF), np.float32)
    table[0, 0] = 1.0
    table[np.arange(1, HALF), HALF - np.arange(1, HALF)] = 1.0
    return table


def split_parts(value):
    high = value.astype(jnp.bfloat16)
    low = (value - high.astype(jnp.float32)).astype(jnp.bfloat16)
    return high, low


def dot_nn(lhs, rhs):
    return lax.dot_general(lhs, rhs, (((1,), (0,)), ((), ())), preferred_element_type=jnp.float32)


def dot_nt(lhs, rhs):
    return lax.dot_general(lhs, rhs, (((1,), (1,)), ((), ())), preferred_element_type=jnp.float32)


def first_kernel(x_ref, high_ref, low_ref, out_ref):
    parts = x_ref.shape[0]
    pair = x_ref.shape[1]
    columns = []
    for s in range(pair):
        columns.append(jnp.concatenate([x_ref[f, s] for f in range(parts)], axis=0))
    value = jnp.concatenate(columns, axis=1)
    high, low = split_parts(value)
    result = dot_nn(high_ref[...], high) + dot_nn(high_ref[...], low) + dot_nn(low_ref[...], high)
    width = x_ref.shape[3]
    for s in range(pair):
        out_ref[s] = result[:, s * width : (s + 1) * width]


def first_section(received, tables):
    parts, segs, rows, width = received.shape
    pair = 2
    return pl.pallas_call(
        first_kernel,
        grid=(segs // pair,),
        in_specs=[
            pl.BlockSpec((parts, pair, rows, width), lambda i: (0, i, 0, 0)),
            pl.BlockSpec((A, A), lambda i: (0, 0)),
            pl.BlockSpec((A, A), lambda i: (0, 0)),
        ],
        out_specs=pl.BlockSpec((pair, A, width), lambda i: (i, 0, 0)),
        out_shape=jax.ShapeDtypeStruct((segs, A, width), jnp.float32),
        compiler_params=pltpu.CompilerParams(vmem_limit_bytes=40 * 2**20),
        cost_estimate=pl.CostEstimate(
            flops=2 * 3 * segs * A * A * width, bytes_accessed=segs * A * width * 8, transcendentals=0
        ),
        name="first_section",
    )(received, *tables)


def second_kernel(
    y_ref, tc_ref, ts_ref, ec_ref, es_ref, ch_ref, cl_ref, sh_ref, sl_ref, wa_ref, wm_ref, q_ref, out_ref
):
    parts = y_ref.shape[0]
    joined = jnp.concatenate([y_ref[f, 0] for f in range(parts)], axis=1)
    real_raw = joined[:HALF]
    imag_raw = joined[HALF:]
    row_ids = lax.broadcasted_iota(jnp.int32, (HALF, B), 0)
    imag_in = jnp.where(row_ids == 0, 0.0, imag_raw)
    twist_cos = tc_ref[...]
    twist_sin = ts_ref[...]
    real_u = real_raw * twist_cos + imag_in * twist_sin
    imag_u = imag_in * twist_cos - real_raw * twist_sin
    edge = imag_raw[0:1]
    edge_rows = jnp.where(
        lax.broadcasted_iota(jnp.int32, (16, B), 0) == 0,
        edge * ec_ref[...],
        jnp.where(lax.broadcasted_iota(jnp.int32, (16, B), 0) == 1, -edge * es_ref[...], 0.0),
    )
    u_high, u_low = split_parts(jnp.concatenate([real_u, imag_u], axis=0))
    e_high, e_low = split_parts(edge_rows)

    def three(high_ref, low_ref, high, low):
        return (
            dot_nt(high_ref[...], high) + dot_nt(high_ref[...], low) + dot_nt(low_ref[...], high)
        )

    by_cos = three(ch_ref, cl_ref, u_high, u_low)
    by_sin = three(sh_ref, sl_ref, u_high, u_low)
    edge_cos = three(ch_ref, cl_ref, e_high, e_low)[:NB]
    edge_sin = three(sh_ref, sl_ref, e_high, e_low)[:NB]
    white = wa_ref[...]
    real_out = ((by_cos[:NB, :HALF] + by_sin[:NB, HALF:]) * white).astype(jnp.bfloat16)
    imag_out = ((by_cos[:NB, HALF:] - by_sin[:NB, :HALF]) * white).astype(jnp.bfloat16)
    next_cos = by_cos[1 : NB + 1]
    next_sin = by_sin[1 : NB + 1]
    lane = lax.broadcasted_iota(jnp.int32, (NB, HALF), 1)
    real_edge = edge_cos[:, 0:1] + edge_sin[:, 1:2]
    imag_edge = edge_cos[:, 1:2] - edge_sin[:, 0:1]
    real_far = jnp.where(lane == 0, real_edge, next_cos[:, :HALF] - next_sin[:, HALF:])
    imag_far = jnp.where(lane == 0, imag_edge, -next_cos[:, HALF:] - next_sin[:, :HALF])
    white_far = wm_ref[...]
    order = q_ref[...]
    real_far = dot_nn((real_far * white_far).astype(jnp.bfloat16), order).astype(jnp.bfloat16)
    imag_far = dot_nn((imag_far * white_far).astype(jnp.bfloat16), order).astype(jnp.bfloat16)
    rows = NB // parts
    for f in range(parts):
        here = slice(f * rows, (f + 1) * rows)
        out_ref[f, 0, 0, :, :HALF] = real_out[here]
        out_ref[f, 0, 0, :, HALF:] = real_far[here]
        out_ref[f, 0, 1, :, :HALF] = imag_out[here]
        out_ref[f, 0, 1, :, HALF:] = imag_far[here]


def second_section(received, tables, white, white_far):
    parts, segs, rows, width = received.shape
    twists, seconds, order = tables

    def whole(array):
        return pl.BlockSpec(array.shape, lambda i: (0,) * array.ndim)

    fixed = (*twists, *seconds, white, white_far, order)
    return pl.pallas_call(
        second_kernel,
        grid=(segs,),
        in_specs=[pl.BlockSpec((parts, 1, rows, width), lambda i: (0, i, 0, 0))]
        + [whole(array) for array in fixed],
        out_specs=pl.BlockSpec((parts, 1, 2, NB // parts, A), lambda i: (0, i, 0, 0, 0)),
        out_shape=jax.ShapeDtypeStruct((parts, segs, 2, NB // parts, A), jnp.bfloat16),
        compiler_params=pltpu.CompilerParams(vmem_limit_bytes=60 * 2**20),
        cost_estimate=pl.CostEstimate(
            flops=2 * 6 * segs * 528 * B * A, bytes_accessed=segs * A * B * 6, transcendentals=0
        ),
        name="second_section",
    )(received, *fixed)


def lag_kernel(place_ref, a_ref, b_ref, x_ref, y_ref, t_ref, c_ref, s_ref, out_ref, acc_ref, even_ref, odd_ref):
    sources = (a_ref, b_ref, x_ref, y_ref)
    segs = a_ref.shape[1] // 2
    depth = t_ref.shape[2]
    per_quad = depth // A
    lag_total = c_ref.shape[1]
    tmpl = out_ref.shape[2]
    step = pl.program_id(0)
    last = pl.num_programs(0) - 1

    def make_rows(rows_ref, jj):
        for chunk in range(A // 128):
            lanes = slice(chunk * 128, (chunk + 1) * 128)
            lag_cos = c_ref[jj, :, lanes]
            lag_sin = s_ref[jj, :, lanes]
            out_lanes = slice(jj * A + chunk * 128, jj * A + (chunk + 1) * 128)
            for index, source in enumerate(sources):
                value = source[jj, :, lanes].astype(jnp.float32)
                for s in range(segs):
                    real = value[s : s + 1]
                    imag = value[segs + s : segs + s + 1]
                    first_row = (index * segs + s) * lag_total
                    rows = slice(first_row, first_row + lag_total)
                    real_q = (real * lag_cos - imag * lag_sin).astype(jnp.bfloat16)
                    imag_q = (real * lag_sin + imag * lag_cos).astype(jnp.bfloat16)
                    rows_ref[0, rows, out_lanes] = real_q
                    rows_ref[1, rows, out_lanes] = imag_q - real_q
                    rows_ref[2, rows, out_lanes] = imag_q + real_q

    def multiply(now_ref, next_ref):
        cut = max(1, per_quad // 2)
        pieces = [(k, n) for k in range(per_quad // cut) for n in range(3)]
        for index, (k, n) in enumerate(pieces):
            if next_ref is not None:
                for jj in range(per_quad):
                    if jj * len(pieces) // per_quad == index:
                        make_rows(next_ref, jj)
            deep = slice(k * cut * A, (k + 1) * cut * A)
            if n == 0:
                columns = t_ref[0, :tmpl, deep] - t_ref[0, tmpl:, deep]
            else:
                columns = t_ref[0, (n - 1) * tmpl : n * tmpl, deep]
            acc_ref[n] += dot_nt(now_ref[n, :, deep], columns)

    @pl.when(step == 0)
    def _():
        acc_ref[...] = jnp.zeros_like(acc_ref)
        for jj in range(per_quad):
            make_rows(even_ref, jj)

    @pl.when((step % 2 == 1) & (step < last))
    def _():
        multiply(even_ref, odd_ref)

    @pl.when((step % 2 == 0) & (step > 0) & (step < last))
    def _():
        multiply(odd_ref, even_ref)

    @pl.when(step == last)
    def _():
        multiply(odd_ref, None)
        shape = (segs, lag_total, tmpl)
        for index in range(len(sources)):
            rows = slice(index * segs * lag_total, (index + 1) * segs * lag_total)
            place = pl.ds((place_ref[0] ^ index) * segs, segs)
            out_ref[place, :lag_total] = (acc_ref[0, rows] + acc_ref[2, rows]).reshape(shape)
            out_ref[place, lag_total:] = (acc_ref[0, rows] + acc_ref[1, rows]).reshape(shape)


def lag_products(sources, place, laid, lag_cos, lag_sin):
    blocks, rows, _ = sources[0].shape
    quads, tmpl2, depth = laid.shape
    per_quad = depth // A
    lag_total = lag_cos.shape[1]
    segs = len(sources) * rows // 2

    def ahead(i):
        return (jnp.minimum(i, quads - 1), 0, 0)

    return pl.pallas_call(
        lag_kernel,
        grid=(quads + 1,),
        in_specs=[pl.BlockSpec(memory_space=pltpu.SMEM)]
        + [pl.BlockSpec((per_quad, rows, A), ahead)] * len(sources)
        + [
            pl.BlockSpec((1, tmpl2, depth), lambda i: (jnp.maximum(i - 1, 0), 0, 0)),
            pl.BlockSpec((per_quad, lag_total, A), ahead),
            pl.BlockSpec((per_quad, lag_total, A), ahead),
        ],
        out_specs=pl.BlockSpec((segs, 2 * lag_total, tmpl2 // 2), lambda i: (0, 0, 0)),
        out_shape=jax.ShapeDtypeStruct((segs, 2 * lag_total, tmpl2 // 2), jnp.float32),
        scratch_shapes=[
            pltpu.VMEM((3, segs * lag_total, tmpl2 // 2), jnp.float32),
            pltpu.VMEM((3, segs * lag_total, depth), jnp.bfloat16),
            pltpu.VMEM((3, segs * lag_total, depth), jnp.bfloat16),
        ],
        compiler_params=pltpu.CompilerParams(vmem_limit_bytes=60 * 2**20),
        cost_estimate=pl.CostEstimate(
            flops=3 * segs * lag_total * tmpl2 * blocks * A,
            bytes_accessed=blocks * A * (tmpl2 * 2 + segs * 4),
            transcendentals=0,
        ),
        name="lag_products",
    )(place, *sources, laid, lag_cos, lag_sin)


def block_rows(data):
    segs, parts, blocks, _ = data.shape
    return data.transpose(2, 1, 0, 3).reshape(blocks, parts * segs, A)


def spread(data):
    def swap(value, bit):
        return lax.ppermute(value, "tmpl", [(n, n ^ bit) for n in range(4)])

    return (data,) + tuple(swap(data, bit) for bit in (1, 2, 3))


def layout_kernel(cut_ref, t_ref, *refs):
    out_ref = refs[-1]
    tmpl, _, rows, _ = t_ref.shape
    per_quad = out_ref.shape[3] // A
    first_row = pl.program_id(0) * rows + cut_ref[cut_ref.shape[0] - 1]
    first_tmpl = pl.program_id(1) * tmpl
    row_ids = lax.broadcasted_iota(jnp.int32, (rows, 128), 0) + first_row
    batch = 16

    @pl.loop(0, tmpl // batch)
    def _(group):
        some = pl.ds(pl.multiple_of(group * batch, batch), batch)
        keeps = [row_ids < cut_ref[first_tmpl + group * batch + n] for n in range(batch)]
        for part in range(2):
            for chunk in range(A // 128):
                lanes = slice(chunk * 128, (chunk + 1) * 128)
                value = t_ref[some, part, :, lanes].astype(jnp.float32)
                value = jnp.stack([jnp.where(keeps[n], value[n], 0.0) for n in range(batch)], axis=0)
                value = jnp.swapaxes(value, 0, 1).astype(jnp.bfloat16)
                for row in range(rows):
                    start = row % per_quad * A + chunk * 128
                    out_ref[row // per_quad, part, some, start : start + 128] = value[row]


def lay_out(templates, cuts, per_quad, piece, pieces, laid):
    tmpl, _, blocks, _ = templates.shape
    rows = min(16, blocks)
    steps = blocks // rows // pieces
    batch = min(64, tmpl)
    shape = (blocks // per_quad, 2, tmpl, per_quad * A)
    first = piece * steps
    info = jnp.concatenate([cuts, jnp.full((1,), first * rows, jnp.int32)])
    earlier = () if laid is None else (laid,)
    return pl.pallas_call(
        layout_kernel,
        grid=(steps, tmpl // batch),
        in_specs=[
            pl.BlockSpec(memory_space=pltpu.SMEM),
            pl.BlockSpec((batch, 2, rows, A), lambda i, j: (j, 0, i + first, 0)),
        ]
        + [pl.BlockSpec(memory_space=pl.ANY)] * len(earlier),
        out_specs=pl.BlockSpec(
            (rows // per_quad, 2, batch, per_quad * A), lambda i, j: (i + first, 0, j, 0)
        ),
        out_shape=jax.ShapeDtypeStruct(shape, jnp.bfloat16),
        input_output_aliases={2: 0} if earlier else {},
        compiler_params=pltpu.CompilerParams(vmem_limit_bytes=40 * 2**20),
        cost_estimate=pl.CostEstimate(
            flops=0, bytes_accessed=8 * tmpl * 2 * blocks * A // pieces, transcendentals=0
        ),
        name="lay_out",
    )(info, templates, *earlier)


def general_transform(strain, psd):
    freq_count = lax.axis_size("freq")
    freq_index = lax.axis_index("freq")
    seg_local = strain.shape[0]
    step_time = B // freq_count
    highest = lax.Precision.HIGHEST
    first_cos, first_sin = cos_sin_table(
        jnp.arange(A, dtype=jnp.int32), jnp.arange(A, dtype=jnp.int32), A
    )
    table = jnp.concatenate([first_cos, -first_sin], axis=0)
    time_ids = freq_index * step_time + jnp.arange(step_time, dtype=jnp.int32)
    twist_cos, twist_sin = cos_sin_table(jnp.arange(A, dtype=jnp.int32), time_ids, LEN)
    slab_blocks = strain.reshape(seg_local, A // freq_count, B)
    both_parts = jnp.einsum(
        "kn,snb->skb",
        table,
        lax.all_to_all(slab_blocks, "freq", split_axis=2, concat_axis=1, tiled=True),
        precision=highest,
    )
    real_part = both_parts[:, :A]
    imag_part = both_parts[:, A:]
    second_cos, second_sin = cos_sin_table(
        jnp.arange(B, dtype=jnp.int32), jnp.arange(NB, dtype=jnp.int32), B
    )
    rotation = jnp.concatenate(
        [
            jnp.concatenate([second_cos, -second_sin], axis=1),
            jnp.concatenate([second_sin, second_cos], axis=1),
        ],
        axis=0,
    )
    amplitude = jnp.sqrt(LEN * psd)
    real_in = lax.all_to_all(
        real_part * twist_cos + imag_part * twist_sin, "freq", split_axis=1, concat_axis=2, tiled=True
    )
    imag_in = lax.all_to_all(
        imag_part * twist_cos - real_part * twist_sin, "freq", split_axis=1, concat_axis=2, tiled=True
    )
    joined = jnp.concatenate([real_in, imag_in], axis=2)
    both_out = jnp.einsum("spc,cm->smp", joined, rotation, precision=highest)
    both_out = both_out.reshape(joined.shape[0], 2, NB, joined.shape[1])
    whitened = (both_out / amplitude).astype(jnp.bfloat16)
    return lax.all_to_all(whitened, "freq", split_axis=2, concat_axis=3, tiled=True)


def exchange(sent):
    return lax.all_to_all(sent, "freq", split_axis=0, concat_axis=0, tiled=True)


def pack_strain(strain, freq_count):
    seg_local = strain.shape[0]
    sent = (strain * STRAIN_SCALE).astype(jnp.float16)
    sent = sent.reshape(seg_local, A // freq_count, freq_count, B // freq_count)
    return sent.transpose(2, 0, 1, 3)


def pack_coefs(received, table):
    freq_count, seg_local, _, width = received.shape
    coefs = first_section(received.astype(jnp.float32) * (1.0 / STRAIN_SCALE), table)
    sent = (coefs * COEF_SCALE).astype(jnp.float16)
    return sent.reshape(freq_count, seg_local // freq_count, A, width)


def whiten(received, tables, white, white_far):
    return second_section(received.astype(jnp.float32) * (1.0 / COEF_SCALE), tables, white, white_far)


def on_device(strain, psd, templates, cutoffs, lags):
    freq_count = lax.axis_size("freq")
    freq_index = lax.axis_index("freq")
    seg_local = strain.shape[0]
    tmpl_local = templates.shape[0]
    blocks_here = templates.shape[2]
    first_block = freq_index * blocks_here
    block_ids = first_block + jnp.arange(blocks_here, dtype=jnp.int32)
    per_quad = min(4, blocks_here)
    quads = blocks_here // per_quad
    cuts = cutoffs - first_block
    tied = lax.optimization_barrier

    block_cos, block_sin = cos_sin_table(block_ids, lags % B, B)
    place = lags[:, None] * jnp.arange(A, dtype=jnp.int32)[None, :] % LEN
    place_angle = place.astype(jnp.float32) * (two_pi / LEN)
    place_cos = jnp.cos(place_angle)[None]
    place_sin = jnp.sin(place_angle)[None]
    block_cos = block_cos[:, :, None]
    block_sin = block_sin[:, :, None]
    lag_cos = block_cos * place_cos - block_sin * place_sin
    lag_sin = block_sin * place_cos + block_cos * place_sin

    sliced = (
        lax.axis_size("tmpl") == 4
        and seg_local == 2 * freq_count == 16
        and (NB // freq_count) % 32 == 0
        and B // freq_count == 128
    )
    if not sliced:
        laid = lay_out(templates, cuts, per_quad, 0, 1, None)
        laid = laid.reshape(quads, 2 * tmpl_local, per_quad * A)
        data = lax.all_gather(general_transform(strain, psd), "tmpl", axis=0, tiled=True)
        origin = jnp.zeros((1,), jnp.int32)
        sums = []
        for start in range(0, data.shape[0], 16):
            sources = [block_rows(data[n : n + 4]) for n in range(start, start + 16, 4)]
            sums.append(lag_products(sources, origin, laid, lag_cos, lag_sin))
        sums = jnp.concatenate(sums, axis=0)
        return lax.psum_scatter(sums, "freq", scatter_dimension=0, tiled=True)

    order = mirror_table()
    psd_all = lax.all_gather(psd, "freq", axis=1, tiled=True)
    psd_far = jnp.dot(psd_all[:, HALF:], order.T, precision=lax.Precision.HIGHEST)
    white = lax.rsqrt(LEN * psd_all[:, :HALF])
    white_far = lax.rsqrt(LEN * psd_far)
    first = first_table()
    second = (twist_tables(), second_tables(), order.astype(ml_dtypes.bfloat16))

    seg_out = seg_local * lax.axis_size("tmpl") // freq_count
    by_owner = strain.reshape(seg_local // seg_out, 2, seg_out // 2, strain.shape[1])
    strain_a, strain_b = (
        pack_strain(by_owner[:, group].reshape(seg_local // 2, strain.shape[1]), freq_count)
        for group in range(2)
    )
    time_a = exchange(strain_a)
    laid = lay_out(templates, cuts, per_quad, 0, 2, None)
    time_a, laid = tied((time_a, laid))
    coefs_a = pack_coefs(time_a, first)
    parts_a = exchange(coefs_a)
    laid = lay_out(templates, cuts, per_quad, 1, 2, laid)
    parts_a, strain_b, laid, white, white_far, lag_cos, lag_sin = tied(
        (parts_a, strain_b, laid, white, white_far, lag_cos, lag_sin)
    )
    time_b = exchange(strain_b)
    white_a = whiten(parts_a, second, white, white_far)
    time_b, white_a = tied((time_b, white_a))
    data_a = exchange(white_a)
    coefs_b = pack_coefs(time_b, first)
    data_a, coefs_b = tied((data_a, coefs_b))
    parts_b = exchange(coefs_b)
    laid = laid.reshape(quads, 2 * tmpl_local, per_quad * A)
    place = lax.axis_index("tmpl").astype(jnp.int32).reshape(1)

    def halves(data):
        data = data.reshape(2, 2, 2, 2, blocks_here, A)
        return [spread(block_rows(data[:, n].reshape(4, 2, blocks_here, A))) for n in range(2)]

    def collect(sums):
        return lax.psum_scatter(sums, "freq", scatter_dimension=0, tiled=True)

    first_a, second_a = halves(data_a)
    white_b = whiten(parts_b, second, white, white_far)
    first_a = tied((first_a, white_b))[0]
    data_b = exchange(white_b)
    sums_a = lag_products(first_a, place, laid, lag_cos, lag_sin)
    data_b, sums_a = tied((data_b, sums_a))
    second_a = tied((second_a, data_b))[0]
    first_b, second_b = halves(data_b)
    sums = [sums_a] + [
        lag_products(part, place, laid, lag_cos, lag_sin) for part in (second_a, first_b, second_b)
    ]
    outputs = [collect(part) for part in sums[:3]]
    shares = exchange(sums[3].reshape(freq_count, 2, 2 * lags.shape[0], tmpl_local))
    outputs.append(jnp.sum(shares, axis=0))
    return jnp.concatenate(outputs, axis=0)


def solution(mesh):
    placed = (P("tmpl", "freq"), P(None, "freq"), P("tmpl", None, "freq", None), P("tmpl"), P())
    return jax.shard_map(
        on_device, mesh=mesh, in_specs=placed, out_specs=P("freq", None, "tmpl"), check_vma=False
    )
```

```python
import math

import jax
import jax.numpy as jnp
import ml_dtypes
import numpy as np
from jax import lax
from jax.experimental import pallas as pl
from jax.experimental.pallas import tpu as pltpu
from jax.sharding import PartitionSpec as P

A = 512
B = 1024
LEN = 524288
NB = 512
HALF = A // 2

STRAIN_SCALE = 8192.0
COEF_SCALE = 16.0

two_pi = 2.0 * math.pi


def cos_sin_table(row_ids, col_ids, modulus):
    product = row_ids[:, None] * col_ids[None, :] % modulus
    phase_angle = product.astype(jnp.float32) * (two_pi / modulus)
    return (jnp.cos(phase_angle), jnp.sin(phase_angle))


def split_const(table):
    high = table.astype(ml_dtypes.bfloat16)
    low = (table - high.astype(np.float64)).astype(ml_dtypes.bfloat16)
    return high, low


def first_table():
    angle = two_pi * (np.outer(np.arange(HALF), np.arange(A)) % A) / A
    table = np.concatenate([np.cos(angle), -np.sin(angle)], axis=0)
    table[HALF] = 1.0 - 2.0 * (np.arange(A) % 2)
    return split_const(table)


def second_tables():
    angle = two_pi * (np.outer(np.arange(528), np.arange(B)) % B) / B
    return split_const(np.cos(angle)) + split_const(np.sin(angle))


def twist_tables():
    angle = two_pi * np.outer(np.arange(HALF), np.arange(B)) / LEN
    edge = two_pi * HALF * np.arange(B)[None, :] / LEN
    return (
        np.cos(angle).astype(np.float32),
        np.sin(angle).astype(np.float32),
        np.cos(edge).astype(np.float32),
        np.sin(edge).astype(np.float32),
    )


def mirror_table():
    table = np.zeros((HALF, HALF), np.float32)
    table[0, 0] = 1.0
    table[np.arange(1, HALF), HALF - np.arange(1, HALF)] = 1.0
    return table


def split_parts(value):
    high = value.astype(jnp.bfloat16)
    low = (value - high.astype(jnp.float32)).astype(jnp.bfloat16)
    return high, low


def dot_nn(lhs, rhs):
    return lax.dot_general(lhs, rhs, (((1,), (0,)), ((), ())), preferred_element_type=jnp.float32)


def dot_nt(lhs, rhs):
    return lax.dot_general(lhs, rhs, (((1,), (1,)), ((), ())), preferred_element_type=jnp.float32)


def first_kernel(x_ref, high_ref, low_ref, out_ref):
    parts = x_ref.shape[0]
    pair = x_ref.shape[1]
    columns = []
    for s in range(pair):
        columns.append(jnp.concatenate([x_ref[f, s] for f in range(parts)], axis=0))
    value = jnp.concatenate(columns, axis=1)
    high, low = split_parts(value)
    result = dot_nn(high_ref[...], high) + dot_nn(high_ref[...], low) + dot_nn(low_ref[...], high)
    width = x_ref.shape[3]
    for s in range(pair):
        out_ref[s] = result[:, s * width : (s + 1) * width]


def first_section(received, tables):
    parts, segs, rows, width = received.shape
    pair = 2
    return pl.pallas_call(
        first_kernel,
        grid=(segs // pair,),
        in_specs=[
            pl.BlockSpec((parts, pair, rows, width), lambda i: (0, i, 0, 0)),
            pl.BlockSpec((A, A), lambda i: (0, 0)),
            pl.BlockSpec((A, A), lambda i: (0, 0)),
        ],
        out_specs=pl.BlockSpec((pair, A, width), lambda i: (i, 0, 0)),
        out_shape=jax.ShapeDtypeStruct((segs, A, width), jnp.float32),
        compiler_params=pltpu.CompilerParams(vmem_limit_bytes=40 * 2**20),
        cost_estimate=pl.CostEstimate(
            flops=2 * 3 * segs * A * A * width, bytes_accessed=segs * A * width * 8, transcendentals=0
        ),
        name="first_section",
    )(received, *tables)


def second_kernel(
    y_ref, tc_ref, ts_ref, ec_ref, es_ref, ch_ref, cl_ref, sh_ref, sl_ref, wa_ref, wm_ref, q_ref, out_ref
):
    parts = y_ref.shape[0]
    joined = jnp.concatenate([y_ref[f, 0] for f in range(parts)], axis=1)
    real_raw = joined[:HALF]
    imag_raw = joined[HALF:]
    row_ids = lax.broadcasted_iota(jnp.int32, (HALF, B), 0)
    imag_in = jnp.where(row_ids == 0, 0.0, imag_raw)
    twist_cos = tc_ref[...]
    twist_sin = ts_ref[...]
    real_u = real_raw * twist_cos + imag_in * twist_sin
    imag_u = imag_in * twist_cos - real_raw * twist_sin
    edge = imag_raw[0:1]
    edge_rows = jnp.where(
        lax.broadcasted_iota(jnp.int32, (16, B), 0) == 0,
        edge * ec_ref[...],
        jnp.where(lax.broadcasted_iota(jnp.int32, (16, B), 0) == 1, -edge * es_ref[...], 0.0),
    )
    u_high, u_low = split_parts(jnp.concatenate([real_u, imag_u], axis=0))
    e_high, e_low = split_parts(edge_rows)

    def three(high_ref, low_ref, high, low):
        return (
            dot_nt(high_ref[...], high) + dot_nt(high_ref[...], low) + dot_nt(low_ref[...], high)
        )

    by_cos = three(ch_ref, cl_ref, u_high, u_low)
    by_sin = three(sh_ref, sl_ref, u_high, u_low)
    edge_cos = three(ch_ref, cl_ref, e_high, e_low)[:NB]
    edge_sin = three(sh_ref, sl_ref, e_high, e_low)[:NB]
    white = wa_ref[...]
    real_out = ((by_cos[:NB, :HALF] + by_sin[:NB, HALF:]) * white).astype(jnp.bfloat16)
    imag_out = ((by_cos[:NB, HALF:] - by_sin[:NB, :HALF]) * white).astype(jnp.bfloat16)
    next_cos = by_cos[1 : NB + 1]
    next_sin = by_sin[1 : NB + 1]
    lane = lax.broadcasted_iota(jnp.int32, (NB, HALF), 1)
    real_edge = edge_cos[:, 0:1] + edge_sin[:, 1:2]
    imag_edge = edge_cos[:, 1:2] - edge_sin[:, 0:1]
    real_far = jnp.where(lane == 0, real_edge, next_cos[:, :HALF] - next_sin[:, HALF:])
    imag_far = jnp.where(lane == 0, imag_edge, -next_cos[:, HALF:] - next_sin[:, :HALF])
    white_far = wm_ref[...]
    order = q_ref[...]
    real_far = dot_nn((real_far * white_far).astype(jnp.bfloat16), order).astype(jnp.bfloat16)
    imag_far = dot_nn((imag_far * white_far).astype(jnp.bfloat16), order).astype(jnp.bfloat16)
    rows = NB // parts
    for f in range(parts):
        here = slice(f * rows, (f + 1) * rows)
        out_ref[f, 0, 0, :, :HALF] = real_out[here]
        out_ref[f, 0, 0, :, HALF:] = real_far[here]
        out_ref[f, 0, 1, :, :HALF] = imag_out[here]
        out_ref[f, 0, 1, :, HALF:] = imag_far[here]


def second_section(received, tables, white, white_far):
    parts, segs, rows, width = received.shape
    twists, seconds, order = tables

    def whole(array):
        return pl.BlockSpec(array.shape, lambda i: (0,) * array.ndim)

    fixed = (*twists, *seconds, white, white_far, order)
    return pl.pallas_call(
        second_kernel,
        grid=(segs,),
        in_specs=[pl.BlockSpec((parts, 1, rows, width), lambda i: (0, i, 0, 0))]
        + [whole(array) for array in fixed],
        out_specs=pl.BlockSpec((parts, 1, 2, NB // parts, A), lambda i: (0, i, 0, 0, 0)),
        out_shape=jax.ShapeDtypeStruct((parts, segs, 2, NB // parts, A), jnp.bfloat16),
        compiler_params=pltpu.CompilerParams(vmem_limit_bytes=60 * 2**20),
        cost_estimate=pl.CostEstimate(
            flops=2 * 6 * segs * 528 * B * A, bytes_accessed=segs * A * B * 6, transcendentals=0
        ),
        name="second_section",
    )(received, *fixed)


def lag_kernel(place_ref, a_ref, b_ref, x_ref, y_ref, t_ref, c_ref, s_ref, out_ref, acc_ref, even_ref, odd_ref):
    sources = (a_ref, b_ref, x_ref, y_ref)
    segs = a_ref.shape[1] // 2
    per_quad = t_ref.shape[0]
    lag_total = c_ref.shape[1]
    tmpl = out_ref.shape[2]
    step = pl.program_id(0)
    last = pl.num_programs(0) - 1
    half = len(sources) * segs * lag_total

    def make_rows(rows_ref, jj):
        for chunk in range(A // 128):
            lanes = slice(chunk * 128, (chunk + 1) * 128)
            lag_cos = c_ref[jj, :, lanes]
            lag_sin = s_ref[jj, :, lanes]
            for index, source in enumerate(sources):
                value = source[jj, :, lanes].astype(jnp.float32)
                for s in range(segs):
                    real = value[s : s + 1]
                    imag = value[segs + s : segs + s + 1]
                    first_row = (index * segs + s) * lag_total
                    rows = slice(first_row, first_row + lag_total)
                    rows_ref[jj, rows, lanes] = (real * lag_cos - imag * lag_sin).astype(jnp.bfloat16)
                    rows = slice(half + first_row, half + first_row + lag_total)
                    rows_ref[jj, rows, lanes] = (real * lag_sin + imag * lag_cos).astype(jnp.bfloat16)

    def multiply(now_ref, jj):
        acc_ref[...] += dot_nt(now_ref[jj], t_ref[jj])

    @pl.when(step == 0)
    def _():
        acc_ref[...] = jnp.zeros_like(acc_ref)

        @pl.loop(0, per_quad)
        def _(jj):
            make_rows(even_ref, jj)

    @pl.when((step % 2 == 1) & (step < last))
    def _():
        @pl.loop(0, per_quad)
        def _(jj):
            make_rows(odd_ref, jj)
            multiply(even_ref, jj)

    @pl.when((step % 2 == 0) & (step > 0) & (step < last))
    def _():
        @pl.loop(0, per_quad)
        def _(jj):
            make_rows(even_ref, jj)
            multiply(odd_ref, jj)

    @pl.when(step == last)
    def _():
        @pl.loop(0, per_quad)
        def _(jj):
            multiply(odd_ref, jj)

        shape = (segs, lag_total, tmpl)
        for index in range(len(sources)):
            low = slice(index * segs * lag_total, (index + 1) * segs * lag_total)
            high = slice(half + low.start, half + low.stop)
            place = pl.ds((place_ref[0] ^ index) * segs, segs)
            out_ref[place, :lag_total] = (acc_ref[low, :tmpl] + acc_ref[high, tmpl:]).reshape(shape)
            out_ref[place, lag_total:] = (acc_ref[high, :tmpl] - acc_ref[low, tmpl:]).reshape(shape)


def lag_products(sources, place, laid, lag_cos, lag_sin):
    blocks, rows, _ = sources[0].shape
    tmpl2 = laid.shape[1]
    per_quad = min(4, blocks)
    quads = blocks // per_quad
    lag_total = lag_cos.shape[1]
    segs = len(sources) * rows // 2

    def ahead(i):
        return (jnp.minimum(i, quads - 1), 0, 0)

    return pl.pallas_call(
        lag_kernel,
        grid=(quads + 1,),
        in_specs=[pl.BlockSpec(memory_space=pltpu.SMEM)]
        + [pl.BlockSpec((per_quad, rows, A), ahead)] * len(sources)
        + [
            pl.BlockSpec((per_quad, tmpl2, A), lambda i: (jnp.maximum(i - 1, 0), 0, 0)),
            pl.BlockSpec((per_quad, lag_total, A), ahead),
            pl.BlockSpec((per_quad, lag_total, A), ahead),
        ],
        out_specs=pl.BlockSpec((segs, 2 * lag_total, tmpl2 // 2), lambda i: (0, 0, 0)),
        out_shape=jax.ShapeDtypeStruct((segs, 2 * lag_total, tmpl2 // 2), jnp.float32),
        scratch_shapes=[
            pltpu.VMEM((2 * segs * lag_total, tmpl2), jnp.float32),
            pltpu.VMEM((per_quad, 2 * segs * lag_total, A), jnp.bfloat16),
            pltpu.VMEM((per_quad, 2 * segs * lag_total, A), jnp.bfloat16),
        ],
        compiler_params=pltpu.CompilerParams(vmem_limit_bytes=60 * 2**20),
        cost_estimate=pl.CostEstimate(
            flops=4 * segs * lag_total * tmpl2 * blocks * A,
            bytes_accessed=blocks * A * (tmpl2 * 2 + segs * 4),
            transcendentals=0,
        ),
        name="lag_products",
    )(place, *sources, laid, lag_cos, lag_sin)


def block_rows(data):
    segs, parts, blocks, _ = data.shape
    return data.transpose(2, 1, 0, 3).reshape(blocks, parts * segs, A)


def spread(data):
    moved = [lax.ppermute(data, "tmpl", [(n, n ^ bit) for n in range(4)]) for bit in (1, 2, 3)]
    return (data, *moved)


def layout_kernel(cut_ref, t_ref, *refs):
    out_ref = refs[-1]
    tmpl, _, rows, _ = t_ref.shape
    first_row = pl.program_id(0) * rows + cut_ref[cut_ref.shape[0] - 1]
    first_tmpl = pl.program_id(1) * tmpl
    row_ids = lax.broadcasted_iota(jnp.int32, (rows, 128), 0) + first_row
    batch = 16

    @pl.loop(0, tmpl // batch)
    def _(group):
        some = pl.ds(pl.multiple_of(group * batch, batch), batch)
        keeps = [row_ids < cut_ref[first_tmpl + group * batch + n] for n in range(batch)]
        for part in range(2):
            for chunk in range(A // 128):
                lanes = slice(chunk * 128, (chunk + 1) * 128)
                value = t_ref[some, part, :, lanes].astype(jnp.float32)
                value = jnp.stack([jnp.where(keeps[n], value[n], 0.0) for n in range(batch)], axis=0)
                value = jnp.swapaxes(value, 0, 1).astype(jnp.bfloat16)
                for row in range(rows):
                    out_ref[row, part, some, lanes] = value[row]


def lay_out(templates, cuts, piece, pieces, laid):
    tmpl, _, blocks, _ = templates.shape
    rows = min(16, blocks)
    steps = blocks // rows // pieces
    batch = min(64, tmpl)
    shape = (blocks, 2, tmpl, A)
    first = piece * steps
    info = jnp.concatenate([cuts, jnp.full((1,), first * rows, jnp.int32)])
    earlier = () if laid is None else (laid,)
    return pl.pallas_call(
        layout_kernel,
        grid=(steps, tmpl // batch),
        in_specs=[
            pl.BlockSpec(memory_space=pltpu.SMEM),
            pl.BlockSpec((batch, 2, rows, A), lambda i, j: (j, 0, i + first, 0)),
        ]
        + [pl.BlockSpec(memory_space=pl.ANY)] * len(earlier),
        out_specs=pl.BlockSpec((rows, 2, batch, A), lambda i, j: (i + first, 0, j, 0)),
        out_shape=jax.ShapeDtypeStruct(shape, jnp.bfloat16),
        input_output_aliases={2: 0} if earlier else {},
        compiler_params=pltpu.CompilerParams(vmem_limit_bytes=40 * 2**20),
        cost_estimate=pl.CostEstimate(
            flops=0, bytes_accessed=8 * tmpl * 2 * blocks * A // pieces, transcendentals=0
        ),
        name="lay_out",
    )(info, templates, *earlier)


def general_transform(strain, psd):
    freq_count = lax.axis_size("freq")
    freq_index = lax.axis_index("freq")
    seg_local = strain.shape[0]
    step_time = B // freq_count
    highest = lax.Precision.HIGHEST
    first_cos, first_sin = cos_sin_table(
        jnp.arange(A, dtype=jnp.int32), jnp.arange(A, dtype=jnp.int32), A
    )
    table = jnp.concatenate([first_cos, -first_sin], axis=0)
    time_ids = freq_index * step_time + jnp.arange(step_time, dtype=jnp.int32)
    twist_cos, twist_sin = cos_sin_table(jnp.arange(A, dtype=jnp.int32), time_ids, LEN)
    slab_blocks = strain.reshape(seg_local, A // freq_count, B)
    both_parts = jnp.einsum(
        "kn,snb->skb",
        table,
        lax.all_to_all(slab_blocks, "freq", split_axis=2, concat_axis=1, tiled=True),
        precision=highest,
    )
    real_part = both_parts[:, :A]
    imag_part = both_parts[:, A:]
    second_cos, second_sin = cos_sin_table(
        jnp.arange(B, dtype=jnp.int32), jnp.arange(NB, dtype=jnp.int32), B
    )
    rotation = jnp.concatenate(
        [
            jnp.concatenate([second_cos, -second_sin], axis=1),
            jnp.concatenate([second_sin, second_cos], axis=1),
        ],
        axis=0,
    )
    amplitude = jnp.sqrt(LEN * psd)
    real_in = lax.all_to_all(
        real_part * twist_cos + imag_part * twist_sin, "freq", split_axis=1, concat_axis=2, tiled=True
    )
    imag_in = lax.all_to_all(
        imag_part * twist_cos - real_part * twist_sin, "freq", split_axis=1, concat_axis=2, tiled=True
    )
    joined = jnp.concatenate([real_in, imag_in], axis=2)
    both_out = jnp.einsum("spc,cm->smp", joined, rotation, precision=highest)
    both_out = both_out.reshape(joined.shape[0], 2, NB, joined.shape[1])
    whitened = (both_out / amplitude).astype(jnp.bfloat16)
    return lax.all_to_all(whitened, "freq", split_axis=2, concat_axis=3, tiled=True)


def exchange(sent):
    return lax.all_to_all(sent, "freq", split_axis=0, concat_axis=0, tiled=True)


def pack_strain(strain, freq_count):
    seg_local = strain.shape[0]
    sent = (strain * STRAIN_SCALE).astype(jnp.float16)
    sent = sent.reshape(seg_local, A // freq_count, freq_count, B // freq_count)
    return sent.transpose(2, 0, 1, 3)


def pack_coefs(received, table):
    freq_count, seg_local, _, width = received.shape
    coefs = first_section(received.astype(jnp.float32) * (1.0 / STRAIN_SCALE), table)
    sent = (coefs * COEF_SCALE).astype(jnp.float16)
    return sent.reshape(freq_count, seg_local // freq_count, A, width)


def whiten(received, tables, white, white_far):
    return second_section(received.astype(jnp.float32) * (1.0 / COEF_SCALE), tables, white, white_far)


def on_device(strain, psd, templates, cutoffs, lags):
    freq_count = lax.axis_size("freq")
    freq_index = lax.axis_index("freq")
    seg_local = strain.shape[0]
    tmpl_local = templates.shape[0]
    blocks_here = templates.shape[2]
    first_block = freq_index * blocks_here
    block_ids = first_block + jnp.arange(blocks_here, dtype=jnp.int32)
    cuts = cutoffs - first_block
    tied = lax.optimization_barrier

    block_cos, block_sin = cos_sin_table(block_ids, lags % B, B)
    place = lags[:, None] * jnp.arange(A, dtype=jnp.int32)[None, :] % LEN
    place_angle = place.astype(jnp.float32) * (two_pi / LEN)
    place_cos = jnp.cos(place_angle)[None]
    place_sin = jnp.sin(place_angle)[None]
    block_cos = block_cos[:, :, None]
    block_sin = block_sin[:, :, None]
    lag_cos = block_cos * place_cos - block_sin * place_sin
    lag_sin = block_sin * place_cos + block_cos * place_sin

    sliced = (
        lax.axis_size("tmpl") == 4
        and seg_local == 2 * freq_count == 16
        and (NB // freq_count) % 32 == 0
        and B // freq_count == 128
    )
    if not sliced:
        laid = lay_out(templates, cuts, 0, 1, None)
        laid = laid.reshape(blocks_here, 2 * tmpl_local, A)
        data = lax.all_gather(general_transform(strain, psd), "tmpl", axis=0, tiled=True)
        origin = jnp.zeros((1,), jnp.int32)
        sums = []
        for start in range(0, data.shape[0], 16):
            sources = [block_rows(data[n : n + 4]) for n in range(start, start + 16, 4)]
            sums.append(lag_products(sources, origin, laid, lag_cos, lag_sin))
        sums = jnp.concatenate(sums, axis=0)
        return lax.psum_scatter(sums, "freq", scatter_dimension=0, tiled=True)

    order = mirror_table()
    psd_all = lax.all_gather(psd, "freq", axis=1, tiled=True)
    psd_far = jnp.dot(psd_all[:, HALF:], order.T, precision=lax.Precision.HIGHEST)
    white = lax.rsqrt(LEN * psd_all[:, :HALF])
    white_far = lax.rsqrt(LEN * psd_far)
    first = first_table()
    second = (twist_tables(), second_tables(), order.astype(ml_dtypes.bfloat16))

    seg_out = seg_local * lax.axis_size("tmpl") // freq_count
    by_owner = strain.reshape(seg_local // seg_out, 2, seg_out // 2, strain.shape[1])
    strain_a, strain_b = (
        pack_strain(by_owner[:, group].reshape(seg_local // 2, strain.shape[1]), freq_count)
        for group in range(2)
    )
    time_a = exchange(strain_a)
    laid = lay_out(templates, cuts, 0, 2, None)
    time_a, laid = tied((time_a, laid))
    coefs_a = pack_coefs(time_a, first)
    parts_a = exchange(coefs_a)
    laid = lay_out(templates, cuts, 1, 2, laid)
    parts_a, strain_b, laid, white, white_far, lag_cos, lag_sin = tied(
        (parts_a, strain_b, laid, white, white_far, lag_cos, lag_sin)
    )
    time_b = exchange(strain_b)
    white_a = whiten(parts_a, second, white, white_far)
    time_b, white_a = tied((time_b, white_a))
    data_a = exchange(white_a)
    coefs_b = pack_coefs(time_b, first)
    data_a, coefs_b = tied((data_a, coefs_b))
    parts_b = exchange(coefs_b)
    laid = laid.reshape(blocks_here, 2 * tmpl_local, A)
    place = lax.axis_index("tmpl").astype(jnp.int32).reshape(1)

    def halves(data):
        data = data.reshape(2, 2, 2, 2, blocks_here, A)
        return [block_rows(data[:, n].reshape(4, 2, blocks_here, A)) for n in range(2)]

    def products(part):
        return lag_products(part, place, laid, lag_cos, lag_sin)

    def collect(sums):
        return lax.psum_scatter(sums, "freq", scatter_dimension=0, tiled=True)

    def collect_late(sums):
        shares = exchange(sums.reshape(freq_count, 2, 2 * lags.shape[0], tmpl_local))
        return jnp.sum(shares, axis=0)

    first_a, second_a = halves(data_a)
    first_a = spread(first_a)
    parts_b, first_a, second_a = tied((parts_b, first_a, second_a))
    second_a = spread(second_a)
    data_b = exchange(whiten(parts_b, second, white, white_far))
    sums_a1 = products(first_a)
    data_b, second_a, sums_a1 = tied((data_b, second_a, sums_a1))
    first_b, second_b = halves(data_b)
    first_b = spread(first_b)
    out_a1 = collect(sums_a1)
    sums_a2 = products(second_a)
    first_b, second_b, sums_a2 = tied((first_b, second_b, sums_a2))
    second_b = spread(second_b)
    out_a2 = collect(sums_a2)
    sums_b1 = products(first_b)
    second_b, sums_b1 = tied((second_b, sums_b1))
    out_b1 = collect_late(sums_b1)
    out_b2 = collect_late(products(second_b))
    return jnp.concatenate([out_a1, out_a2, out_b1, out_b2], axis=0)


def solution(mesh):
    placed = (P("tmpl", "freq"), P(None, "freq"), P("tmpl", None, "freq", None), P("tmpl"), P())
    return jax.shard_map(
        on_device, mesh=mesh, in_specs=placed, out_specs=P("freq", None, "tmpl"), check_vma=False
    )
```

```python
import math

import jax
import jax.numpy as jnp
import ml_dtypes
import numpy as np
from jax import lax
from jax.experimental import pallas as pl
from jax.experimental.pallas import tpu as pltpu
from jax.sharding import PartitionSpec as P

A = 512
B = 1024
LEN = 524288
NB = 512
HALF = A // 2

STRAIN_SCALE = 8192.0
COEF_SCALE = 16.0

two_pi = 2.0 * math.pi


def cos_sin_table(row_ids, col_ids, modulus):
    product = row_ids[:, None] * col_ids[None, :] % modulus
    phase_angle = product.astype(jnp.float32) * (two_pi / modulus)
    return (jnp.cos(phase_angle), jnp.sin(phase_angle))


def split_const(table):
    high = table.astype(ml_dtypes.bfloat16)
    low = (table - high.astype(np.float64)).astype(ml_dtypes.bfloat16)
    return high, low


def first_table():
    angle = two_pi * (np.outer(np.arange(HALF), np.arange(A)) % A) / A
    table = np.concatenate([np.cos(angle), -np.sin(angle)], axis=0)
    table[HALF] = 1.0 - 2.0 * (np.arange(A) % 2)
    return split_const(table)


def second_tables():
    angle = two_pi * (np.outer(np.arange(528), np.arange(B)) % B) / B
    return split_const(np.cos(angle)) + split_const(np.sin(angle))


def twist_tables():
    angle = two_pi * np.outer(np.arange(HALF), np.arange(B)) / LEN
    edge = two_pi * HALF * np.arange(B)[None, :] / LEN
    return (
        np.cos(angle).astype(np.float32),
        np.sin(angle).astype(np.float32),
        np.cos(edge).astype(np.float32),
        np.sin(edge).astype(np.float32),
    )


def mirror_table():
    table = np.zeros((HALF, HALF), np.float32)
    table[0, 0] = 1.0
    table[np.arange(1, HALF), HALF - np.arange(1, HALF)] = 1.0
    return table


def split_parts(value):
    high = value.astype(jnp.bfloat16)
    low = (value - high.astype(jnp.float32)).astype(jnp.bfloat16)
    return high, low


def dot_nn(lhs, rhs):
    return lax.dot_general(lhs, rhs, (((1,), (0,)), ((), ())), preferred_element_type=jnp.float32)


def dot_nt(lhs, rhs):
    return lax.dot_general(lhs, rhs, (((1,), (1,)), ((), ())), preferred_element_type=jnp.float32)


def first_kernel(x_ref, high_ref, low_ref, out_ref):
    parts = x_ref.shape[0]
    pair = x_ref.shape[1]
    columns = []
    for s in range(pair):
        columns.append(jnp.concatenate([x_ref[f, s] for f in range(parts)], axis=0))
    value = jnp.concatenate(columns, axis=1)
    high, low = split_parts(value)
    result = dot_nn(high_ref[...], high) + dot_nn(high_ref[...], low) + dot_nn(low_ref[...], high)
    width = x_ref.shape[3]
    for s in range(pair):
        out_ref[s] = result[:, s * width : (s + 1) * width]


def first_section(received, tables):
    parts, segs, rows, width = received.shape
    pair = 2
    return pl.pallas_call(
        first_kernel,
        grid=(segs // pair,),
        in_specs=[
            pl.BlockSpec((parts, pair, rows, width), lambda i: (0, i, 0, 0)),
            pl.BlockSpec((A, A), lambda i: (0, 0)),
            pl.BlockSpec((A, A), lambda i: (0, 0)),
        ],
        out_specs=pl.BlockSpec((pair, A, width), lambda i: (i, 0, 0)),
        out_shape=jax.ShapeDtypeStruct((segs, A, width), jnp.float32),
        compiler_params=pltpu.CompilerParams(vmem_limit_bytes=40 * 2**20),
        cost_estimate=pl.CostEstimate(
            flops=2 * 3 * segs * A * A * width, bytes_accessed=segs * A * width * 8, transcendentals=0
        ),
        name="first_section",
    )(received, *tables)


def second_kernel(
    y_ref, tc_ref, ts_ref, ec_ref, es_ref, ch_ref, cl_ref, sh_ref, sl_ref, wa_ref, wm_ref, q_ref, out_ref
):
    parts = y_ref.shape[0]
    joined = jnp.concatenate([y_ref[f, 0] for f in range(parts)], axis=1)
    real_raw = joined[:HALF]
    imag_raw = joined[HALF:]
    row_ids = lax.broadcasted_iota(jnp.int32, (HALF, B), 0)
    imag_in = jnp.where(row_ids == 0, 0.0, imag_raw)
    twist_cos = tc_ref[...]
    twist_sin = ts_ref[...]
    real_u = real_raw * twist_cos + imag_in * twist_sin
    imag_u = imag_in * twist_cos - real_raw * twist_sin
    edge = imag_raw[0:1]
    edge_rows = jnp.where(
        lax.broadcasted_iota(jnp.int32, (16, B), 0) == 0,
        edge * ec_ref[...],
        jnp.where(lax.broadcasted_iota(jnp.int32, (16, B), 0) == 1, -edge * es_ref[...], 0.0),
    )
    u_high, u_low = split_parts(jnp.concatenate([real_u, imag_u], axis=0))
    e_high, e_low = split_parts(edge_rows)

    def three(high_ref, low_ref, high, low):
        return (
            dot_nt(high_ref[...], high) + dot_nt(high_ref[...], low) + dot_nt(low_ref[...], high)
        )

    by_cos = three(ch_ref, cl_ref, u_high, u_low)
    by_sin = three(sh_ref, sl_ref, u_high, u_low)
    edge_cos = three(ch_ref, cl_ref, e_high, e_low)[:NB]
    edge_sin = three(sh_ref, sl_ref, e_high, e_low)[:NB]
    white = wa_ref[...]
    real_out = ((by_cos[:NB, :HALF] + by_sin[:NB, HALF:]) * white).astype(jnp.bfloat16)
    imag_out = ((by_cos[:NB, HALF:] - by_sin[:NB, :HALF]) * white).astype(jnp.bfloat16)
    next_cos = by_cos[1 : NB + 1]
    next_sin = by_sin[1 : NB + 1]
    lane = lax.broadcasted_iota(jnp.int32, (NB, HALF), 1)
    real_edge = edge_cos[:, 0:1] + edge_sin[:, 1:2]
    imag_edge = edge_cos[:, 1:2] - edge_sin[:, 0:1]
    real_far = jnp.where(lane == 0, real_edge, next_cos[:, :HALF] - next_sin[:, HALF:])
    imag_far = jnp.where(lane == 0, imag_edge, -next_cos[:, HALF:] - next_sin[:, :HALF])
    white_far = wm_ref[...]
    order = q_ref[...]
    real_far = dot_nn((real_far * white_far).astype(jnp.bfloat16), order).astype(jnp.bfloat16)
    imag_far = dot_nn((imag_far * white_far).astype(jnp.bfloat16), order).astype(jnp.bfloat16)
    rows = NB // parts
    for f in range(parts):
        here = slice(f * rows, (f + 1) * rows)
        out_ref[f, 0, 0, :, :HALF] = real_out[here]
        out_ref[f, 0, 0, :, HALF:] = real_far[here]
        out_ref[f, 0, 1, :, :HALF] = imag_out[here]
        out_ref[f, 0, 1, :, HALF:] = imag_far[here]


def second_section(received, tables, white, white_far):
    parts, segs, rows, width = received.shape
    twists, seconds, order = tables

    def whole(array):
        return pl.BlockSpec(array.shape, lambda i: (0,) * array.ndim)

    fixed = (*twists, *seconds, white, white_far, order)
    return pl.pallas_call(
        second_kernel,
        grid=(segs,),
        in_specs=[pl.BlockSpec((parts, 1, rows, width), lambda i: (0, i, 0, 0))]
        + [whole(array) for array in fixed],
        out_specs=pl.BlockSpec((parts, 1, 2, NB // parts, A), lambda i: (0, i, 0, 0, 0)),
        out_shape=jax.ShapeDtypeStruct((parts, segs, 2, NB // parts, A), jnp.bfloat16),
        compiler_params=pltpu.CompilerParams(vmem_limit_bytes=60 * 2**20),
        cost_estimate=pl.CostEstimate(
            flops=2 * 6 * segs * 528 * B * A, bytes_accessed=segs * A * B * 6, transcendentals=0
        ),
        name="second_section",
    )(received, *fixed)


def lag_kernel(place_ref, a_ref, b_ref, x_ref, y_ref, t_ref, c_ref, s_ref, out_ref, acc_ref, even_ref, odd_ref):
    sources = (a_ref, b_ref, x_ref, y_ref)
    segs = a_ref.shape[1] // 2
    per_quad = t_ref.shape[0]
    lag_total = c_ref.shape[2]
    tmpl = out_ref.shape[2]
    step = pl.program_id(0)
    last = pl.num_programs(0) - 1
    seg_total = len(sources) * segs
    half = seg_total * lag_total

    def make_rows(rows_ref, jj):
        for chunk in range(A // 128):
            lanes = slice(chunk * 128, (chunk + 1) * 128)
            values = [source[jj, :, lanes].astype(jnp.float32) for source in sources]
            real = jnp.concatenate([value[:segs] for value in values], axis=0)
            imag = jnp.concatenate([value[segs:] for value in values], axis=0)
            for lag in range(lag_total):
                repeated = pl.ds(lag, 8, stride=0)
                lag_cos = jnp.concatenate([c_ref[jj, chunk, repeated]] * (seg_total // 8), axis=0)
                lag_sin = jnp.concatenate([s_ref[jj, chunk, repeated]] * (seg_total // 8), axis=0)
                rows = slice(lag * seg_total, (lag + 1) * seg_total)
                rows_ref[jj, rows, lanes] = (real * lag_cos - imag * lag_sin).astype(jnp.bfloat16)
                rows = slice(half + lag * seg_total, half + (lag + 1) * seg_total)
                rows_ref[jj, rows, lanes] = (real * lag_sin + imag * lag_cos).astype(jnp.bfloat16)

    def multiply(now_ref, jj):
        acc_ref[...] += dot_nt(now_ref[jj], t_ref[jj])

    @pl.when(step == 0)
    def _():
        acc_ref[...] = jnp.zeros_like(acc_ref)

        @pl.loop(0, per_quad)
        def _(jj):
            make_rows(even_ref, jj)

    @pl.when((step % 2 == 1) & (step < last))
    def _():
        @pl.loop(0, per_quad)
        def _(jj):
            make_rows(odd_ref, jj)
            multiply(even_ref, jj)

    @pl.when((step % 2 == 0) & (step > 0) & (step < last))
    def _():
        @pl.loop(0, per_quad)
        def _(jj):
            make_rows(even_ref, jj)
            multiply(odd_ref, jj)

    @pl.when(step == last)
    def _():
        @pl.loop(0, per_quad)
        def _(jj):
            multiply(odd_ref, jj)

        shape = (lag_total, seg_total, tmpl)
        real = acc_ref[:half, :tmpl] + acc_ref[half:, tmpl:]
        imag = acc_ref[half:, :tmpl] - acc_ref[:half, tmpl:]
        real = jnp.swapaxes(real.reshape(shape), 0, 1)
        imag = jnp.swapaxes(imag.reshape(shape), 0, 1)
        for index in range(len(sources)):
            here = slice(index * segs, (index + 1) * segs)
            place = pl.ds((place_ref[0] ^ index) * segs, segs)
            out_ref[place, :lag_total] = real[here]
            out_ref[place, lag_total:] = imag[here]


def lag_products(sources, place, laid, lag_cos, lag_sin):
    blocks, rows, _ = sources[0].shape
    tmpl2 = laid.shape[1]
    per_quad = min(4, blocks)
    quads = blocks // per_quad
    _, chunks, lag_total, lanes = lag_cos.shape
    segs = len(sources) * rows // 2

    def ahead(i):
        return (jnp.minimum(i, quads - 1), 0, 0)

    def ahead_lags(i):
        return (jnp.minimum(i, quads - 1), 0, 0, 0)

    return pl.pallas_call(
        lag_kernel,
        grid=(quads + 1,),
        in_specs=[pl.BlockSpec(memory_space=pltpu.SMEM)]
        + [pl.BlockSpec((per_quad, rows, A), ahead)] * len(sources)
        + [
            pl.BlockSpec((per_quad, tmpl2, A), lambda i: (jnp.maximum(i - 1, 0), 0, 0)),
            pl.BlockSpec((per_quad, chunks, lag_total, lanes), ahead_lags),
            pl.BlockSpec((per_quad, chunks, lag_total, lanes), ahead_lags),
        ],
        out_specs=pl.BlockSpec((segs, 2 * lag_total, tmpl2 // 2), lambda i: (0, 0, 0)),
        out_shape=jax.ShapeDtypeStruct((segs, 2 * lag_total, tmpl2 // 2), jnp.float32),
        scratch_shapes=[
            pltpu.VMEM((2 * segs * lag_total, tmpl2), jnp.float32),
            pltpu.VMEM((per_quad, 2 * segs * lag_total, A), jnp.bfloat16),
            pltpu.VMEM((per_quad, 2 * segs * lag_total, A), jnp.bfloat16),
        ],
        compiler_params=pltpu.CompilerParams(vmem_limit_bytes=60 * 2**20),
        cost_estimate=pl.CostEstimate(
            flops=4 * segs * lag_total * tmpl2 * blocks * A,
            bytes_accessed=blocks * A * (tmpl2 * 2 + segs * 4),
            transcendentals=0,
        ),
        name="lag_products",
    )(place, *sources, laid, lag_cos, lag_sin)


def block_rows(data):
    segs, parts, blocks, _ = data.shape
    return data.transpose(2, 1, 0, 3).reshape(blocks, parts * segs, A)


def spread(data):
    moved = [lax.ppermute(data, "tmpl", [(n, n ^ bit) for n in range(4)]) for bit in (1, 2, 3)]
    return (data, *moved)


def layout_kernel(cut_ref, t_ref, *refs):
    out_ref = refs[-1]
    tmpl, _, rows, _ = t_ref.shape
    first_row = pl.program_id(0) * rows + cut_ref[cut_ref.shape[0] - 1]
    first_tmpl = pl.program_id(1) * tmpl
    row_ids = lax.broadcasted_iota(jnp.int32, (rows, 128), 0) + first_row
    batch = 16

    @pl.loop(0, tmpl // batch)
    def _(group):
        some = pl.ds(pl.multiple_of(group * batch, batch), batch)
        keeps = [row_ids < cut_ref[first_tmpl + group * batch + n] for n in range(batch)]
        for part in range(2):
            for chunk in range(A // 128):
                lanes = slice(chunk * 128, (chunk + 1) * 128)
                value = t_ref[some, part, :, lanes].astype(jnp.float32)
                value = jnp.stack([jnp.where(keeps[n], value[n], 0.0) for n in range(batch)], axis=0)
                value = jnp.swapaxes(value, 0, 1).astype(jnp.bfloat16)
                for row in range(rows):
                    out_ref[row, part, some, lanes] = value[row]


def lay_out(templates, cuts, piece, pieces, laid):
    tmpl, _, blocks, _ = templates.shape
    rows = min(16, blocks)
    steps = blocks // rows // pieces
    batch = min(64, tmpl)
    shape = (blocks, 2, tmpl, A)
    first = piece * steps
    info = jnp.concatenate([cuts, jnp.full((1,), first * rows, jnp.int32)])
    earlier = () if laid is None else (laid,)
    return pl.pallas_call(
        layout_kernel,
        grid=(steps, tmpl // batch),
        in_specs=[
            pl.BlockSpec(memory_space=pltpu.SMEM),
            pl.BlockSpec((batch, 2, rows, A), lambda i, j: (j, 0, i + first, 0)),
        ]
        + [pl.BlockSpec(memory_space=pl.ANY)] * len(earlier),
        out_specs=pl.BlockSpec((rows, 2, batch, A), lambda i, j: (i + first, 0, j, 0)),
        out_shape=jax.ShapeDtypeStruct(shape, jnp.bfloat16),
        input_output_aliases={2: 0} if earlier else {},
        compiler_params=pltpu.CompilerParams(vmem_limit_bytes=40 * 2**20),
        cost_estimate=pl.CostEstimate(
            flops=0, bytes_accessed=8 * tmpl * 2 * blocks * A // pieces, transcendentals=0
        ),
        name="lay_out",
    )(info, templates, *earlier)


def general_transform(strain, psd):
    freq_count = lax.axis_size("freq")
    freq_index = lax.axis_index("freq")
    seg_local = strain.shape[0]
    step_time = B // freq_count
    highest = lax.Precision.HIGHEST
    first_cos, first_sin = cos_sin_table(
        jnp.arange(A, dtype=jnp.int32), jnp.arange(A, dtype=jnp.int32), A
    )
    table = jnp.concatenate([first_cos, -first_sin], axis=0)
    time_ids = freq_index * step_time + jnp.arange(step_time, dtype=jnp.int32)
    twist_cos, twist_sin = cos_sin_table(jnp.arange(A, dtype=jnp.int32), time_ids, LEN)
    slab_blocks = strain.reshape(seg_local, A // freq_count, B)
    both_parts = jnp.einsum(
        "kn,snb->skb",
        table,
        lax.all_to_all(slab_blocks, "freq", split_axis=2, concat_axis=1, tiled=True),
        precision=highest,
    )
    real_part = both_parts[:, :A]
    imag_part = both_parts[:, A:]
    second_cos, second_sin = cos_sin_table(
        jnp.arange(B, dtype=jnp.int32), jnp.arange(NB, dtype=jnp.int32), B
    )
    rotation = jnp.concatenate(
        [
            jnp.concatenate([second_cos, -second_sin], axis=1),
            jnp.concatenate([second_sin, second_cos], axis=1),
        ],
        axis=0,
    )
    amplitude = jnp.sqrt(LEN * psd)
    real_in = lax.all_to_all(
        real_part * twist_cos + imag_part * twist_sin, "freq", split_axis=1, concat_axis=2, tiled=True
    )
    imag_in = lax.all_to_all(
        imag_part * twist_cos - real_part * twist_sin, "freq", split_axis=1, concat_axis=2, tiled=True
    )
    joined = jnp.concatenate([real_in, imag_in], axis=2)
    both_out = jnp.einsum("spc,cm->smp", joined, rotation, precision=highest)
    both_out = both_out.reshape(joined.shape[0], 2, NB, joined.shape[1])
    whitened = (both_out / amplitude).astype(jnp.bfloat16)
    return lax.all_to_all(whitened, "freq", split_axis=2, concat_axis=3, tiled=True)


def exchange(sent):
    return lax.all_to_all(sent, "freq", split_axis=0, concat_axis=0, tiled=True)


def pack_strain(strain, freq_count):
    seg_local = strain.shape[0]
    sent = (strain * STRAIN_SCALE).astype(jnp.float16)
    sent = sent.reshape(seg_local, A // freq_count, freq_count, B // freq_count)
    return sent.transpose(2, 0, 1, 3)


def pack_coefs(received, table):
    freq_count, seg_local, _, width = received.shape
    coefs = first_section(received.astype(jnp.float32) * (1.0 / STRAIN_SCALE), table)
    sent = (coefs * COEF_SCALE).astype(jnp.float16)
    return sent.reshape(freq_count, seg_local // freq_count, A, width)


def whiten(received, tables, white, white_far):
    return second_section(received.astype(jnp.float32) * (1.0 / COEF_SCALE), tables, white, white_far)


def on_device(strain, psd, templates, cutoffs, lags):
    freq_count = lax.axis_size("freq")
    freq_index = lax.axis_index("freq")
    seg_local = strain.shape[0]
    tmpl_local = templates.shape[0]
    blocks_here = templates.shape[2]
    first_block = freq_index * blocks_here
    block_ids = first_block + jnp.arange(blocks_here, dtype=jnp.int32)
    cuts = cutoffs - first_block
    tied = lax.optimization_barrier

    block_cos, block_sin = cos_sin_table(block_ids, lags % B, B)
    position = jnp.arange(A, dtype=jnp.int32).reshape(A // 128, 1, 128)
    place = lags[None, :, None] * position % LEN
    place_angle = place.astype(jnp.float32) * (two_pi / LEN)
    place_cos = jnp.cos(place_angle)[None]
    place_sin = jnp.sin(place_angle)[None]
    block_cos = block_cos[:, None, :, None]
    block_sin = block_sin[:, None, :, None]
    lag_cos = block_cos * place_cos - block_sin * place_sin
    lag_sin = block_sin * place_cos + block_cos * place_sin

    sliced = (
        lax.axis_size("tmpl") == 4
        and seg_local == 2 * freq_count == 16
        and (NB // freq_count) % 32 == 0
        and B // freq_count == 128
    )
    if not sliced:
        laid = lay_out(templates, cuts, 0, 1, None)
        laid = laid.reshape(blocks_here, 2 * tmpl_local, A)
        data = lax.all_gather(general_transform(strain, psd), "tmpl", axis=0, tiled=True)
        origin = jnp.zeros((1,), jnp.int32)
        sums = []
        for start in range(0, data.shape[0], 16):
            sources = [block_rows(data[n : n + 4]) for n in range(start, start + 16, 4)]
            sums.append(lag_products(sources, origin, laid, lag_cos, lag_sin))
        sums = jnp.concatenate(sums, axis=0)
        return lax.psum_scatter(sums, "freq", scatter_dimension=0, tiled=True)

    order = mirror_table()
    psd_all = lax.all_gather(psd, "freq", axis=1, tiled=True)
    psd_far = jnp.dot(psd_all[:, HALF:], order.T, precision=lax.Precision.HIGHEST)
    white = lax.rsqrt(LEN * psd_all[:, :HALF])
    white_far = lax.rsqrt(LEN * psd_far)
    first = first_table()
    second = (twist_tables(), second_tables(), order.astype(ml_dtypes.bfloat16))

    seg_out = seg_local * lax.axis_size("tmpl") // freq_count
    by_owner = strain.reshape(seg_local // seg_out, 2, seg_out // 2, strain.shape[1])
    strain_a, strain_b = (
        pack_strain(by_owner[:, group].reshape(seg_local // 2, strain.shape[1]), freq_count)
        for group in range(2)
    )
    time_a = exchange(strain_a)
    laid = lay_out(templates, cuts, 0, 2, None)
    time_a, laid = tied((time_a, laid))
    coefs_a = pack_coefs(time_a, first)
    parts_a = exchange(coefs_a)
    laid = lay_out(templates, cuts, 1, 2, laid)
    parts_a, strain_b, laid, white, white_far, lag_cos, lag_sin = tied(
        (parts_a, strain_b, laid, white, white_far, lag_cos, lag_sin)
    )
    time_b = exchange(strain_b)
    white_a = whiten(parts_a, second, white, white_far)
    time_b, white_a = tied((time_b, white_a))
    data_a = exchange(white_a)
    coefs_b = pack_coefs(time_b, first)
    data_a, coefs_b = tied((data_a, coefs_b))
    parts_b = exchange(coefs_b)
    laid = laid.reshape(blocks_here, 2 * tmpl_local, A)
    place = lax.axis_index("tmpl").astype(jnp.int32).reshape(1)

    def halves(data):
        data = data.reshape(2, 2, 2, 2, blocks_here, A)
        return [block_rows(data[:, n].reshape(4, 2, blocks_here, A)) for n in range(2)]

    def products(part):
        return lag_products(part, place, laid, lag_cos, lag_sin)

    def collect(sums):
        return lax.psum_scatter(sums, "freq", scatter_dimension=0, tiled=True)

    def collect_late(sums):
        shares = exchange(sums.reshape(freq_count, 2, 2 * lags.shape[0], tmpl_local))
        return jnp.sum(shares, axis=0)

    first_a, second_a = halves(data_a)
    first_a = spread(first_a)
    parts_b, first_a, second_a = tied((parts_b, first_a, second_a))
    second_a = spread(second_a)
    data_b = exchange(whiten(parts_b, second, white, white_far))
    sums_a1 = products(first_a)
    data_b, second_a, sums_a1 = tied((data_b, second_a, sums_a1))
    first_b, second_b = halves(data_b)
    first_b = spread(first_b)
    out_a1 = collect(sums_a1)
    sums_a2 = products(second_a)
    first_b, second_b, sums_a2 = tied((first_b, second_b, sums_a2))
    second_b = spread(second_b)
    out_a2 = collect(sums_a2)
    sums_b1 = products(first_b)
    second_b, sums_b1 = tied((second_b, sums_b1))
    out_b1 = collect_late(sums_b1)
    sums_b2 = products(second_b)
    out_a1, out_a2, out_b1, sums_b2 = tied((out_a1, out_a2, out_b1, sums_b2))
    out_b2 = collect_late(sums_b2)
    return jnp.concatenate([out_a1, out_a2, out_b1, out_b2], axis=0)


def solution(mesh):
    placed = (P("tmpl", "freq"), P(None, "freq"), P("tmpl", None, "freq", None), P("tmpl"), P())
    return jax.shard_map(
        on_device, mesh=mesh, in_specs=placed, out_specs=P("freq", None, "tmpl"), check_vma=False
    )
```

```python
import math

import jax
import jax.numpy as jnp
import ml_dtypes
import numpy as np
from jax import lax
from jax.experimental import pallas as pl
from jax.experimental.pallas import tpu as pltpu
from jax.sharding import PartitionSpec as P

A = 512
B = 1024
LEN = 524288
NB = 512
HALF = A // 2

STRAIN_SCALE = 8192.0
COEF_SCALE = 16.0

two_pi = 2.0 * math.pi


def cos_sin_table(row_ids, col_ids, modulus):
    product = row_ids[:, None] * col_ids[None, :] % modulus
    phase_angle = product.astype(jnp.float32) * (two_pi / modulus)
    return (jnp.cos(phase_angle), jnp.sin(phase_angle))


def split_const(table):
    high = table.astype(ml_dtypes.bfloat16)
    low = (table - high.astype(np.float64)).astype(ml_dtypes.bfloat16)
    return high, low


def first_table():
    angle = two_pi * (np.outer(np.arange(HALF), np.arange(A)) % A) / A
    table = np.concatenate([np.cos(angle), -np.sin(angle)], axis=0)
    table[HALF] = 1.0 - 2.0 * (np.arange(A) % 2)
    return split_const(table)


def second_tables():
    angle = two_pi * (np.outer(np.arange(528), np.arange(B)) % B) / B
    return split_const(np.cos(angle)) + split_const(np.sin(angle))


def twist_tables():
    angle = two_pi * np.outer(np.arange(HALF), np.arange(B)) / LEN
    edge = two_pi * HALF * np.arange(B)[None, :] / LEN
    return (
        np.cos(angle).astype(np.float32),
        np.sin(angle).astype(np.float32),
        np.cos(edge).astype(np.float32),
        np.sin(edge).astype(np.float32),
    )


def mirror_table():
    table = np.zeros((HALF, HALF), np.float32)
    table[0, 0] = 1.0
    table[np.arange(1, HALF), HALF - np.arange(1, HALF)] = 1.0
    return table


def split_parts(value):
    high = value.astype(jnp.bfloat16)
    low = (value - high.astype(jnp.float32)).astype(jnp.bfloat16)
    return high, low


def dot_nn(lhs, rhs):
    return lax.dot_general(lhs, rhs, (((1,), (0,)), ((), ())), preferred_element_type=jnp.float32)


def dot_nt(lhs, rhs):
    return lax.dot_general(lhs, rhs, (((1,), (1,)), ((), ())), preferred_element_type=jnp.float32)


def first_kernel(x_ref, high_ref, low_ref, out_ref):
    parts = x_ref.shape[0]
    pair = x_ref.shape[1]
    columns = []
    for s in range(pair):
        columns.append(jnp.concatenate([x_ref[f, s] for f in range(parts)], axis=0))
    value = jnp.concatenate(columns, axis=1)
    high, low = split_parts(value)
    result = dot_nn(high_ref[...], high) + dot_nn(high_ref[...], low) + dot_nn(low_ref[...], high)
    width = x_ref.shape[3]
    for s in range(pair):
        out_ref[s] = result[:, s * width : (s + 1) * width]


def first_section(received, tables):
    parts, segs, rows, width = received.shape
    pair = 2
    return pl.pallas_call(
        first_kernel,
        grid=(segs // pair,),
        in_specs=[
            pl.BlockSpec((parts, pair, rows, width), lambda i: (0, i, 0, 0)),
            pl.BlockSpec((A, A), lambda i: (0, 0)),
            pl.BlockSpec((A, A), lambda i: (0, 0)),
        ],
        out_specs=pl.BlockSpec((pair, A, width), lambda i: (i, 0, 0)),
        out_shape=jax.ShapeDtypeStruct((segs, A, width), jnp.float32),
        compiler_params=pltpu.CompilerParams(vmem_limit_bytes=40 * 2**20),
        cost_estimate=pl.CostEstimate(
            flops=2 * 3 * segs * A * A * width, bytes_accessed=segs * A * width * 8, transcendentals=0
        ),
        name="first_section",
    )(received, *tables)


def second_kernel(
    y_ref, tc_ref, ts_ref, ec_ref, es_ref, ch_ref, cl_ref, sh_ref, sl_ref, wa_ref, wm_ref, q_ref, out_ref
):
    parts = y_ref.shape[0]
    joined = jnp.concatenate([y_ref[f, 0] for f in range(parts)], axis=1)
    real_raw = joined[:HALF]
    imag_raw = joined[HALF:]
    row_ids = lax.broadcasted_iota(jnp.int32, (HALF, B), 0)
    imag_in = jnp.where(row_ids == 0, 0.0, imag_raw)
    twist_cos = tc_ref[...]
    twist_sin = ts_ref[...]
    real_u = real_raw * twist_cos + imag_in * twist_sin
    imag_u = imag_in * twist_cos - real_raw * twist_sin
    edge = imag_raw[0:1]
    edge_rows = jnp.where(
        lax.broadcasted_iota(jnp.int32, (16, B), 0) == 0,
        edge * ec_ref[...],
        jnp.where(lax.broadcasted_iota(jnp.int32, (16, B), 0) == 1, -edge * es_ref[...], 0.0),
    )
    u_high, u_low = split_parts(jnp.concatenate([real_u, imag_u], axis=0))
    e_high, e_low = split_parts(edge_rows)

    def three(high_ref, low_ref, high, low):
        return (
            dot_nt(high_ref[...], high) + dot_nt(high_ref[...], low) + dot_nt(low_ref[...], high)
        )

    by_cos = three(ch_ref, cl_ref, u_high, u_low)
    by_sin = three(sh_ref, sl_ref, u_high, u_low)
    edge_cos = three(ch_ref, cl_ref, e_high, e_low)[:NB]
    edge_sin = three(sh_ref, sl_ref, e_high, e_low)[:NB]
    white = wa_ref[...]
    real_out = ((by_cos[:NB, :HALF] + by_sin[:NB, HALF:]) * white).astype(jnp.bfloat16)
    imag_out = ((by_cos[:NB, HALF:] - by_sin[:NB, :HALF]) * white).astype(jnp.bfloat16)
    next_cos = by_cos[1 : NB + 1]
    next_sin = by_sin[1 : NB + 1]
    lane = lax.broadcasted_iota(jnp.int32, (NB, HALF), 1)
    real_edge = edge_cos[:, 0:1] + edge_sin[:, 1:2]
    imag_edge = edge_cos[:, 1:2] - edge_sin[:, 0:1]
    real_far = jnp.where(lane == 0, real_edge, next_cos[:, :HALF] - next_sin[:, HALF:])
    imag_far = jnp.where(lane == 0, imag_edge, -next_cos[:, HALF:] - next_sin[:, :HALF])
    white_far = wm_ref[...]
    order = q_ref[...]
    real_far = dot_nn((real_far * white_far).astype(jnp.bfloat16), order).astype(jnp.bfloat16)
    imag_far = dot_nn((imag_far * white_far).astype(jnp.bfloat16), order).astype(jnp.bfloat16)
    rows = NB // parts
    for f in range(parts):
        here = slice(f * rows, (f + 1) * rows)
        out_ref[f, 0, 0, :, :HALF] = real_out[here]
        out_ref[f, 0, 0, :, HALF:] = real_far[here]
        out_ref[f, 0, 1, :, :HALF] = imag_out[here]
        out_ref[f, 0, 1, :, HALF:] = imag_far[here]


def second_section(received, tables, white, white_far):
    parts, segs, rows, width = received.shape
    twists, seconds, order = tables

    def whole(array):
        return pl.BlockSpec(array.shape, lambda i: (0,) * array.ndim)

    fixed = (*twists, *seconds, white, white_far, order)
    return pl.pallas_call(
        second_kernel,
        grid=(segs,),
        in_specs=[pl.BlockSpec((parts, 1, rows, width), lambda i: (0, i, 0, 0))]
        + [whole(array) for array in fixed],
        out_specs=pl.BlockSpec((parts, 1, 2, NB // parts, A), lambda i: (0, i, 0, 0, 0)),
        out_shape=jax.ShapeDtypeStruct((parts, segs, 2, NB // parts, A), jnp.bfloat16),
        compiler_params=pltpu.CompilerParams(vmem_limit_bytes=60 * 2**20),
        cost_estimate=pl.CostEstimate(
            flops=2 * 6 * segs * 528 * B * A, bytes_accessed=segs * A * B * 6, transcendentals=0
        ),
        name="second_section",
    )(received, *fixed)


def lag_kernel(place_ref, a_ref, b_ref, x_ref, y_ref, t_ref, c_ref, s_ref, out_ref, acc_ref, even_ref, odd_ref):
    sources = (a_ref, b_ref, x_ref, y_ref)
    segs = a_ref.shape[1] // 2
    per_quad = t_ref.shape[0]
    lag_total = c_ref.shape[2]
    tmpl = out_ref.shape[2]
    step = pl.program_id(0)
    last = pl.num_programs(0) - 1
    seg_total = len(sources) * segs
    half = seg_total * lag_total

    def make_rows(rows_ref, jj, chunk):
        lanes = slice(chunk * 128, (chunk + 1) * 128)
        values = [source[jj, :, lanes].astype(jnp.float32) for source in sources]
        real = jnp.concatenate([value[:segs] for value in values], axis=0)
        imag = jnp.concatenate([value[segs:] for value in values], axis=0)
        for lag in range(lag_total):
            repeated = pl.ds(lag, 8, stride=0)
            lag_cos = jnp.concatenate([c_ref[jj, chunk, repeated]] * (seg_total // 8), axis=0)
            lag_sin = jnp.concatenate([s_ref[jj, chunk, repeated]] * (seg_total // 8), axis=0)
            rows = slice(lag * seg_total, (lag + 1) * seg_total)
            rows_ref[jj, rows, lanes] = (real * lag_cos - imag * lag_sin).astype(jnp.bfloat16)
            rows = slice(half + lag * seg_total, half + (lag + 1) * seg_total)
            rows_ref[jj, rows, lanes] = (real * lag_sin + imag * lag_cos).astype(jnp.bfloat16)

    def one_block(next_ref, now_ref, units, jj):
        deep = 256
        for k in range(A // deep):
            inner = slice(k * deep, (k + 1) * deep)
            if now_ref is not None:
                for unit in range(2):
                    columns = t_ref[jj, unit * tmpl : (unit + 1) * tmpl, inner]
                    pltpu.matmul_push_rhs(columns, k % 2, unit, transpose=True)
            if next_ref is not None:
                for chunk in range(k * deep // 128, (k + 1) * deep // 128):
                    make_rows(next_ref, jj, chunk)
            if now_ref is not None:
                for unit_ref in units:
                    pltpu.matmul_acc_lhs(unit_ref, now_ref[jj, :, inner], load_staged_rhs=k % 2)

    def one_group(next_ref, now_ref):
        def scoped(*units):
            @pl.loop(0, per_quad)
            def _(jj):
                one_block(next_ref, now_ref, units, jj)

            for unit, unit_ref in enumerate(units):
                acc_ref[unit] += pltpu.matmul_pop(unit_ref)

        shape = acc_ref.shape[1:]
        pl.run_scoped(scoped, pltpu.ACC(0)(shape, jnp.float32), pltpu.ACC(1)(shape, jnp.float32))

    @pl.when(step == 0)
    def _():
        acc_ref[...] = jnp.zeros_like(acc_ref)

        @pl.loop(0, per_quad)
        def _(jj):
            one_block(even_ref, None, (), jj)

    @pl.when((step % 2 == 1) & (step < last))
    def _():
        one_group(odd_ref, even_ref)

    @pl.when((step % 2 == 0) & (step > 0) & (step < last))
    def _():
        one_group(even_ref, odd_ref)

    @pl.when(step == last)
    def _():
        one_group(None, odd_ref)
        by_real = acc_ref[0]
        by_imag = acc_ref[1]
        shape = (lag_total, seg_total, tmpl)
        real = by_real[:half] + by_imag[half:]
        imag = by_real[half:] - by_imag[:half]
        real = jnp.swapaxes(real.reshape(shape), 0, 1)
        imag = jnp.swapaxes(imag.reshape(shape), 0, 1)
        for index in range(len(sources)):
            here = slice(index * segs, (index + 1) * segs)
            place = pl.ds((place_ref[0] ^ index) * segs, segs)
            out_ref[place, :lag_total] = real[here]
            out_ref[place, lag_total:] = imag[here]


def lag_products(sources, place, laid, lag_cos, lag_sin):
    blocks, rows, _ = sources[0].shape
    tmpl2 = laid.shape[1]
    per_quad = min(4, blocks)
    quads = blocks // per_quad
    _, chunks, lag_total, lanes = lag_cos.shape
    segs = len(sources) * rows // 2

    def ahead(i):
        return (jnp.minimum(i, quads - 1), 0, 0)

    def ahead_lags(i):
        return (jnp.minimum(i, quads - 1), 0, 0, 0)

    return pl.pallas_call(
        lag_kernel,
        grid=(quads + 1,),
        in_specs=[pl.BlockSpec(memory_space=pltpu.SMEM)]
        + [pl.BlockSpec((per_quad, rows, A), ahead)] * len(sources)
        + [
            pl.BlockSpec((per_quad, tmpl2, A), lambda i: (jnp.maximum(i - 1, 0), 0, 0)),
            pl.BlockSpec((per_quad, chunks, lag_total, lanes), ahead_lags),
            pl.BlockSpec((per_quad, chunks, lag_total, lanes), ahead_lags),
        ],
        out_specs=pl.BlockSpec((segs, 2 * lag_total, tmpl2 // 2), lambda i: (0, 0, 0)),
        out_shape=jax.ShapeDtypeStruct((segs, 2 * lag_total, tmpl2 // 2), jnp.float32),
        scratch_shapes=[
            pltpu.VMEM((2, 2 * segs * lag_total, tmpl2 // 2), jnp.float32),
            pltpu.VMEM((per_quad, 2 * segs * lag_total, A), jnp.bfloat16),
            pltpu.VMEM((per_quad, 2 * segs * lag_total, A), jnp.bfloat16),
        ],
        compiler_params=pltpu.CompilerParams(vmem_limit_bytes=60 * 2**20),
        cost_estimate=pl.CostEstimate(
            flops=4 * segs * lag_total * tmpl2 * blocks * A,
            bytes_accessed=blocks * A * (tmpl2 * 2 + segs * 4),
            transcendentals=0,
        ),
        name="lag_products",
    )(place, *sources, laid, lag_cos, lag_sin)


def block_rows(data):
    segs, parts, blocks, _ = data.shape
    return data.transpose(2, 1, 0, 3).reshape(blocks, parts * segs, A)


def spread(data):
    moved = [lax.ppermute(data, "tmpl", [(n, n ^ bit) for n in range(4)]) for bit in (1, 2, 3)]
    return (data, *moved)


def layout_kernel(cut_ref, t_ref, *refs):
    out_ref = refs[-1]
    tmpl, _, rows, _ = t_ref.shape
    first_row = pl.program_id(0) * rows + cut_ref[cut_ref.shape[0] - 1]
    first_tmpl = pl.program_id(1) * tmpl
    row_ids = lax.broadcasted_iota(jnp.int32, (rows, 128), 0) + first_row
    batch = 16

    @pl.loop(0, tmpl // batch)
    def _(group):
        some = pl.ds(pl.multiple_of(group * batch, batch), batch)
        keeps = [row_ids < cut_ref[first_tmpl + group * batch + n] for n in range(batch)]
        for part in range(2):
            for chunk in range(A // 128):
                lanes = slice(chunk * 128, (chunk + 1) * 128)
                value = t_ref[some, part, :, lanes].astype(jnp.float32)
                value = jnp.stack([jnp.where(keeps[n], value[n], 0.0) for n in range(batch)], axis=0)
                value = jnp.swapaxes(value, 0, 1).astype(jnp.bfloat16)
                for row in range(rows):
                    out_ref[row, part, some, lanes] = value[row]


def lay_out(templates, cuts, piece, pieces, laid):
    tmpl, _, blocks, _ = templates.shape
    rows = min(16, blocks)
    steps = blocks // rows // pieces
    batch = min(64, tmpl)
    shape = (blocks, 2, tmpl, A)
    first = piece * steps
    info = jnp.concatenate([cuts, jnp.full((1,), first * rows, jnp.int32)])
    earlier = () if laid is None else (laid,)
    return pl.pallas_call(
        layout_kernel,
        grid=(steps, tmpl // batch),
        in_specs=[
            pl.BlockSpec(memory_space=pltpu.SMEM),
            pl.BlockSpec((batch, 2, rows, A), lambda i, j: (j, 0, i + first, 0)),
        ]
        + [pl.BlockSpec(memory_space=pl.ANY)] * len(earlier),
        out_specs=pl.BlockSpec((rows, 2, batch, A), lambda i, j: (i + first, 0, j, 0)),
        out_shape=jax.ShapeDtypeStruct(shape, jnp.bfloat16),
        input_output_aliases={2: 0} if earlier else {},
        compiler_params=pltpu.CompilerParams(vmem_limit_bytes=40 * 2**20),
        cost_estimate=pl.CostEstimate(
            flops=0, bytes_accessed=8 * tmpl * 2 * blocks * A // pieces, transcendentals=0
        ),
        name="lay_out",
    )(info, templates, *earlier)


def general_transform(strain, psd):
    freq_count = lax.axis_size("freq")
    freq_index = lax.axis_index("freq")
    seg_local = strain.shape[0]
    step_time = B // freq_count
    highest = lax.Precision.HIGHEST
    first_cos, first_sin = cos_sin_table(
        jnp.arange(A, dtype=jnp.int32), jnp.arange(A, dtype=jnp.int32), A
    )
    table = jnp.concatenate([first_cos, -first_sin], axis=0)
    time_ids = freq_index * step_time + jnp.arange(step_time, dtype=jnp.int32)
    twist_cos, twist_sin = cos_sin_table(jnp.arange(A, dtype=jnp.int32), time_ids, LEN)
    slab_blocks = strain.reshape(seg_local, A // freq_count, B)
    both_parts = jnp.einsum(
        "kn,snb->skb",
        table,
        lax.all_to_all(slab_blocks, "freq", split_axis=2, concat_axis=1, tiled=True),
        precision=highest,
    )
    real_part = both_parts[:, :A]
    imag_part = both_parts[:, A:]
    second_cos, second_sin = cos_sin_table(
        jnp.arange(B, dtype=jnp.int32), jnp.arange(NB, dtype=jnp.int32), B
    )
    rotation = jnp.concatenate(
        [
            jnp.concatenate([second_cos, -second_sin], axis=1),
            jnp.concatenate([second_sin, second_cos], axis=1),
        ],
        axis=0,
    )
    amplitude = jnp.sqrt(LEN * psd)
    real_in = lax.all_to_all(
        real_part * twist_cos + imag_part * twist_sin, "freq", split_axis=1, concat_axis=2, tiled=True
    )
    imag_in = lax.all_to_all(
        imag_part * twist_cos - real_part * twist_sin, "freq", split_axis=1, concat_axis=2, tiled=True
    )
    joined = jnp.concatenate([real_in, imag_in], axis=2)
    both_out = jnp.einsum("spc,cm->smp", joined, rotation, precision=highest)
    both_out = both_out.reshape(joined.shape[0], 2, NB, joined.shape[1])
    whitened = (both_out / amplitude).astype(jnp.bfloat16)
    return lax.all_to_all(whitened, "freq", split_axis=2, concat_axis=3, tiled=True)


def exchange(sent):
    return lax.all_to_all(sent, "freq", split_axis=0, concat_axis=0, tiled=True)


def pack_strain(strain, freq_count):
    seg_local = strain.shape[0]
    sent = (strain * STRAIN_SCALE).astype(jnp.float16)
    sent = sent.reshape(seg_local, A // freq_count, freq_count, B // freq_count)
    return sent.transpose(2, 0, 1, 3)


def pack_coefs(received, table):
    freq_count, seg_local, _, width = received.shape
    coefs = first_section(received.astype(jnp.float32) * (1.0 / STRAIN_SCALE), table)
    sent = (coefs * COEF_SCALE).astype(jnp.float16)
    return sent.reshape(freq_count, seg_local // freq_count, A, width)


def whiten(received, tables, white, white_far):
    return second_section(received.astype(jnp.float32) * (1.0 / COEF_SCALE), tables, white, white_far)


def on_device(strain, psd, templates, cutoffs, lags):
    freq_count = lax.axis_size("freq")
    freq_index = lax.axis_index("freq")
    seg_local = strain.shape[0]
    tmpl_local = templates.shape[0]
    blocks_here = templates.shape[2]
    first_block = freq_index * blocks_here
    block_ids = first_block + jnp.arange(blocks_here, dtype=jnp.int32)
    cuts = cutoffs - first_block
    tied = lax.optimization_barrier

    block_cos, block_sin = cos_sin_table(block_ids, lags % B, B)
    position = jnp.arange(A, dtype=jnp.int32).reshape(A // 128, 1, 128)
    place = lags[None, :, None] * position % LEN
    place_angle = place.astype(jnp.float32) * (two_pi / LEN)
    place_cos = jnp.cos(place_angle)[None]
    place_sin = jnp.sin(place_angle)[None]
    block_cos = block_cos[:, None, :, None]
    block_sin = block_sin[:, None, :, None]
    lag_cos = block_cos * place_cos - block_sin * place_sin
    lag_sin = block_sin * place_cos + block_cos * place_sin

    sliced = (
        lax.axis_size("tmpl") == 4
        and seg_local == 2 * freq_count == 16
        and (NB // freq_count) % 32 == 0
        and B // freq_count == 128
    )
    if not sliced:
        laid = lay_out(templates, cuts, 0, 1, None)
        laid = laid.reshape(blocks_here, 2 * tmpl_local, A)
        data = lax.all_gather(general_transform(strain, psd), "tmpl", axis=0, tiled=True)
        origin = jnp.zeros((1,), jnp.int32)
        sums = []
        for start in range(0, data.shape[0], 16):
            sources = [block_rows(data[n : n + 4]) for n in range(start, start + 16, 4)]
            sums.append(lag_products(sources, origin, laid, lag_cos, lag_sin))
        sums = jnp.concatenate(sums, axis=0)
        return lax.psum_scatter(sums, "freq", scatter_dimension=0, tiled=True)

    order = mirror_table()
    psd_all = lax.all_gather(psd, "freq", axis=1, tiled=True)
    psd_far = jnp.dot(psd_all[:, HALF:], order.T, precision=lax.Precision.HIGHEST)
    white = lax.rsqrt(LEN * psd_all[:, :HALF])
    white_far = lax.rsqrt(LEN * psd_far)
    first = first_table()
    second = (twist_tables(), second_tables(), order.astype(ml_dtypes.bfloat16))

    seg_out = seg_local * lax.axis_size("tmpl") // freq_count
    by_owner = strain.reshape(seg_local // seg_out, 2, seg_out // 2, strain.shape[1])
    strain_a, strain_b = (
        pack_strain(by_owner[:, group].reshape(seg_local // 2, strain.shape[1]), freq_count)
        for group in range(2)
    )
    time_a = exchange(strain_a)
    laid = lay_out(templates, cuts, 0, 2, None)
    time_a, laid = tied((time_a, laid))
    coefs_a = pack_coefs(time_a, first)
    parts_a = exchange(coefs_a)
    laid = lay_out(templates, cuts, 1, 2, laid)
    parts_a, strain_b, laid, white, white_far, lag_cos, lag_sin = tied(
        (parts_a, strain_b, laid, white, white_far, lag_cos, lag_sin)
    )
    time_b = exchange(strain_b)
    white_a = whiten(parts_a, second, white, white_far)
    time_b, white_a = tied((time_b, white_a))
    data_a = exchange(white_a)
    coefs_b = pack_coefs(time_b, first)
    data_a, coefs_b = tied((data_a, coefs_b))
    parts_b = exchange(coefs_b)
    laid = laid.reshape(blocks_here, 2 * tmpl_local, A)
    place = lax.axis_index("tmpl").astype(jnp.int32).reshape(1)

    def halves(data):
        data = data.reshape(2, 2, 2, 2, blocks_here, A)
        return [block_rows(data[:, n].reshape(4, 2, blocks_here, A)) for n in range(2)]

    def products(part):
        return lag_products(part, place, laid, lag_cos, lag_sin)

    def collect(sums):
        return lax.psum_scatter(sums, "freq", scatter_dimension=0, tiled=True)

    def collect_late(sums):
        shares = exchange(sums.reshape(freq_count, 2, 2 * lags.shape[0], tmpl_local))
        return jnp.sum(shares, axis=0)

    first_a, second_a = halves(data_a)
    first_a = spread(first_a)
    parts_b, first_a, second_a = tied((parts_b, first_a, second_a))
    second_a = spread(second_a)
    data_b = exchange(whiten(parts_b, second, white, white_far))
    sums_a1 = products(first_a)
    data_b, second_a, sums_a1 = tied((data_b, second_a, sums_a1))
    first_b, second_b = halves(data_b)
    first_b = spread(first_b)
    out_a1 = collect(sums_a1)
    sums_a2 = products(second_a)
    first_b, second_b, sums_a2 = tied((first_b, second_b, sums_a2))
    second_b = spread(second_b)
    out_a2 = collect(sums_a2)
    sums_b1 = products(first_b)
    second_b, sums_b1 = tied((second_b, sums_b1))
    out_b1 = collect_late(sums_b1)
    sums_b2 = products(second_b)
    out_a1, out_a2, out_b1, sums_b2 = tied((out_a1, out_a2, out_b1, sums_b2))
    out_b2 = collect_late(sums_b2)
    return jnp.concatenate([out_a1, out_a2, out_b1, out_b2], axis=0)


def solution(mesh):
    placed = (P("tmpl", "freq"), P(None, "freq"), P("tmpl", None, "freq", None), P("tmpl"), P())
    return jax.shard_map(
        on_device, mesh=mesh, in_specs=placed, out_specs=P("freq", None, "tmpl"), check_vma=False
    )
```

```python
import math

import jax
import jax.numpy as jnp
import ml_dtypes
import numpy as np
from jax import lax
from jax.experimental import pallas as pl
from jax.experimental.pallas import tpu as pltpu
from jax.sharding import PartitionSpec as P

A = 512
B = 1024
LEN = 524288
NB = 512
HALF = A // 2

STRAIN_SCALE = 8192.0
COEF_SCALE = 16.0

two_pi = 2.0 * math.pi


def cos_sin_table(row_ids, col_ids, modulus):
    product = row_ids[:, None] * col_ids[None, :] % modulus
    phase_angle = product.astype(jnp.float32) * (two_pi / modulus)
    return (jnp.cos(phase_angle), jnp.sin(phase_angle))


def split_const(table):
    high = table.astype(ml_dtypes.bfloat16)
    low = (table - high.astype(np.float64)).astype(ml_dtypes.bfloat16)
    return high, low


def first_table():
    angle = two_pi * (np.outer(np.arange(HALF), np.arange(A)) % A) / A
    table = np.concatenate([np.cos(angle), -np.sin(angle)], axis=0)
    table[HALF] = 1.0 - 2.0 * (np.arange(A) % 2)
    return split_const(table)


def second_tables():
    angle = two_pi * (np.outer(np.arange(528), np.arange(B)) % B) / B
    return split_const(np.cos(angle)) + split_const(np.sin(angle))


def twist_tables():
    angle = two_pi * np.outer(np.arange(HALF), np.arange(B)) / LEN
    edge = two_pi * HALF * np.arange(B)[None, :] / LEN
    return (
        np.cos(angle).astype(np.float32),
        np.sin(angle).astype(np.float32),
        np.cos(edge).astype(np.float32),
        np.sin(edge).astype(np.float32),
    )


def mirror_table():
    table = np.zeros((HALF, HALF), np.float32)
    table[0, 0] = 1.0
    table[np.arange(1, HALF), HALF - np.arange(1, HALF)] = 1.0
    return table


def split_parts(value):
    high = value.astype(jnp.bfloat16)
    low = (value - high.astype(jnp.float32)).astype(jnp.bfloat16)
    return high, low


def dot_nn(lhs, rhs):
    return lax.dot_general(lhs, rhs, (((1,), (0,)), ((), ())), preferred_element_type=jnp.float32)


def dot_nt(lhs, rhs):
    return lax.dot_general(lhs, rhs, (((1,), (1,)), ((), ())), preferred_element_type=jnp.float32)


def first_kernel(x_ref, high_ref, low_ref, out_ref):
    parts = x_ref.shape[0]
    pair = x_ref.shape[1]
    columns = []
    for s in range(pair):
        columns.append(jnp.concatenate([x_ref[f, s] for f in range(parts)], axis=0))
    value = jnp.concatenate(columns, axis=1)
    high, low = split_parts(value)
    result = dot_nn(high_ref[...], high) + dot_nn(high_ref[...], low) + dot_nn(low_ref[...], high)
    width = x_ref.shape[3]
    for s in range(pair):
        out_ref[s] = result[:, s * width : (s + 1) * width]


def first_section(received, tables):
    parts, segs, rows, width = received.shape
    pair = 2
    return pl.pallas_call(
        first_kernel,
        grid=(segs // pair,),
        in_specs=[
            pl.BlockSpec((parts, pair, rows, width), lambda i: (0, i, 0, 0)),
            pl.BlockSpec((A, A), lambda i: (0, 0)),
            pl.BlockSpec((A, A), lambda i: (0, 0)),
        ],
        out_specs=pl.BlockSpec((pair, A, width), lambda i: (i, 0, 0)),
        out_shape=jax.ShapeDtypeStruct((segs, A, width), jnp.float32),
        compiler_params=pltpu.CompilerParams(vmem_limit_bytes=40 * 2**20),
        cost_estimate=pl.CostEstimate(
            flops=2 * 3 * segs * A * A * width, bytes_accessed=segs * A * width * 8, transcendentals=0
        ),
        name="first_section",
    )(received, *tables)


def second_kernel(
    y_ref, tc_ref, ts_ref, ec_ref, es_ref, ch_ref, cl_ref, sh_ref, sl_ref, wa_ref, wm_ref, q_ref, out_ref
):
    parts = y_ref.shape[0]
    joined = jnp.concatenate([y_ref[f, 0] for f in range(parts)], axis=1)
    real_raw = joined[:HALF]
    imag_raw = joined[HALF:]
    row_ids = lax.broadcasted_iota(jnp.int32, (HALF, B), 0)
    imag_in = jnp.where(row_ids == 0, 0.0, imag_raw)
    twist_cos = tc_ref[...]
    twist_sin = ts_ref[...]
    real_u = real_raw * twist_cos + imag_in * twist_sin
    imag_u = imag_in * twist_cos - real_raw * twist_sin
    edge = imag_raw[0:1]
    edge_rows = jnp.where(
        lax.broadcasted_iota(jnp.int32, (16, B), 0) == 0,
        edge * ec_ref[...],
        jnp.where(lax.broadcasted_iota(jnp.int32, (16, B), 0) == 1, -edge * es_ref[...], 0.0),
    )
    u_high, u_low = split_parts(jnp.concatenate([real_u, imag_u], axis=0))
    e_high, e_low = split_parts(edge_rows)

    def three(high_ref, low_ref, high, low):
        return (
            dot_nt(high_ref[...], high) + dot_nt(high_ref[...], low) + dot_nt(low_ref[...], high)
        )

    by_cos = three(ch_ref, cl_ref, u_high, u_low)
    by_sin = three(sh_ref, sl_ref, u_high, u_low)
    edge_cos = three(ch_ref, cl_ref, e_high, e_low)[:NB]
    edge_sin = three(sh_ref, sl_ref, e_high, e_low)[:NB]
    white = wa_ref[...]
    real_out = ((by_cos[:NB, :HALF] + by_sin[:NB, HALF:]) * white).astype(jnp.bfloat16)
    imag_out = ((by_cos[:NB, HALF:] - by_sin[:NB, :HALF]) * white).astype(jnp.bfloat16)
    next_cos = by_cos[1 : NB + 1]
    next_sin = by_sin[1 : NB + 1]
    lane = lax.broadcasted_iota(jnp.int32, (NB, HALF), 1)
    real_edge = edge_cos[:, 0:1] + edge_sin[:, 1:2]
    imag_edge = edge_cos[:, 1:2] - edge_sin[:, 0:1]
    real_far = jnp.where(lane == 0, real_edge, next_cos[:, :HALF] - next_sin[:, HALF:])
    imag_far = jnp.where(lane == 0, imag_edge, -next_cos[:, HALF:] - next_sin[:, :HALF])
    white_far = wm_ref[...]
    order = q_ref[...]
    real_far = dot_nn((real_far * white_far).astype(jnp.bfloat16), order).astype(jnp.bfloat16)
    imag_far = dot_nn((imag_far * white_far).astype(jnp.bfloat16), order).astype(jnp.bfloat16)
    rows = NB // parts
    for f in range(parts):
        here = slice(f * rows, (f + 1) * rows)
        out_ref[f, 0, 0, :, :HALF] = real_out[here]
        out_ref[f, 0, 0, :, HALF:] = real_far[here]
        out_ref[f, 0, 1, :, :HALF] = imag_out[here]
        out_ref[f, 0, 1, :, HALF:] = imag_far[here]


def second_section(received, tables, white, white_far):
    parts, segs, rows, width = received.shape
    twists, seconds, order = tables

    def whole(array):
        return pl.BlockSpec(array.shape, lambda i: (0,) * array.ndim)

    fixed = (*twists, *seconds, white, white_far, order)
    return pl.pallas_call(
        second_kernel,
        grid=(segs,),
        in_specs=[pl.BlockSpec((parts, 1, rows, width), lambda i: (0, i, 0, 0))]
        + [whole(array) for array in fixed],
        out_specs=pl.BlockSpec((parts, 1, 2, NB // parts, A), lambda i: (0, i, 0, 0, 0)),
        out_shape=jax.ShapeDtypeStruct((parts, segs, 2, NB // parts, A), jnp.bfloat16),
        compiler_params=pltpu.CompilerParams(vmem_limit_bytes=60 * 2**20),
        cost_estimate=pl.CostEstimate(
            flops=2 * 6 * segs * 528 * B * A, bytes_accessed=segs * A * B * 6, transcendentals=0
        ),
        name="second_section",
    )(received, *fixed)


def lag_kernel(place_ref, a_ref, b_ref, x_ref, y_ref, t_ref, c_ref, s_ref, out_ref, acc_ref, even_ref, odd_ref):
    sources = (a_ref, b_ref, x_ref, y_ref)
    segs = a_ref.shape[1] // 2
    per_quad = t_ref.shape[0]
    lag_total = c_ref.shape[2]
    tmpl = out_ref.shape[2]
    step = pl.program_id(0)
    last = pl.num_programs(0) - 1
    seg_total = len(sources) * segs
    half = seg_total * lag_total

    def make_rows(rows_ref, jj, chunk):
        lanes = slice(chunk * 128, (chunk + 1) * 128)
        values = [source[jj, :, lanes].astype(jnp.float32) for source in sources]
        real = jnp.concatenate([value[:segs] for value in values], axis=0)
        imag = jnp.concatenate([value[segs:] for value in values], axis=0)
        for lag in range(lag_total):
            repeated = pl.ds(lag, 8, stride=0)
            lag_cos = jnp.concatenate([c_ref[jj, chunk, repeated]] * (seg_total // 8), axis=0)
            lag_sin = jnp.concatenate([s_ref[jj, chunk, repeated]] * (seg_total // 8), axis=0)
            rows = slice(lag * seg_total, (lag + 1) * seg_total)
            rows_ref[jj, rows, lanes] = (real * lag_cos - imag * lag_sin).astype(jnp.bfloat16)
            rows = slice(half + lag * seg_total, half + (lag + 1) * seg_total)
            rows_ref[jj, rows, lanes] = (real * lag_sin + imag * lag_cos).astype(jnp.bfloat16)

    deep = 256
    tiles = [(jj, k) for jj in range(per_quad) for k in range(A // deep)]

    def push(index):
        jj, k = tiles[index]
        for unit in range(2):
            columns = t_ref[jj, unit * tmpl : (unit + 1) * tmpl, k * deep : (k + 1) * deep]
            pltpu.matmul_push_rhs(columns, index % 2, unit, transpose=True)

    def one_group(next_ref, now_ref):
        def scoped(*units):
            push(0)
            for index, (jj, k) in enumerate(tiles):
                if index + 1 < len(tiles):
                    push(index + 1)
                for unit_ref in units:
                    rows = now_ref[jj, :, k * deep : (k + 1) * deep]
                    pltpu.matmul_acc_lhs(unit_ref, rows, load_staged_rhs=index % 2)
                if next_ref is not None:
                    for chunk in range(k * deep // 128, (k + 1) * deep // 128):
                        make_rows(next_ref, jj, chunk)
            for unit, unit_ref in enumerate(units):
                acc_ref[unit] += pltpu.matmul_pop(unit_ref)

        shape = acc_ref.shape[1:]
        pl.run_scoped(scoped, pltpu.ACC(0)(shape, jnp.float32), pltpu.ACC(1)(shape, jnp.float32))

    @pl.when(step == 0)
    def _():
        acc_ref[...] = jnp.zeros_like(acc_ref)

        @pl.loop(0, per_quad)
        def _(jj):
            for chunk in range(A // 128):
                make_rows(even_ref, jj, chunk)

    @pl.when((step % 2 == 1) & (step < last))
    def _():
        one_group(odd_ref, even_ref)

    @pl.when((step % 2 == 0) & (step > 0) & (step < last))
    def _():
        one_group(even_ref, odd_ref)

    @pl.when(step == last)
    def _():
        one_group(None, odd_ref)
        by_real = acc_ref[0]
        by_imag = acc_ref[1]
        shape = (lag_total, seg_total, tmpl)
        real = by_real[:half] + by_imag[half:]
        imag = by_real[half:] - by_imag[:half]
        real = jnp.swapaxes(real.reshape(shape), 0, 1)
        imag = jnp.swapaxes(imag.reshape(shape), 0, 1)
        for index in range(len(sources)):
            here = slice(index * segs, (index + 1) * segs)
            place = pl.ds((place_ref[0] ^ index) * segs, segs)
            out_ref[place, :lag_total] = real[here]
            out_ref[place, lag_total:] = imag[here]


def lag_products(sources, place, laid, lag_cos, lag_sin):
    blocks, rows, _ = sources[0].shape
    tmpl2 = laid.shape[1]
    per_quad = min(4, blocks)
    quads = blocks // per_quad
    _, chunks, lag_total, lanes = lag_cos.shape
    segs = len(sources) * rows // 2

    def ahead(i):
        return (jnp.minimum(i, quads - 1), 0, 0)

    def ahead_lags(i):
        return (jnp.minimum(i, quads - 1), 0, 0, 0)

    return pl.pallas_call(
        lag_kernel,
        grid=(quads + 1,),
        in_specs=[pl.BlockSpec(memory_space=pltpu.SMEM)]
        + [pl.BlockSpec((per_quad, rows, A), ahead)] * len(sources)
        + [
            pl.BlockSpec((per_quad, tmpl2, A), lambda i: (jnp.maximum(i - 1, 0), 0, 0)),
            pl.BlockSpec((per_quad, chunks, lag_total, lanes), ahead_lags),
            pl.BlockSpec((per_quad, chunks, lag_total, lanes), ahead_lags),
        ],
        out_specs=pl.BlockSpec((segs, 2 * lag_total, tmpl2 // 2), lambda i: (0, 0, 0)),
        out_shape=jax.ShapeDtypeStruct((segs, 2 * lag_total, tmpl2 // 2), jnp.float32),
        scratch_shapes=[
            pltpu.VMEM((2, 2 * segs * lag_total, tmpl2 // 2), jnp.float32),
            pltpu.VMEM((per_quad, 2 * segs * lag_total, A), jnp.bfloat16),
            pltpu.VMEM((per_quad, 2 * segs * lag_total, A), jnp.bfloat16),
        ],
        compiler_params=pltpu.CompilerParams(vmem_limit_bytes=60 * 2**20),
        cost_estimate=pl.CostEstimate(
            flops=4 * segs * lag_total * tmpl2 * blocks * A,
            bytes_accessed=blocks * A * (tmpl2 * 2 + segs * 4),
            transcendentals=0,
        ),
        name="lag_products",
    )(place, *sources, laid, lag_cos, lag_sin)


def block_rows(data):
    segs, parts, blocks, _ = data.shape
    return data.transpose(2, 1, 0, 3).reshape(blocks, parts * segs, A)


def spread(data):
    moved = [lax.ppermute(data, "tmpl", [(n, n ^ bit) for n in range(4)]) for bit in (1, 2, 3)]
    return (data, *moved)


def layout_kernel(cut_ref, t_ref, *refs):
    out_ref = refs[-1]
    tmpl, _, rows, _ = t_ref.shape
    first_row = pl.program_id(0) * rows + cut_ref[cut_ref.shape[0] - 1]
    first_tmpl = pl.program_id(1) * tmpl
    row_ids = lax.broadcasted_iota(jnp.int32, (rows, 128), 0) + first_row
    batch = 16

    @pl.loop(0, tmpl // batch)
    def _(group):
        some = pl.ds(pl.multiple_of(group * batch, batch), batch)
        keeps = [row_ids < cut_ref[first_tmpl + group * batch + n] for n in range(batch)]
        for part in range(2):
            for chunk in range(A // 128):
                lanes = slice(chunk * 128, (chunk + 1) * 128)
                value = t_ref[some, part, :, lanes].astype(jnp.float32)
                value = jnp.stack([jnp.where(keeps[n], value[n], 0.0) for n in range(batch)], axis=0)
                value = jnp.swapaxes(value, 0, 1).astype(jnp.bfloat16)
                for row in range(rows):
                    out_ref[row, part, some, lanes] = value[row]


def lay_out(templates, cuts, piece, pieces, laid):
    tmpl, _, blocks, _ = templates.shape
    rows = min(16, blocks)
    steps = blocks // rows // pieces
    batch = min(64, tmpl)
    shape = (blocks, 2, tmpl, A)
    first = piece * steps
    info = jnp.concatenate([cuts, jnp.full((1,), first * rows, jnp.int32)])
    earlier = () if laid is None else (laid,)
    return pl.pallas_call(
        layout_kernel,
        grid=(steps, tmpl // batch),
        in_specs=[
            pl.BlockSpec(memory_space=pltpu.SMEM),
            pl.BlockSpec((batch, 2, rows, A), lambda i, j: (j, 0, i + first, 0)),
        ]
        + [pl.BlockSpec(memory_space=pl.ANY)] * len(earlier),
        out_specs=pl.BlockSpec((rows, 2, batch, A), lambda i, j: (i + first, 0, j, 0)),
        out_shape=jax.ShapeDtypeStruct(shape, jnp.bfloat16),
        input_output_aliases={2: 0} if earlier else {},
        compiler_params=pltpu.CompilerParams(vmem_limit_bytes=40 * 2**20),
        cost_estimate=pl.CostEstimate(
            flops=0, bytes_accessed=8 * tmpl * 2 * blocks * A // pieces, transcendentals=0
        ),
        name="lay_out",
    )(info, templates, *earlier)


def general_transform(strain, psd):
    freq_count = lax.axis_size("freq")
    freq_index = lax.axis_index("freq")
    seg_local = strain.shape[0]
    step_time = B // freq_count
    highest = lax.Precision.HIGHEST
    first_cos, first_sin = cos_sin_table(
        jnp.arange(A, dtype=jnp.int32), jnp.arange(A, dtype=jnp.int32), A
    )
    table = jnp.concatenate([first_cos, -first_sin], axis=0)
    time_ids = freq_index * step_time + jnp.arange(step_time, dtype=jnp.int32)
    twist_cos, twist_sin = cos_sin_table(jnp.arange(A, dtype=jnp.int32), time_ids, LEN)
    slab_blocks = strain.reshape(seg_local, A // freq_count, B)
    both_parts = jnp.einsum(
        "kn,snb->skb",
        table,
        lax.all_to_all(slab_blocks, "freq", split_axis=2, concat_axis=1, tiled=True),
        precision=highest,
    )
    real_part = both_parts[:, :A]
    imag_part = both_parts[:, A:]
    second_cos, second_sin = cos_sin_table(
        jnp.arange(B, dtype=jnp.int32), jnp.arange(NB, dtype=jnp.int32), B
    )
    rotation = jnp.concatenate(
        [
            jnp.concatenate([second_cos, -second_sin], axis=1),
            jnp.concatenate([second_sin, second_cos], axis=1),
        ],
        axis=0,
    )
    amplitude = jnp.sqrt(LEN * psd)
    real_in = lax.all_to_all(
        real_part * twist_cos + imag_part * twist_sin, "freq", split_axis=1, concat_axis=2, tiled=True
    )
    imag_in = lax.all_to_all(
        imag_part * twist_cos - real_part * twist_sin, "freq", split_axis=1, concat_axis=2, tiled=True
    )
    joined = jnp.concatenate([real_in, imag_in], axis=2)
    both_out = jnp.einsum("spc,cm->smp", joined, rotation, precision=highest)
    both_out = both_out.reshape(joined.shape[0], 2, NB, joined.shape[1])
    whitened = (both_out / amplitude).astype(jnp.bfloat16)
    return lax.all_to_all(whitened, "freq", split_axis=2, concat_axis=3, tiled=True)


def exchange(sent):
    return lax.all_to_all(sent, "freq", split_axis=0, concat_axis=0, tiled=True)


def pack_strain(strain, freq_count):
    seg_local = strain.shape[0]
    sent = (strain * STRAIN_SCALE).astype(jnp.float16)
    sent = sent.reshape(seg_local, A // freq_count, freq_count, B // freq_count)
    return sent.transpose(2, 0, 1, 3)


def pack_coefs(received, table):
    freq_count, seg_local, _, width = received.shape
    coefs = first_section(received.astype(jnp.float32) * (1.0 / STRAIN_SCALE), table)
    sent = (coefs * COEF_SCALE).astype(jnp.float16)
    return sent.reshape(freq_count, seg_local // freq_count, A, width)


def whiten(received, tables, white, white_far):
    return second_section(received.astype(jnp.float32) * (1.0 / COEF_SCALE), tables, white, white_far)


def on_device(strain, psd, templates, cutoffs, lags):
    freq_count = lax.axis_size("freq")
    freq_index = lax.axis_index("freq")
    seg_local = strain.shape[0]
    tmpl_local = templates.shape[0]
    blocks_here = templates.shape[2]
    first_block = freq_index * blocks_here
    block_ids = first_block + jnp.arange(blocks_here, dtype=jnp.int32)
    cuts = cutoffs - first_block
    tied = lax.optimization_barrier

    block_cos, block_sin = cos_sin_table(block_ids, lags % B, B)
    position = jnp.arange(A, dtype=jnp.int32).reshape(A // 128, 1, 128)
    place = lags[None, :, None] * position % LEN
    place_angle = place.astype(jnp.float32) * (two_pi / LEN)
    place_cos = jnp.cos(place_angle)[None]
    place_sin = jnp.sin(place_angle)[None]
    block_cos = block_cos[:, None, :, None]
    block_sin = block_sin[:, None, :, None]
    lag_cos = block_cos * place_cos - block_sin * place_sin
    lag_sin = block_sin * place_cos + block_cos * place_sin

    sliced = (
        lax.axis_size("tmpl") == 4
        and seg_local == 2 * freq_count == 16
        and (NB // freq_count) % 32 == 0
        and B // freq_count == 128
    )
    if not sliced:
        laid = lay_out(templates, cuts, 0, 1, None)
        laid = laid.reshape(blocks_here, 2 * tmpl_local, A)
        data = lax.all_gather(general_transform(strain, psd), "tmpl", axis=0, tiled=True)
        origin = jnp.zeros((1,), jnp.int32)
        sums = []
        for start in range(0, data.shape[0], 16):
            sources = [block_rows(data[n : n + 4]) for n in range(start, start + 16, 4)]
            sums.append(lag_products(sources, origin, laid, lag_cos, lag_sin))
        sums = jnp.concatenate(sums, axis=0)
        return lax.psum_scatter(sums, "freq", scatter_dimension=0, tiled=True)

    order = mirror_table()
    psd_all = lax.all_gather(psd, "freq", axis=1, tiled=True)
    psd_far = jnp.dot(psd_all[:, HALF:], order.T, precision=lax.Precision.HIGHEST)
    white = lax.rsqrt(LEN * psd_all[:, :HALF])
    white_far = lax.rsqrt(LEN * psd_far)
    first = first_table()
    second = (twist_tables(), second_tables(), order.astype(ml_dtypes.bfloat16))

    seg_out = seg_local * lax.axis_size("tmpl") // freq_count
    by_owner = strain.reshape(seg_local // seg_out, 2, seg_out // 2, strain.shape[1])
    strain_a, strain_b = (
        pack_strain(by_owner[:, group].reshape(seg_local // 2, strain.shape[1]), freq_count)
        for group in range(2)
    )
    time_a = exchange(strain_a)
    laid = lay_out(templates, cuts, 0, 2, None)
    time_a, laid = tied((time_a, laid))
    coefs_a = pack_coefs(time_a, first)
    parts_a = exchange(coefs_a)
    laid = lay_out(templates, cuts, 1, 2, laid)
    parts_a, strain_b, laid, white, white_far, lag_cos, lag_sin = tied(
        (parts_a, strain_b, laid, white, white_far, lag_cos, lag_sin)
    )
    time_b = exchange(strain_b)
    white_a = whiten(parts_a, second, white, white_far)
    time_b, white_a = tied((time_b, white_a))
    data_a = exchange(white_a)
    coefs_b = pack_coefs(time_b, first)
    data_a, coefs_b = tied((data_a, coefs_b))
    parts_b = exchange(coefs_b)
    laid = laid.reshape(blocks_here, 2 * tmpl_local, A)
    place = lax.axis_index("tmpl").astype(jnp.int32).reshape(1)

    def halves(data):
        data = data.reshape(2, 2, 2, 2, blocks_here, A)
        return [block_rows(data[:, n].reshape(4, 2, blocks_here, A)) for n in range(2)]

    def products(part):
        return lag_products(part, place, laid, lag_cos, lag_sin)

    def collect(sums):
        return lax.psum_scatter(sums, "freq", scatter_dimension=0, tiled=True)

    def collect_late(sums):
        shares = exchange(sums.reshape(freq_count, 2, 2 * lags.shape[0], tmpl_local))
        return jnp.sum(shares, axis=0)

    first_a, second_a = halves(data_a)
    first_a = spread(first_a)
    parts_b, first_a, second_a = tied((parts_b, first_a, second_a))
    second_a = spread(second_a)
    data_b = exchange(whiten(parts_b, second, white, white_far))
    sums_a1 = products(first_a)
    data_b, second_a, sums_a1 = tied((data_b, second_a, sums_a1))
    first_b, second_b = halves(data_b)
    first_b = spread(first_b)
    out_a1 = collect(sums_a1)
    sums_a2 = products(second_a)
    first_b, second_b, sums_a2 = tied((first_b, second_b, sums_a2))
    second_b = spread(second_b)
    out_a2 = collect(sums_a2)
    sums_b1 = products(first_b)
    second_b, sums_b1 = tied((second_b, sums_b1))
    out_b1 = collect_late(sums_b1)
    sums_b2 = products(second_b)
    out_a1, out_a2, out_b1, sums_b2 = tied((out_a1, out_a2, out_b1, sums_b2))
    out_b2 = collect_late(sums_b2)
    return jnp.concatenate([out_a1, out_a2, out_b1, out_b2], axis=0)


def solution(mesh):
    placed = (P("tmpl", "freq"), P(None, "freq"), P("tmpl", None, "freq", None), P("tmpl"), P())
    return jax.shard_map(
        on_device, mesh=mesh, in_specs=placed, out_specs=P("freq", None, "tmpl"), check_vma=False
    )
```

```python
import math

import jax
import jax.numpy as jnp
import ml_dtypes
import numpy as np
from jax import lax
from jax.experimental import pallas as pl
from jax.experimental.pallas import tpu as pltpu
from jax.sharding import PartitionSpec as P

A = 512
B = 1024
LEN = 524288
NB = 512
HALF = A // 2

STRAIN_SCALE = 8192.0
COEF_SCALE = 16.0

two_pi = 2.0 * math.pi


def cos_sin_table(row_ids, col_ids, modulus):
    product = row_ids[:, None] * col_ids[None, :] % modulus
    phase_angle = product.astype(jnp.float32) * (two_pi / modulus)
    return (jnp.cos(phase_angle), jnp.sin(phase_angle))


def split_const(table):
    high = table.astype(ml_dtypes.bfloat16)
    low = (table - high.astype(np.float64)).astype(ml_dtypes.bfloat16)
    return high, low


def first_table():
    angle = two_pi * (np.outer(np.arange(HALF), np.arange(A)) % A) / A
    table = np.concatenate([np.cos(angle), -np.sin(angle)], axis=0)
    table[HALF] = 1.0 - 2.0 * (np.arange(A) % 2)
    return split_const(table)


def second_tables():
    angle = two_pi * (np.outer(np.arange(528), np.arange(B)) % B) / B
    return split_const(np.cos(angle)) + split_const(np.sin(angle))


def twist_tables():
    angle = two_pi * np.outer(np.arange(HALF), np.arange(B)) / LEN
    edge = two_pi * HALF * np.arange(B)[None, :] / LEN
    return (
        np.cos(angle).astype(np.float32),
        np.sin(angle).astype(np.float32),
        np.cos(edge).astype(np.float32),
        np.sin(edge).astype(np.float32),
    )


def mirror_table():
    table = np.zeros((HALF, HALF), np.float32)
    table[0, 0] = 1.0
    table[np.arange(1, HALF), HALF - np.arange(1, HALF)] = 1.0
    return table


def split_parts(value):
    high = value.astype(jnp.bfloat16)
    low = (value - high.astype(jnp.float32)).astype(jnp.bfloat16)
    return high, low


def dot_nn(lhs, rhs):
    return lax.dot_general(lhs, rhs, (((1,), (0,)), ((), ())), preferred_element_type=jnp.float32)


def dot_nt(lhs, rhs):
    return lax.dot_general(lhs, rhs, (((1,), (1,)), ((), ())), preferred_element_type=jnp.float32)


def first_kernel(x_ref, high_ref, low_ref, out_ref):
    parts = x_ref.shape[0]
    pair = x_ref.shape[1]
    columns = []
    for s in range(pair):
        columns.append(jnp.concatenate([x_ref[f, s] for f in range(parts)], axis=0))
    value = jnp.concatenate(columns, axis=1)
    high, low = split_parts(value)
    result = dot_nn(high_ref[...], high) + dot_nn(high_ref[...], low) + dot_nn(low_ref[...], high)
    width = x_ref.shape[3]
    for s in range(pair):
        out_ref[s] = result[:, s * width : (s + 1) * width]


def first_section(received, tables):
    parts, segs, rows, width = received.shape
    pair = 2
    return pl.pallas_call(
        first_kernel,
        grid=(segs // pair,),
        in_specs=[
            pl.BlockSpec((parts, pair, rows, width), lambda i: (0, i, 0, 0)),
            pl.BlockSpec((A, A), lambda i: (0, 0)),
            pl.BlockSpec((A, A), lambda i: (0, 0)),
        ],
        out_specs=pl.BlockSpec((pair, A, width), lambda i: (i, 0, 0)),
        out_shape=jax.ShapeDtypeStruct((segs, A, width), jnp.float32),
        compiler_params=pltpu.CompilerParams(vmem_limit_bytes=40 * 2**20),
        cost_estimate=pl.CostEstimate(
            flops=2 * 3 * segs * A * A * width, bytes_accessed=segs * A * width * 8, transcendentals=0
        ),
        name="first_section",
    )(received, *tables)


def second_kernel(
    y_ref, tc_ref, ts_ref, ec_ref, es_ref, ch_ref, cl_ref, sh_ref, sl_ref, wa_ref, wm_ref, q_ref, out_ref
):
    parts = y_ref.shape[0]
    joined = jnp.concatenate([y_ref[f, 0] for f in range(parts)], axis=1)
    real_raw = joined[:HALF]
    imag_raw = joined[HALF:]
    row_ids = lax.broadcasted_iota(jnp.int32, (HALF, B), 0)
    imag_in = jnp.where(row_ids == 0, 0.0, imag_raw)
    twist_cos = tc_ref[...]
    twist_sin = ts_ref[...]
    real_u = real_raw * twist_cos + imag_in * twist_sin
    imag_u = imag_in * twist_cos - real_raw * twist_sin
    edge = imag_raw[0:1]
    edge_rows = jnp.where(
        lax.broadcasted_iota(jnp.int32, (16, B), 0) == 0,
        edge * ec_ref[...],
        jnp.where(lax.broadcasted_iota(jnp.int32, (16, B), 0) == 1, -edge * es_ref[...], 0.0),
    )
    u_high, u_low = split_parts(jnp.concatenate([real_u, imag_u], axis=0))
    e_high, e_low = split_parts(edge_rows)

    def three(high_ref, low_ref, high, low):
        return (
            dot_nt(high_ref[...], high) + dot_nt(high_ref[...], low) + dot_nt(low_ref[...], high)
        )

    by_cos = three(ch_ref, cl_ref, u_high, u_low)
    by_sin = three(sh_ref, sl_ref, u_high, u_low)
    edge_cos = three(ch_ref, cl_ref, e_high, e_low)[:NB]
    edge_sin = three(sh_ref, sl_ref, e_high, e_low)[:NB]
    white = wa_ref[...]
    real_out = ((by_cos[:NB, :HALF] + by_sin[:NB, HALF:]) * white).astype(jnp.bfloat16)
    imag_out = ((by_cos[:NB, HALF:] - by_sin[:NB, :HALF]) * white).astype(jnp.bfloat16)
    next_cos = by_cos[1 : NB + 1]
    next_sin = by_sin[1 : NB + 1]
    lane = lax.broadcasted_iota(jnp.int32, (NB, HALF), 1)
    real_edge = edge_cos[:, 0:1] + edge_sin[:, 1:2]
    imag_edge = edge_cos[:, 1:2] - edge_sin[:, 0:1]
    real_far = jnp.where(lane == 0, real_edge, next_cos[:, :HALF] - next_sin[:, HALF:])
    imag_far = jnp.where(lane == 0, imag_edge, -next_cos[:, HALF:] - next_sin[:, :HALF])
    white_far = wm_ref[...]
    order = q_ref[...]
    real_far = dot_nn((real_far * white_far).astype(jnp.bfloat16), order).astype(jnp.bfloat16)
    imag_far = dot_nn((imag_far * white_far).astype(jnp.bfloat16), order).astype(jnp.bfloat16)
    rows = NB // parts
    for f in range(parts):
        here = slice(f * rows, (f + 1) * rows)
        out_ref[f, 0, 0, :, :HALF] = real_out[here]
        out_ref[f, 0, 0, :, HALF:] = real_far[here]
        out_ref[f, 0, 1, :, :HALF] = imag_out[here]
        out_ref[f, 0, 1, :, HALF:] = imag_far[here]


def second_section(received, tables, white, white_far):
    parts, segs, rows, width = received.shape
    twists, seconds, order = tables

    def whole(array):
        return pl.BlockSpec(array.shape, lambda i: (0,) * array.ndim)

    fixed = (*twists, *seconds, white, white_far, order)
    return pl.pallas_call(
        second_kernel,
        grid=(segs,),
        in_specs=[pl.BlockSpec((parts, 1, rows, width), lambda i: (0, i, 0, 0))]
        + [whole(array) for array in fixed],
        out_specs=pl.BlockSpec((parts, 1, 2, NB // parts, A), lambda i: (0, i, 0, 0, 0)),
        out_shape=jax.ShapeDtypeStruct((parts, segs, 2, NB // parts, A), jnp.bfloat16),
        compiler_params=pltpu.CompilerParams(vmem_limit_bytes=60 * 2**20),
        cost_estimate=pl.CostEstimate(
            flops=2 * 6 * segs * 528 * B * A, bytes_accessed=segs * A * B * 6, transcendentals=0
        ),
        name="second_section",
    )(received, *fixed)


def lag_kernel(place_ref, a_ref, b_ref, x_ref, y_ref, t_ref, c_ref, s_ref, out_ref, acc_ref, even_ref, odd_ref):
    sources = (a_ref, b_ref, x_ref, y_ref)
    segs = a_ref.shape[1] // 2
    per_quad = t_ref.shape[0]
    lag_total = c_ref.shape[2]
    tmpl = out_ref.shape[2]
    step = pl.program_id(0)
    last = pl.num_programs(0) - 1
    seg_total = len(sources) * segs
    half = seg_total * lag_total

    def make_rows(rows_ref, jj, chunk):
        lanes = slice(chunk * 128, (chunk + 1) * 128)
        values = [source[jj, :, lanes].astype(jnp.float32) for source in sources]
        real = jnp.concatenate([value[:segs] for value in values], axis=0)
        imag = jnp.concatenate([value[segs:] for value in values], axis=0)
        for lag in range(lag_total):
            repeated = pl.ds(lag, 8, stride=0)
            lag_cos = jnp.concatenate([c_ref[jj, chunk, repeated]] * (seg_total // 8), axis=0)
            lag_sin = jnp.concatenate([s_ref[jj, chunk, repeated]] * (seg_total // 8), axis=0)
            rows = slice(lag * seg_total, (lag + 1) * seg_total)
            rows_ref[jj, rows, lanes] = (real * lag_cos - imag * lag_sin).astype(jnp.bfloat16)
            rows = slice(half + lag * seg_total, half + (lag + 1) * seg_total)
            rows_ref[jj, rows, lanes] = (real * lag_sin + imag * lag_cos).astype(jnp.bfloat16)

    deep = 256
    tiles = [(jj, k) for jj in range(per_quad) for k in range(A // deep)]

    def push(index):
        jj, k = tiles[index]
        for unit in range(2):
            columns = t_ref[jj, unit * tmpl : (unit + 1) * tmpl, k * deep : (k + 1) * deep]
            pltpu.matmul_push_rhs(columns, index % 2, unit, transpose=True)

    def one_group(next_ref, now_ref):
        def scoped(*sums):
            push(0)
            for index, (jj, k) in enumerate(tiles):
                if index + 1 < len(tiles):
                    push(index + 1)
                chunks = list(range(k * deep // 128, (k + 1) * deep // 128))
                for part in range(2):
                    rows = now_ref[jj, part * half : (part + 1) * half, k * deep : (k + 1) * deep]
                    for unit in range(2):
                        staged = index % 2 if part == 0 else None
                        pltpu.matmul_acc_lhs(sums[unit * 2 + part], rows, load_staged_rhs=staged)
                    if next_ref is not None:
                        make_rows(next_ref, jj, chunks[part])
            for unit in range(2):
                for part in range(2):
                    here = slice(part * half, (part + 1) * half)
                    acc_ref[unit, here] += pltpu.matmul_pop(sums[unit * 2 + part])

        shape = (half, tmpl)
        pl.run_scoped(scoped, *[pltpu.ACC(unit)(shape, jnp.float32) for unit in (0, 0, 1, 1)])

    @pl.when(step == 0)
    def _():
        acc_ref[...] = jnp.zeros_like(acc_ref)

        @pl.loop(0, per_quad)
        def _(jj):
            for chunk in range(A // 128):
                make_rows(even_ref, jj, chunk)

    @pl.when((step % 2 == 1) & (step < last))
    def _():
        one_group(odd_ref, even_ref)

    @pl.when((step % 2 == 0) & (step > 0) & (step < last))
    def _():
        one_group(even_ref, odd_ref)

    @pl.when(step == last)
    def _():
        one_group(None, odd_ref)
        by_real = acc_ref[0]
        by_imag = acc_ref[1]
        shape = (lag_total, seg_total, tmpl)
        real = by_real[:half] + by_imag[half:]
        imag = by_real[half:] - by_imag[:half]
        real = jnp.swapaxes(real.reshape(shape), 0, 1)
        imag = jnp.swapaxes(imag.reshape(shape), 0, 1)
        for index in range(len(sources)):
            here = slice(index * segs, (index + 1) * segs)
            place = pl.ds((place_ref[0] ^ index) * segs, segs)
            out_ref[place, :lag_total] = real[here]
            out_ref[place, lag_total:] = imag[here]


def lag_products(sources, place, laid, lag_cos, lag_sin):
    blocks, rows, _ = sources[0].shape
    tmpl2 = laid.shape[1]
    per_quad = min(4, blocks)
    quads = blocks // per_quad
    _, chunks, lag_total, lanes = lag_cos.shape
    segs = len(sources) * rows // 2

    def ahead(i):
        return (jnp.minimum(i, quads - 1), 0, 0)

    def ahead_lags(i):
        return (jnp.minimum(i, quads - 1), 0, 0, 0)

    return pl.pallas_call(
        lag_kernel,
        grid=(quads + 1,),
        in_specs=[pl.BlockSpec(memory_space=pltpu.SMEM)]
        + [pl.BlockSpec((per_quad, rows, A), ahead)] * len(sources)
        + [
            pl.BlockSpec((per_quad, tmpl2, A), lambda i: (jnp.maximum(i - 1, 0), 0, 0)),
            pl.BlockSpec((per_quad, chunks, lag_total, lanes), ahead_lags),
            pl.BlockSpec((per_quad, chunks, lag_total, lanes), ahead_lags),
        ],
        out_specs=pl.BlockSpec((segs, 2 * lag_total, tmpl2 // 2), lambda i: (0, 0, 0)),
        out_shape=jax.ShapeDtypeStruct((segs, 2 * lag_total, tmpl2 // 2), jnp.float32),
        scratch_shapes=[
            pltpu.VMEM((2, 2 * segs * lag_total, tmpl2 // 2), jnp.float32),
            pltpu.VMEM((per_quad, 2 * segs * lag_total, A), jnp.bfloat16),
            pltpu.VMEM((per_quad, 2 * segs * lag_total, A), jnp.bfloat16),
        ],
        compiler_params=pltpu.CompilerParams(vmem_limit_bytes=60 * 2**20),
        cost_estimate=pl.CostEstimate(
            flops=4 * segs * lag_total * tmpl2 * blocks * A,
            bytes_accessed=blocks * A * (tmpl2 * 2 + segs * 4),
            transcendentals=0,
        ),
        name="lag_products",
    )(place, *sources, laid, lag_cos, lag_sin)


def block_rows(data):
    segs, parts, blocks, _ = data.shape
    return data.transpose(2, 1, 0, 3).reshape(blocks, parts * segs, A)


def spread(data):
    moved = [lax.ppermute(data, "tmpl", [(n, n ^ bit) for n in range(4)]) for bit in (1, 2, 3)]
    return (data, *moved)


def layout_kernel(cut_ref, t_ref, *refs):
    out_ref = refs[-1]
    tmpl, _, rows, _ = t_ref.shape
    first_row = pl.program_id(0) * rows + cut_ref[cut_ref.shape[0] - 1]
    first_tmpl = pl.program_id(1) * tmpl
    row_ids = lax.broadcasted_iota(jnp.int32, (rows, 128), 0) + first_row
    batch = 16

    @pl.loop(0, tmpl // batch)
    def _(group):
        some = pl.ds(pl.multiple_of(group * batch, batch), batch)
        keeps = [row_ids < cut_ref[first_tmpl + group * batch + n] for n in range(batch)]
        for part in range(2):
            for chunk in range(A // 128):
                lanes = slice(chunk * 128, (chunk + 1) * 128)
                value = t_ref[some, part, :, lanes].astype(jnp.float32)
                value = jnp.stack([jnp.where(keeps[n], value[n], 0.0) for n in range(batch)], axis=0)
                value = jnp.swapaxes(value, 0, 1).astype(jnp.bfloat16)
                for row in range(rows):
                    out_ref[row, part, some, lanes] = value[row]


def lay_out(templates, cuts, piece, pieces, laid):
    tmpl, _, blocks, _ = templates.shape
    rows = min(16, blocks)
    steps = blocks // rows // pieces
    batch = min(64, tmpl)
    shape = (blocks, 2, tmpl, A)
    first = piece * steps
    info = jnp.concatenate([cuts, jnp.full((1,), first * rows, jnp.int32)])
    earlier = () if laid is None else (laid,)
    return pl.pallas_call(
        layout_kernel,
        grid=(steps, tmpl // batch),
        in_specs=[
            pl.BlockSpec(memory_space=pltpu.SMEM),
            pl.BlockSpec((batch, 2, rows, A), lambda i, j: (j, 0, i + first, 0)),
        ]
        + [pl.BlockSpec(memory_space=pl.ANY)] * len(earlier),
        out_specs=pl.BlockSpec((rows, 2, batch, A), lambda i, j: (i + first, 0, j, 0)),
        out_shape=jax.ShapeDtypeStruct(shape, jnp.bfloat16),
        input_output_aliases={2: 0} if earlier else {},
        compiler_params=pltpu.CompilerParams(vmem_limit_bytes=40 * 2**20),
        cost_estimate=pl.CostEstimate(
            flops=0, bytes_accessed=8 * tmpl * 2 * blocks * A // pieces, transcendentals=0
        ),
        name="lay_out",
    )(info, templates, *earlier)


def general_transform(strain, psd):
    freq_count = lax.axis_size("freq")
    freq_index = lax.axis_index("freq")
    seg_local = strain.shape[0]
    step_time = B // freq_count
    highest = lax.Precision.HIGHEST
    first_cos, first_sin = cos_sin_table(
        jnp.arange(A, dtype=jnp.int32), jnp.arange(A, dtype=jnp.int32), A
    )
    table = jnp.concatenate([first_cos, -first_sin], axis=0)
    time_ids = freq_index * step_time + jnp.arange(step_time, dtype=jnp.int32)
    twist_cos, twist_sin = cos_sin_table(jnp.arange(A, dtype=jnp.int32), time_ids, LEN)
    slab_blocks = strain.reshape(seg_local, A // freq_count, B)
    both_parts = jnp.einsum(
        "kn,snb->skb",
        table,
        lax.all_to_all(slab_blocks, "freq", split_axis=2, concat_axis=1, tiled=True),
        precision=highest,
    )
    real_part = both_parts[:, :A]
    imag_part = both_parts[:, A:]
    second_cos, second_sin = cos_sin_table(
        jnp.arange(B, dtype=jnp.int32), jnp.arange(NB, dtype=jnp.int32), B
    )
    rotation = jnp.concatenate(
        [
            jnp.concatenate([second_cos, -second_sin], axis=1),
            jnp.concatenate([second_sin, second_cos], axis=1),
        ],
        axis=0,
    )
    amplitude = jnp.sqrt(LEN * psd)
    real_in = lax.all_to_all(
        real_part * twist_cos + imag_part * twist_sin, "freq", split_axis=1, concat_axis=2, tiled=True
    )
    imag_in = lax.all_to_all(
        imag_part * twist_cos - real_part * twist_sin, "freq", split_axis=1, concat_axis=2, tiled=True
    )
    joined = jnp.concatenate([real_in, imag_in], axis=2)
    both_out = jnp.einsum("spc,cm->smp", joined, rotation, precision=highest)
    both_out = both_out.reshape(joined.shape[0], 2, NB, joined.shape[1])
    whitened = (both_out / amplitude).astype(jnp.bfloat16)
    return lax.all_to_all(whitened, "freq", split_axis=2, concat_axis=3, tiled=True)


def exchange(sent):
    return lax.all_to_all(sent, "freq", split_axis=0, concat_axis=0, tiled=True)


def pack_strain(strain, freq_count):
    seg_local = strain.shape[0]
    sent = (strain * STRAIN_SCALE).astype(jnp.float16)
    sent = sent.reshape(seg_local, A // freq_count, freq_count, B // freq_count)
    return sent.transpose(2, 0, 1, 3)


def pack_coefs(received, table):
    freq_count, seg_local, _, width = received.shape
    coefs = first_section(received.astype(jnp.float32) * (1.0 / STRAIN_SCALE), table)
    sent = (coefs * COEF_SCALE).astype(jnp.float16)
    return sent.reshape(freq_count, seg_local // freq_count, A, width)


def whiten(received, tables, white, white_far):
    return second_section(received.astype(jnp.float32) * (1.0 / COEF_SCALE), tables, white, white_far)


def on_device(strain, psd, templates, cutoffs, lags):
    freq_count = lax.axis_size("freq")
    freq_index = lax.axis_index("freq")
    seg_local = strain.shape[0]
    tmpl_local = templates.shape[0]
    blocks_here = templates.shape[2]
    first_block = freq_index * blocks_here
    block_ids = first_block + jnp.arange(blocks_here, dtype=jnp.int32)
    cuts = cutoffs - first_block
    tied = lax.optimization_barrier

    block_cos, block_sin = cos_sin_table(block_ids, lags % B, B)
    position = jnp.arange(A, dtype=jnp.int32).reshape(A // 128, 1, 128)
    place = lags[None, :, None] * position % LEN
    place_angle = place.astype(jnp.float32) * (two_pi / LEN)
    place_cos = jnp.cos(place_angle)[None]
    place_sin = jnp.sin(place_angle)[None]
    block_cos = block_cos[:, None, :, None]
    block_sin = block_sin[:, None, :, None]
    lag_cos = block_cos * place_cos - block_sin * place_sin
    lag_sin = block_sin * place_cos + block_cos * place_sin

    sliced = (
        lax.axis_size("tmpl") == 4
        and seg_local == 2 * freq_count == 16
        and (NB // freq_count) % 32 == 0
        and B // freq_count == 128
    )
    if not sliced:
        laid = lay_out(templates, cuts, 0, 1, None)
        laid = laid.reshape(blocks_here, 2 * tmpl_local, A)
        data = lax.all_gather(general_transform(strain, psd), "tmpl", axis=0, tiled=True)
        origin = jnp.zeros((1,), jnp.int32)
        sums = []
        for start in range(0, data.shape[0], 16):
            sources = [block_rows(data[n : n + 4]) for n in range(start, start + 16, 4)]
            sums.append(lag_products(sources, origin, laid, lag_cos, lag_sin))
        sums = jnp.concatenate(sums, axis=0)
        return lax.psum_scatter(sums, "freq", scatter_dimension=0, tiled=True)

    order = mirror_table()
    psd_all = lax.all_gather(psd, "freq", axis=1, tiled=True)
    psd_far = jnp.dot(psd_all[:, HALF:], order.T, precision=lax.Precision.HIGHEST)
    white = lax.rsqrt(LEN * psd_all[:, :HALF])
    white_far = lax.rsqrt(LEN * psd_far)
    first = first_table()
    second = (twist_tables(), second_tables(), order.astype(ml_dtypes.bfloat16))

    seg_out = seg_local * lax.axis_size("tmpl") // freq_count
    by_owner = strain.reshape(seg_local // seg_out, 2, seg_out // 2, strain.shape[1])
    strain_a, strain_b = (
        pack_strain(by_owner[:, group].reshape(seg_local // 2, strain.shape[1]), freq_count)
        for group in range(2)
    )
    time_a = exchange(strain_a)
    laid = lay_out(templates, cuts, 0, 2, None)
    time_a, laid, strain_b = tied((time_a, laid, strain_b))
    coefs_a = pack_coefs(time_a, first)
    parts_a = exchange(coefs_a)
    parts_a, strain_b, white, white_far, lag_cos, lag_sin = tied(
        (parts_a, strain_b, white, white_far, lag_cos, lag_sin)
    )
    time_b = exchange(strain_b)
    white_a = whiten(parts_a, second, white, white_far)
    time_b, white_a = tied((time_b, white_a))
    data_a = exchange(white_a)
    coefs_b = pack_coefs(time_b, first)
    laid = lay_out(templates, cuts, 1, 2, laid)
    data_a, coefs_b, laid = tied((data_a, coefs_b, laid))
    parts_b = exchange(coefs_b)
    laid = laid.reshape(blocks_here, 2 * tmpl_local, A)
    place = lax.axis_index("tmpl").astype(jnp.int32).reshape(1)

    def halves(data):
        data = data.reshape(2, 2, 2, 2, blocks_here, A)
        return [block_rows(data[:, n].reshape(4, 2, blocks_here, A)) for n in range(2)]

    def products(part):
        return lag_products(part, place, laid, lag_cos, lag_sin)

    def collect(sums):
        return lax.psum_scatter(sums, "freq", scatter_dimension=0, tiled=True)

    def collect_late(sums):
        shares = exchange(sums.reshape(freq_count, 2, 2 * lags.shape[0], tmpl_local))
        return jnp.sum(shares, axis=0)

    first_a, second_a = halves(data_a)
    first_a = spread(first_a)
    parts_b, first_a, second_a = tied((parts_b, first_a, second_a))
    second_a = spread(second_a)
    data_b = exchange(whiten(parts_b, second, white, white_far))
    sums_a1 = products(first_a)
    data_b, second_a, sums_a1 = tied((data_b, second_a, sums_a1))
    first_b, second_b = halves(data_b)
    first_b = spread(first_b)
    out_a1 = collect(sums_a1)
    sums_a2 = products(second_a)
    first_b, second_b, sums_a2 = tied((first_b, second_b, sums_a2))
    second_b = spread(second_b)
    out_a2 = collect(sums_a2)
    sums_b1 = products(first_b)
    second_b, sums_b1 = tied((second_b, sums_b1))
    out_b1 = collect(sums_b1)
    sums_b2 = products(second_b)
    out_a1, out_a2, sums_b2 = tied((out_a1, out_a2, sums_b2))
    out_b2 = collect_late(sums_b2)
    return jnp.concatenate([out_a1, out_a2, out_b1, out_b2], axis=0)


def solution(mesh):
    placed = (P("tmpl", "freq"), P(None, "freq"), P("tmpl", None, "freq", None), P("tmpl"), P())
    return jax.shard_map(
        on_device, mesh=mesh, in_specs=placed, out_specs=P("freq", None, "tmpl"), check_vma=False
    )
```

```python
import math

import jax
import jax.numpy as jnp
import ml_dtypes
import numpy as np
from jax import lax
from jax.experimental import pallas as pl
from jax.experimental.pallas import tpu as pltpu
from jax.sharding import PartitionSpec as P

A = 512
B = 1024
LEN = 524288
NB = 512
HALF = A // 2

STRAIN_SCALE = 8192.0
COEF_SCALE = 16.0

two_pi = 2.0 * math.pi


def cos_sin_table(row_ids, col_ids, modulus):
    product = row_ids[:, None] * col_ids[None, :] % modulus
    phase_angle = product.astype(jnp.float32) * (two_pi / modulus)
    return (jnp.cos(phase_angle), jnp.sin(phase_angle))


def split_const(table):
    high = table.astype(ml_dtypes.bfloat16)
    low = (table - high.astype(np.float64)).astype(ml_dtypes.bfloat16)
    return high, low


def first_table():
    angle = two_pi * (np.outer(np.arange(HALF), np.arange(A)) % A) / A
    table = np.concatenate([np.cos(angle), -np.sin(angle)], axis=0)
    table[HALF] = 1.0 - 2.0 * (np.arange(A) % 2)
    return split_const(table)


def second_tables():
    angle = two_pi * (np.outer(np.arange(528), np.arange(B)) % B) / B
    return split_const(np.cos(angle)) + split_const(np.sin(angle))


def twist_tables():
    angle = two_pi * np.outer(np.arange(HALF), np.arange(B)) / LEN
    edge = two_pi * HALF * np.arange(B)[None, :] / LEN
    return (
        np.cos(angle).astype(np.float32),
        np.sin(angle).astype(np.float32),
        np.cos(edge).astype(np.float32),
        np.sin(edge).astype(np.float32),
    )


def mirror_table():
    table = np.zeros((HALF, HALF), np.float32)
    table[0, 0] = 1.0
    table[np.arange(1, HALF), HALF - np.arange(1, HALF)] = 1.0
    return table


def split_parts(value):
    high = value.astype(jnp.bfloat16)
    low = (value - high.astype(jnp.float32)).astype(jnp.bfloat16)
    return high, low


def dot_nn(lhs, rhs):
    return lax.dot_general(lhs, rhs, (((1,), (0,)), ((), ())), preferred_element_type=jnp.float32)


def dot_nt(lhs, rhs):
    return lax.dot_general(lhs, rhs, (((1,), (1,)), ((), ())), preferred_element_type=jnp.float32)


def first_kernel(x_ref, high_ref, low_ref, out_ref):
    parts = x_ref.shape[0]
    pair = x_ref.shape[1]
    columns = []
    for s in range(pair):
        columns.append(jnp.concatenate([x_ref[f, s] for f in range(parts)], axis=0))
    value = jnp.concatenate(columns, axis=1)
    high, low = split_parts(value)
    result = dot_nn(high_ref[...], high) + dot_nn(high_ref[...], low) + dot_nn(low_ref[...], high)
    width = x_ref.shape[3]
    for s in range(pair):
        out_ref[s] = result[:, s * width : (s + 1) * width]


def first_section(received, tables):
    parts, segs, rows, width = received.shape
    pair = 2
    return pl.pallas_call(
        first_kernel,
        grid=(segs // pair,),
        in_specs=[
            pl.BlockSpec((parts, pair, rows, width), lambda i: (0, i, 0, 0)),
            pl.BlockSpec((A, A), lambda i: (0, 0)),
            pl.BlockSpec((A, A), lambda i: (0, 0)),
        ],
        out_specs=pl.BlockSpec((pair, A, width), lambda i: (i, 0, 0)),
        out_shape=jax.ShapeDtypeStruct((segs, A, width), jnp.float32),
        compiler_params=pltpu.CompilerParams(vmem_limit_bytes=40 * 2**20),
        cost_estimate=pl.CostEstimate(
            flops=2 * 3 * segs * A * A * width, bytes_accessed=segs * A * width * 8, transcendentals=0
        ),
        name="first_section",
    )(received, *tables)


def second_kernel(
    y_ref, tc_ref, ts_ref, ec_ref, es_ref, ch_ref, cl_ref, sh_ref, sl_ref, wa_ref, wm_ref, q_ref, out_ref
):
    parts = y_ref.shape[0]
    joined = jnp.concatenate([y_ref[f, 0] for f in range(parts)], axis=1)
    real_raw = joined[:HALF]
    imag_raw = joined[HALF:]
    row_ids = lax.broadcasted_iota(jnp.int32, (HALF, B), 0)
    imag_in = jnp.where(row_ids == 0, 0.0, imag_raw)
    twist_cos = tc_ref[...]
    twist_sin = ts_ref[...]
    real_u = real_raw * twist_cos + imag_in * twist_sin
    imag_u = imag_in * twist_cos - real_raw * twist_sin
    edge = imag_raw[0:1]
    edge_rows = jnp.where(
        lax.broadcasted_iota(jnp.int32, (16, B), 0) == 0,
        edge * ec_ref[...],
        jnp.where(lax.broadcasted_iota(jnp.int32, (16, B), 0) == 1, -edge * es_ref[...], 0.0),
    )
    u_high, u_low = split_parts(jnp.concatenate([real_u, imag_u], axis=0))
    e_high, e_low = split_parts(edge_rows)

    def three(high_ref, low_ref, high, low):
        return (
            dot_nt(high_ref[...], high) + dot_nt(high_ref[...], low) + dot_nt(low_ref[...], high)
        )

    by_cos = three(ch_ref, cl_ref, u_high, u_low)
    by_sin = three(sh_ref, sl_ref, u_high, u_low)
    edge_cos = three(ch_ref, cl_ref, e_high, e_low)[:NB]
    edge_sin = three(sh_ref, sl_ref, e_high, e_low)[:NB]
    white = wa_ref[...]
    real_out = ((by_cos[:NB, :HALF] + by_sin[:NB, HALF:]) * white).astype(jnp.bfloat16)
    imag_out = ((by_cos[:NB, HALF:] - by_sin[:NB, :HALF]) * white).astype(jnp.bfloat16)
    next_cos = by_cos[1 : NB + 1]
    next_sin = by_sin[1 : NB + 1]
    lane = lax.broadcasted_iota(jnp.int32, (NB, HALF), 1)
    real_edge = edge_cos[:, 0:1] + edge_sin[:, 1:2]
    imag_edge = edge_cos[:, 1:2] - edge_sin[:, 0:1]
    real_far = jnp.where(lane == 0, real_edge, next_cos[:, :HALF] - next_sin[:, HALF:])
    imag_far = jnp.where(lane == 0, imag_edge, -next_cos[:, HALF:] - next_sin[:, :HALF])
    white_far = wm_ref[...]
    order = q_ref[...]
    real_far = dot_nn((real_far * white_far).astype(jnp.bfloat16), order).astype(jnp.bfloat16)
    imag_far = dot_nn((imag_far * white_far).astype(jnp.bfloat16), order).astype(jnp.bfloat16)
    rows = NB // parts
    for f in range(parts):
        here = slice(f * rows, (f + 1) * rows)
        out_ref[f, 0, 0, :, :HALF] = real_out[here]
        out_ref[f, 0, 0, :, HALF:] = real_far[here]
        out_ref[f, 0, 1, :, :HALF] = imag_out[here]
        out_ref[f, 0, 1, :, HALF:] = imag_far[here]


def second_section(received, tables, white, white_far):
    parts, segs, rows, width = received.shape
    twists, seconds, order = tables

    def whole(array):
        return pl.BlockSpec(array.shape, lambda i: (0,) * array.ndim)

    fixed = (*twists, *seconds, white, white_far, order)
    return pl.pallas_call(
        second_kernel,
        grid=(segs,),
        in_specs=[pl.BlockSpec((parts, 1, rows, width), lambda i: (0, i, 0, 0))]
        + [whole(array) for array in fixed],
        out_specs=pl.BlockSpec((parts, 1, 2, NB // parts, A), lambda i: (0, i, 0, 0, 0)),
        out_shape=jax.ShapeDtypeStruct((parts, segs, 2, NB // parts, A), jnp.bfloat16),
        compiler_params=pltpu.CompilerParams(vmem_limit_bytes=60 * 2**20),
        cost_estimate=pl.CostEstimate(
            flops=2 * 6 * segs * 528 * B * A, bytes_accessed=segs * A * B * 6, transcendentals=0
        ),
        name="second_section",
    )(received, *fixed)


def lag_kernel(place_ref, a_ref, b_ref, x_ref, y_ref, t_ref, c_ref, s_ref, out_ref, acc_ref, even_ref, odd_ref):
    sources = (a_ref, b_ref, x_ref, y_ref)
    segs = a_ref.shape[1] // 2
    per_quad = t_ref.shape[0]
    lag_total = c_ref.shape[2]
    tmpl = out_ref.shape[2]
    step = pl.program_id(0)
    last = pl.num_programs(0) - 1
    seg_total = len(sources) * segs
    half = seg_total * lag_total

    def make_rows(rows_ref, jj, chunk):
        lanes = slice(chunk * 128, (chunk + 1) * 128)
        values = [source[jj, :, lanes].astype(jnp.float32) for source in sources]
        real = jnp.concatenate([value[:segs] for value in values], axis=0)
        imag = jnp.concatenate([value[segs:] for value in values], axis=0)
        batch = min(8, lag_total)
        for first in range(0, lag_total, batch):
            lags_here = range(first, first + batch)
            repeated = [pl.ds(lag, 8, stride=0) for lag in lags_here]
            factors = [(c_ref[jj, chunk, lag], s_ref[jj, chunk, lag]) for lag in repeated]
            made = []
            for once_cos, once_sin in factors:
                lag_cos = jnp.concatenate([once_cos] * (seg_total // 8), axis=0)
                lag_sin = jnp.concatenate([once_sin] * (seg_total // 8), axis=0)
                real_q = (real * lag_cos - imag * lag_sin).astype(jnp.bfloat16)
                imag_q = (real * lag_sin + imag * lag_cos).astype(jnp.bfloat16)
                made.append((real_q, imag_q))
            for lag, (real_q, imag_q) in zip(lags_here, made):
                start = lag * seg_total
                rows_ref[jj, start : start + seg_total, lanes] = real_q
                rows_ref[jj, half + start : half + start + seg_total, lanes] = imag_q

    deep = 256
    tiles = [(jj, k) for jj in range(per_quad) for k in range(A // deep)]

    def push(index):
        jj, k = tiles[index]
        for unit in range(2):
            columns = t_ref[jj, unit * tmpl : (unit + 1) * tmpl, k * deep : (k + 1) * deep]
            pltpu.matmul_push_rhs(columns, index % 2, unit, transpose=True)

    def one_group(next_ref, now_ref):
        def scoped(*sums):
            push(0)
            for index, (jj, k) in enumerate(tiles):
                if index + 1 < len(tiles):
                    push(index + 1)
                chunks = list(range(k * deep // 128, (k + 1) * deep // 128))
                for part in range(2):
                    rows = now_ref[jj, part * half : (part + 1) * half, k * deep : (k + 1) * deep]
                    for unit in range(2):
                        staged = index % 2 if part == 0 else None
                        pltpu.matmul_acc_lhs(sums[unit * 2 + part], rows, load_staged_rhs=staged)
                    if next_ref is not None:
                        make_rows(next_ref, jj, chunks[part])
            for unit in range(2):
                for part in range(2):
                    here = slice(part * half, (part + 1) * half)
                    acc_ref[unit, here] += pltpu.matmul_pop(sums[unit * 2 + part])

        shape = (half, tmpl)
        pl.run_scoped(scoped, *[pltpu.ACC(unit)(shape, jnp.float32) for unit in (0, 0, 1, 1)])

    @pl.when(step == 0)
    def _():
        acc_ref[...] = jnp.zeros_like(acc_ref)

        @pl.loop(0, per_quad)
        def _(jj):
            for chunk in range(A // 128):
                make_rows(even_ref, jj, chunk)

    @pl.when((step % 2 == 1) & (step < last))
    def _():
        one_group(odd_ref, even_ref)

    @pl.when((step % 2 == 0) & (step > 0) & (step < last))
    def _():
        one_group(even_ref, odd_ref)

    @pl.when(step == last)
    def _():
        one_group(None, odd_ref)
        by_real = acc_ref[0]
        by_imag = acc_ref[1]
        shape = (lag_total, seg_total, tmpl)
        real = by_real[:half] + by_imag[half:]
        imag = by_real[half:] - by_imag[:half]
        real = jnp.swapaxes(real.reshape(shape), 0, 1)
        imag = jnp.swapaxes(imag.reshape(shape), 0, 1)
        for index in range(len(sources)):
            here = slice(index * segs, (index + 1) * segs)
            place = pl.ds((place_ref[0] ^ index) * segs, segs)
            out_ref[place, :lag_total] = real[here]
            out_ref[place, lag_total:] = imag[here]


def lag_products(sources, place, laid, lag_cos, lag_sin):
    blocks, rows, _ = sources[0].shape
    tmpl2 = laid.shape[1]
    per_quad = min(4, blocks)
    quads = blocks // per_quad
    _, chunks, lag_total, lanes = lag_cos.shape
    segs = len(sources) * rows // 2

    def ahead(i):
        return (jnp.minimum(i, quads - 1), 0, 0)

    def ahead_lags(i):
        return (jnp.minimum(i, quads - 1), 0, 0, 0)

    return pl.pallas_call(
        lag_kernel,
        grid=(quads + 1,),
        in_specs=[pl.BlockSpec(memory_space=pltpu.SMEM)]
        + [pl.BlockSpec((per_quad, rows, A), ahead)] * len(sources)
        + [
            pl.BlockSpec((per_quad, tmpl2, A), lambda i: (jnp.maximum(i - 1, 0), 0, 0)),
            pl.BlockSpec((per_quad, chunks, lag_total, lanes), ahead_lags),
            pl.BlockSpec((per_quad, chunks, lag_total, lanes), ahead_lags),
        ],
        out_specs=pl.BlockSpec((segs, 2 * lag_total, tmpl2 // 2), lambda i: (0, 0, 0)),
        out_shape=jax.ShapeDtypeStruct((segs, 2 * lag_total, tmpl2 // 2), jnp.float32),
        scratch_shapes=[
            pltpu.VMEM((2, 2 * segs * lag_total, tmpl2 // 2), jnp.float32),
            pltpu.VMEM((per_quad, 2 * segs * lag_total, A), jnp.bfloat16),
            pltpu.VMEM((per_quad, 2 * segs * lag_total, A), jnp.bfloat16),
        ],
        compiler_params=pltpu.CompilerParams(vmem_limit_bytes=60 * 2**20),
        cost_estimate=pl.CostEstimate(
            flops=4 * segs * lag_total * tmpl2 * blocks * A,
            bytes_accessed=blocks * A * (tmpl2 * 2 + segs * 4),
            transcendentals=0,
        ),
        name="lag_products",
    )(place, *sources, laid, lag_cos, lag_sin)


def block_rows(data):
    segs, parts, blocks, _ = data.shape
    return data.transpose(2, 1, 0, 3).reshape(blocks, parts * segs, A)


def spread(data):
    moved = [lax.ppermute(data, "tmpl", [(n, n ^ bit) for n in range(4)]) for bit in (1, 2, 3)]
    return (data, *moved)


def layout_kernel(cut_ref, t_ref, *refs):
    out_ref = refs[-1]
    tmpl, _, rows, _ = t_ref.shape
    first_row = pl.program_id(0) * rows + cut_ref[cut_ref.shape[0] - 1]
    first_tmpl = pl.program_id(1) * tmpl
    row_ids = lax.broadcasted_iota(jnp.int32, (rows, 128), 0) + first_row
    batch = 16

    @pl.loop(0, tmpl // batch)
    def _(group):
        some = pl.ds(pl.multiple_of(group * batch, batch), batch)
        keeps = [row_ids < cut_ref[first_tmpl + group * batch + n] for n in range(batch)]
        for part in range(2):
            for chunk in range(A // 128):
                lanes = slice(chunk * 128, (chunk + 1) * 128)
                value = t_ref[some, part, :, lanes].astype(jnp.float32)
                value = jnp.stack([jnp.where(keeps[n], value[n], 0.0) for n in range(batch)], axis=0)
                value = jnp.swapaxes(value, 0, 1).astype(jnp.bfloat16)
                for row in range(rows):
                    out_ref[row, part, some, lanes] = value[row]


def lay_out(templates, cuts, piece, pieces, laid):
    tmpl, _, blocks, _ = templates.shape
    rows = min(16, blocks)
    steps = blocks // rows // pieces
    batch = min(64, tmpl)
    shape = (blocks, 2, tmpl, A)
    first = piece * steps
    info = jnp.concatenate([cuts, jnp.full((1,), first * rows, jnp.int32)])
    earlier = () if laid is None else (laid,)
    return pl.pallas_call(
        layout_kernel,
        grid=(steps, tmpl // batch),
        in_specs=[
            pl.BlockSpec(memory_space=pltpu.SMEM),
            pl.BlockSpec((batch, 2, rows, A), lambda i, j: (j, 0, i + first, 0)),
        ]
        + [pl.BlockSpec(memory_space=pl.ANY)] * len(earlier),
        out_specs=pl.BlockSpec((rows, 2, batch, A), lambda i, j: (i + first, 0, j, 0)),
        out_shape=jax.ShapeDtypeStruct(shape, jnp.bfloat16),
        input_output_aliases={2: 0} if earlier else {},
        compiler_params=pltpu.CompilerParams(vmem_limit_bytes=40 * 2**20),
        cost_estimate=pl.CostEstimate(
            flops=0, bytes_accessed=8 * tmpl * 2 * blocks * A // pieces, transcendentals=0
        ),
        name="lay_out",
    )(info, templates, *earlier)


def general_transform(strain, psd):
    freq_count = lax.axis_size("freq")
    freq_index = lax.axis_index("freq")
    seg_local = strain.shape[0]
    step_time = B // freq_count
    highest = lax.Precision.HIGHEST
    first_cos, first_sin = cos_sin_table(
        jnp.arange(A, dtype=jnp.int32), jnp.arange(A, dtype=jnp.int32), A
    )
    table = jnp.concatenate([first_cos, -first_sin], axis=0)
    time_ids = freq_index * step_time + jnp.arange(step_time, dtype=jnp.int32)
    twist_cos, twist_sin = cos_sin_table(jnp.arange(A, dtype=jnp.int32), time_ids, LEN)
    slab_blocks = strain.reshape(seg_local, A // freq_count, B)
    both_parts = jnp.einsum(
        "kn,snb->skb",
        table,
        lax.all_to_all(slab_blocks, "freq", split_axis=2, concat_axis=1, tiled=True),
        precision=highest,
    )
    real_part = both_parts[:, :A]
    imag_part = both_parts[:, A:]
    second_cos, second_sin = cos_sin_table(
        jnp.arange(B, dtype=jnp.int32), jnp.arange(NB, dtype=jnp.int32), B
    )
    rotation = jnp.concatenate(
        [
            jnp.concatenate([second_cos, -second_sin], axis=1),
            jnp.concatenate([second_sin, second_cos], axis=1),
        ],
        axis=0,
    )
    amplitude = jnp.sqrt(LEN * psd)
    real_in = lax.all_to_all(
        real_part * twist_cos + imag_part * twist_sin, "freq", split_axis=1, concat_axis=2, tiled=True
    )
    imag_in = lax.all_to_all(
        imag_part * twist_cos - real_part * twist_sin, "freq", split_axis=1, concat_axis=2, tiled=True
    )
    joined = jnp.concatenate([real_in, imag_in], axis=2)
    both_out = jnp.einsum("spc,cm->smp", joined, rotation, precision=highest)
    both_out = both_out.reshape(joined.shape[0], 2, NB, joined.shape[1])
    whitened = (both_out / amplitude).astype(jnp.bfloat16)
    return lax.all_to_all(whitened, "freq", split_axis=2, concat_axis=3, tiled=True)


def exchange(sent):
    return lax.all_to_all(sent, "freq", split_axis=0, concat_axis=0, tiled=True)


def pack_strain(strain, freq_count):
    seg_local = strain.shape[0]
    sent = (strain * STRAIN_SCALE).astype(jnp.float16)
    sent = sent.reshape(seg_local, A // freq_count, freq_count, B // freq_count)
    return sent.transpose(2, 0, 1, 3)


def pack_coefs(received, table):
    freq_count, seg_local, _, width = received.shape
    coefs = first_section(received.astype(jnp.float32) * (1.0 / STRAIN_SCALE), table)
    sent = (coefs * COEF_SCALE).astype(jnp.float16)
    return sent.reshape(freq_count, seg_local // freq_count, A, width)


def whiten(received, tables, white, white_far):
    return second_section(received.astype(jnp.float32) * (1.0 / COEF_SCALE), tables, white, white_far)


def on_device(strain, psd, templates, cutoffs, lags):
    freq_count = lax.axis_size("freq")
    freq_index = lax.axis_index("freq")
    seg_local = strain.shape[0]
    tmpl_local = templates.shape[0]
    blocks_here = templates.shape[2]
    first_block = freq_index * blocks_here
    block_ids = first_block + jnp.arange(blocks_here, dtype=jnp.int32)
    cuts = cutoffs - first_block
    tied = lax.optimization_barrier

    block_cos, block_sin = cos_sin_table(block_ids, lags % B, B)
    position = jnp.arange(A, dtype=jnp.int32).reshape(A // 128, 1, 128)
    place = lags[None, :, None] * position % LEN
    place_angle = place.astype(jnp.float32) * (two_pi / LEN)
    place_cos = jnp.cos(place_angle)[None]
    place_sin = jnp.sin(place_angle)[None]
    block_cos = block_cos[:, None, :, None]
    block_sin = block_sin[:, None, :, None]
    lag_cos = block_cos * place_cos - block_sin * place_sin
    lag_sin = block_sin * place_cos + block_cos * place_sin

    sliced = (
        lax.axis_size("tmpl") == 4
        and seg_local == 2 * freq_count == 16
        and (NB // freq_count) % 32 == 0
        and B // freq_count == 128
    )
    if not sliced:
        laid = lay_out(templates, cuts, 0, 1, None)
        laid = laid.reshape(blocks_here, 2 * tmpl_local, A)
        data = lax.all_gather(general_transform(strain, psd), "tmpl", axis=0, tiled=True)
        origin = jnp.zeros((1,), jnp.int32)
        sums = []
        for start in range(0, data.shape[0], 16):
            sources = [block_rows(data[n : n + 4]) for n in range(start, start + 16, 4)]
            sums.append(lag_products(sources, origin, laid, lag_cos, lag_sin))
        sums = jnp.concatenate(sums, axis=0)
        return lax.psum_scatter(sums, "freq", scatter_dimension=0, tiled=True)

    order = mirror_table()
    psd_all = lax.all_gather(psd, "freq", axis=1, tiled=True)
    psd_far = jnp.dot(psd_all[:, HALF:], order.T, precision=lax.Precision.HIGHEST)
    white = lax.rsqrt(LEN * psd_all[:, :HALF])
    white_far = lax.rsqrt(LEN * psd_far)
    first = first_table()
    second = (twist_tables(), second_tables(), order.astype(ml_dtypes.bfloat16))

    seg_out = seg_local * lax.axis_size("tmpl") // freq_count
    by_owner = strain.reshape(seg_local // seg_out, 2, seg_out // 2, strain.shape[1])
    strain_a, strain_b = (
        pack_strain(by_owner[:, group].reshape(seg_local // 2, strain.shape[1]), freq_count)
        for group in range(2)
    )
    time_a = exchange(strain_a)
    laid = lay_out(templates, cuts, 0, 2, None)
    time_a, laid, strain_b = tied((time_a, laid, strain_b))
    coefs_a = pack_coefs(time_a, first)
    parts_a = exchange(coefs_a)
    parts_a, strain_b, white, white_far, lag_cos, lag_sin = tied(
        (parts_a, strain_b, white, white_far, lag_cos, lag_sin)
    )
    time_b = exchange(strain_b)
    white_a = whiten(parts_a, second, white, white_far)
    time_b, white_a = tied((time_b, white_a))
    data_a = exchange(white_a)
    coefs_b = pack_coefs(time_b, first)
    laid = lay_out(templates, cuts, 1, 2, laid)
    data_a, coefs_b, laid = tied((data_a, coefs_b, laid))
    parts_b = exchange(coefs_b)
    laid = laid.reshape(blocks_here, 2 * tmpl_local, A)
    place = lax.axis_index("tmpl").astype(jnp.int32).reshape(1)

    def halves(data):
        data = data.reshape(2, 2, 2, 2, blocks_here, A)
        return [block_rows(data[:, n].reshape(4, 2, blocks_here, A)) for n in range(2)]

    def products(part):
        return lag_products(part, place, laid, lag_cos, lag_sin)

    def collect(sums):
        return lax.psum_scatter(sums, "freq", scatter_dimension=0, tiled=True)

    def collect_late(sums):
        shares = exchange(sums.reshape(freq_count, 2, 2 * lags.shape[0], tmpl_local))
        return jnp.sum(shares, axis=0)

    first_a, second_a = halves(data_a)
    first_a = spread(first_a)
    parts_b, first_a, second_a = tied((parts_b, first_a, second_a))
    second_a = spread(second_a)
    data_b = exchange(whiten(parts_b, second, white, white_far))
    sums_a1 = products(first_a)
    data_b, second_a, sums_a1 = tied((data_b, second_a, sums_a1))
    first_b, second_b = halves(data_b)
    first_b = spread(first_b)
    out_a1 = collect(sums_a1)
    sums_a2 = products(second_a)
    first_b, second_b, sums_a2 = tied((first_b, second_b, sums_a2))
    second_b = spread(second_b)
    out_a2 = collect(sums_a2)
    sums_b1 = products(first_b)
    second_b, sums_b1 = tied((second_b, sums_b1))
    out_b1 = collect(sums_b1)
    sums_b2 = products(second_b)
    out_a1, out_a2, sums_b2 = tied((out_a1, out_a2, sums_b2))
    out_b2 = collect_late(sums_b2)
    return jnp.concatenate([out_a1, out_a2, out_b1, out_b2], axis=0)


def solution(mesh):
    placed = (P("tmpl", "freq"), P(None, "freq"), P("tmpl", None, "freq", None), P("tmpl"), P())
    return jax.shard_map(
        on_device, mesh=mesh, in_specs=placed, out_specs=P("freq", None, "tmpl"), check_vma=False
    )
```

```python
import math

import jax
import jax.numpy as jnp
import ml_dtypes
import numpy as np
from jax import lax
from jax.experimental import pallas as pl
from jax.experimental.pallas import tpu as pltpu
from jax.sharding import PartitionSpec as P

A = 512
B = 1024
LEN = 524288
NB = 512
HALF = A // 2

STRAIN_SCALE = 8192.0
COEF_SCALE = 16.0

two_pi = 2.0 * math.pi


def cos_sin_table(row_ids, col_ids, modulus):
    product = row_ids[:, None] * col_ids[None, :] % modulus
    phase_angle = product.astype(jnp.float32) * (two_pi / modulus)
    return (jnp.cos(phase_angle), jnp.sin(phase_angle))


def split_const(table):
    high = table.astype(ml_dtypes.bfloat16)
    low = (table - high.astype(np.float64)).astype(ml_dtypes.bfloat16)
    return high, low


def first_table():
    angle = two_pi * (np.outer(np.arange(HALF), np.arange(A)) % A) / A
    table = np.concatenate([np.cos(angle), -np.sin(angle)], axis=0)
    table[HALF] = 1.0 - 2.0 * (np.arange(A) % 2)
    return split_const(table)


def second_tables():
    angle = two_pi * (np.outer(np.arange(528), np.arange(B)) % B) / B
    return split_const(np.cos(angle)) + split_const(np.sin(angle))


def twist_tables():
    angle = two_pi * np.outer(np.arange(HALF), np.arange(B)) / LEN
    edge = two_pi * HALF * np.arange(B)[None, :] / LEN
    return (
        np.cos(angle).astype(np.float32),
        np.sin(angle).astype(np.float32),
        np.cos(edge).astype(np.float32),
        np.sin(edge).astype(np.float32),
    )


def mirror_table():
    table = np.zeros((HALF, HALF), np.float32)
    table[0, 0] = 1.0
    table[np.arange(1, HALF), HALF - np.arange(1, HALF)] = 1.0
    return table


def split_parts(value):
    high = value.astype(jnp.bfloat16)
    low = (value - high.astype(jnp.float32)).astype(jnp.bfloat16)
    return high, low


def dot_nn(lhs, rhs):
    return lax.dot_general(lhs, rhs, (((1,), (0,)), ((), ())), preferred_element_type=jnp.float32)


def dot_nt(lhs, rhs):
    return lax.dot_general(lhs, rhs, (((1,), (1,)), ((), ())), preferred_element_type=jnp.float32)


def first_kernel(x_ref, high_ref, low_ref, out_ref):
    parts = x_ref.shape[0]
    pair = x_ref.shape[1]
    columns = []
    for s in range(pair):
        columns.append(jnp.concatenate([x_ref[f, s] for f in range(parts)], axis=0))
    value = jnp.concatenate(columns, axis=1)
    high, low = split_parts(value)
    result = dot_nn(high_ref[...], high) + dot_nn(high_ref[...], low) + dot_nn(low_ref[...], high)
    width = x_ref.shape[3]
    for s in range(pair):
        out_ref[s] = result[:, s * width : (s + 1) * width]


def first_section(received, tables):
    parts, segs, rows, width = received.shape
    pair = 2
    return pl.pallas_call(
        first_kernel,
        grid=(segs // pair,),
        in_specs=[
            pl.BlockSpec((parts, pair, rows, width), lambda i: (0, i, 0, 0)),
            pl.BlockSpec((A, A), lambda i: (0, 0)),
            pl.BlockSpec((A, A), lambda i: (0, 0)),
        ],
        out_specs=pl.BlockSpec((pair, A, width), lambda i: (i, 0, 0)),
        out_shape=jax.ShapeDtypeStruct((segs, A, width), jnp.float32),
        compiler_params=pltpu.CompilerParams(vmem_limit_bytes=40 * 2**20),
        cost_estimate=pl.CostEstimate(
            flops=2 * 3 * segs * A * A * width, bytes_accessed=segs * A * width * 8, transcendentals=0
        ),
        name="first_section",
    )(received, *tables)


def second_kernel(
    y_ref, tc_ref, ts_ref, ec_ref, es_ref, ch_ref, cl_ref, sh_ref, sl_ref, wa_ref, wm_ref, q_ref, out_ref
):
    parts = y_ref.shape[0]
    joined = jnp.concatenate([y_ref[f, 0] for f in range(parts)], axis=1)
    real_raw = joined[:HALF]
    imag_raw = joined[HALF:]
    row_ids = lax.broadcasted_iota(jnp.int32, (HALF, B), 0)
    imag_in = jnp.where(row_ids == 0, 0.0, imag_raw)
    twist_cos = tc_ref[...]
    twist_sin = ts_ref[...]
    real_u = real_raw * twist_cos + imag_in * twist_sin
    imag_u = imag_in * twist_cos - real_raw * twist_sin
    edge = imag_raw[0:1]
    edge_rows = jnp.where(
        lax.broadcasted_iota(jnp.int32, (16, B), 0) == 0,
        edge * ec_ref[...],
        jnp.where(lax.broadcasted_iota(jnp.int32, (16, B), 0) == 1, -edge * es_ref[...], 0.0),
    )
    u_high, u_low = split_parts(jnp.concatenate([real_u, imag_u], axis=0))
    e_high, e_low = split_parts(edge_rows)

    def three(high_ref, low_ref, high, low):
        return (
            dot_nt(high_ref[...], high) + dot_nt(high_ref[...], low) + dot_nt(low_ref[...], high)
        )

    by_cos = three(ch_ref, cl_ref, u_high, u_low)
    by_sin = three(sh_ref, sl_ref, u_high, u_low)
    e_both = jnp.concatenate([e_high, e_low], axis=0)

    def edge(high_ref, low_ref):
        both = dot_nt(high_ref[:NB], e_both)
        small = dot_nt(low_ref[:NB], e_high)
        return [both[:, n : n + 1] + both[:, 16 + n : 17 + n] + small[:, n : n + 1] for n in range(2)]

    edge_cos = edge(ch_ref, cl_ref)
    edge_sin = edge(sh_ref, sl_ref)
    white = wa_ref[...]
    real_out = ((by_cos[:NB, :HALF] + by_sin[:NB, HALF:]) * white).astype(jnp.bfloat16)
    imag_out = ((by_cos[:NB, HALF:] - by_sin[:NB, :HALF]) * white).astype(jnp.bfloat16)
    next_cos = by_cos[1 : NB + 1]
    next_sin = by_sin[1 : NB + 1]
    lane = lax.broadcasted_iota(jnp.int32, (NB, HALF), 1)
    real_edge = edge_cos[0] + edge_sin[1]
    imag_edge = edge_cos[1] - edge_sin[0]
    real_far = jnp.where(lane == 0, real_edge, next_cos[:, :HALF] - next_sin[:, HALF:])
    imag_far = jnp.where(lane == 0, imag_edge, -next_cos[:, HALF:] - next_sin[:, :HALF])
    white_far = wm_ref[...]
    order = q_ref[...]
    real_far = dot_nn((real_far * white_far).astype(jnp.bfloat16), order).astype(jnp.bfloat16)
    imag_far = dot_nn((imag_far * white_far).astype(jnp.bfloat16), order).astype(jnp.bfloat16)
    rows = NB // parts
    for f in range(parts):
        here = slice(f * rows, (f + 1) * rows)
        out_ref[f, 0, 0, :, :HALF] = real_out[here]
        out_ref[f, 0, 0, :, HALF:] = real_far[here]
        out_ref[f, 0, 1, :, :HALF] = imag_out[here]
        out_ref[f, 0, 1, :, HALF:] = imag_far[here]


def second_section(received, tables, white, white_far):
    parts, segs, rows, width = received.shape
    twists, seconds, order = tables

    def whole(array):
        return pl.BlockSpec(array.shape, lambda i: (0,) * array.ndim)

    fixed = (*twists, *seconds, white, white_far, order)
    return pl.pallas_call(
        second_kernel,
        grid=(segs,),
        in_specs=[pl.BlockSpec((parts, 1, rows, width), lambda i: (0, i, 0, 0))]
        + [whole(array) for array in fixed],
        out_specs=pl.BlockSpec((parts, 1, 2, NB // parts, A), lambda i: (0, i, 0, 0, 0)),
        out_shape=jax.ShapeDtypeStruct((parts, segs, 2, NB // parts, A), jnp.bfloat16),
        compiler_params=pltpu.CompilerParams(vmem_limit_bytes=60 * 2**20),
        cost_estimate=pl.CostEstimate(
            flops=2 * 6 * segs * 528 * B * A, bytes_accessed=segs * A * B * 6, transcendentals=0
        ),
        name="second_section",
    )(received, *fixed)


def lag_kernel(place_ref, a_ref, b_ref, x_ref, y_ref, t_ref, c_ref, s_ref, out_ref, acc_ref, even_ref, odd_ref):
    sources = (a_ref, b_ref, x_ref, y_ref)
    segs = a_ref.shape[1] // 2
    per_quad = t_ref.shape[0]
    lag_total = c_ref.shape[2]
    tmpl = out_ref.shape[2]
    step = pl.program_id(0)
    last = pl.num_programs(0) - 1
    seg_total = len(sources) * segs
    half = seg_total * lag_total

    def make_rows(rows_ref, jj, chunk):
        lanes = slice(chunk * 128, (chunk + 1) * 128)
        values = [source[jj, :, lanes].astype(jnp.float32) for source in sources]
        real = jnp.concatenate([value[:segs] for value in values], axis=0)
        imag = jnp.concatenate([value[segs:] for value in values], axis=0)
        batch = min(8, lag_total)
        for first in range(0, lag_total, batch):
            lags_here = range(first, first + batch)
            repeated = [pl.ds(lag, 8, stride=0) for lag in lags_here]
            factors = [(c_ref[jj, chunk, lag], s_ref[jj, chunk, lag]) for lag in repeated]
            made = []
            for once_cos, once_sin in factors:
                lag_cos = jnp.concatenate([once_cos] * (seg_total // 8), axis=0)
                lag_sin = jnp.concatenate([once_sin] * (seg_total // 8), axis=0)
                real_q = (real * lag_cos - imag * lag_sin).astype(jnp.bfloat16)
                imag_q = (real * lag_sin + imag * lag_cos).astype(jnp.bfloat16)
                made.append((real_q, imag_q))
            for lag, (real_q, imag_q) in zip(lags_here, made):
                start = lag * seg_total
                rows_ref[jj, start : start + seg_total, lanes] = real_q
                rows_ref[jj, half + start : half + start + seg_total, lanes] = imag_q

    deep = 256
    tiles = [(jj, k) for jj in range(per_quad) for k in range(A // deep)]

    def push(index):
        jj, k = tiles[index]
        for unit in range(2):
            columns = t_ref[jj, unit * tmpl : (unit + 1) * tmpl, k * deep : (k + 1) * deep]
            pltpu.matmul_push_rhs(columns, index % 2, unit, transpose=True)

    def one_group(next_ref, now_ref):
        def scoped(*sums):
            push(0)
            for index, (jj, k) in enumerate(tiles):
                if index + 1 < len(tiles):
                    push(index + 1)
                chunks = list(range(k * deep // 128, (k + 1) * deep // 128))
                for part in range(2):
                    rows = now_ref[jj, part * half : (part + 1) * half, k * deep : (k + 1) * deep]
                    for unit in range(2):
                        staged = index % 2 if part == 0 else None
                        pltpu.matmul_acc_lhs(sums[unit * 2 + part], rows, load_staged_rhs=staged)
                    if next_ref is not None:
                        make_rows(next_ref, jj, chunks[part])
            for unit in range(2):
                for part in range(2):
                    here = slice(part * half, (part + 1) * half)
                    acc_ref[unit, here] += pltpu.matmul_pop(sums[unit * 2 + part])

        shape = (half, tmpl)
        pl.run_scoped(scoped, *[pltpu.ACC(unit)(shape, jnp.float32) for unit in (0, 0, 1, 1)])

    @pl.when(step == 0)
    def _():
        acc_ref[...] = jnp.zeros_like(acc_ref)

        @pl.loop(0, per_quad)
        def _(jj):
            for chunk in range(A // 128):
                make_rows(even_ref, jj, chunk)

    @pl.when((step % 2 == 1) & (step < last))
    def _():
        one_group(odd_ref, even_ref)

    @pl.when((step % 2 == 0) & (step > 0) & (step < last))
    def _():
        one_group(even_ref, odd_ref)

    @pl.when(step == last)
    def _():
        one_group(None, odd_ref)
        by_real = acc_ref[0]
        by_imag = acc_ref[1]
        shape = (lag_total, seg_total, tmpl)
        real = by_real[:half] + by_imag[half:]
        imag = by_real[half:] - by_imag[:half]
        real = jnp.swapaxes(real.reshape(shape), 0, 1)
        imag = jnp.swapaxes(imag.reshape(shape), 0, 1)
        for index in range(len(sources)):
            here = slice(index * segs, (index + 1) * segs)
            place = pl.ds((place_ref[0] ^ index) * segs, segs)
            out_ref[place, :lag_total] = real[here]
            out_ref[place, lag_total:] = imag[here]


def lag_products(sources, place, laid, lag_cos, lag_sin):
    blocks, rows, _ = sources[0].shape
    tmpl2 = laid.shape[1]
    per_quad = min(4, blocks)
    quads = blocks // per_quad
    _, chunks, lag_total, lanes = lag_cos.shape
    segs = len(sources) * rows // 2

    def ahead(i):
        return (jnp.minimum(i, quads - 1), 0, 0)

    def ahead_lags(i):
        return (jnp.minimum(i, quads - 1), 0, 0, 0)

    return pl.pallas_call(
        lag_kernel,
        grid=(quads + 1,),
        in_specs=[pl.BlockSpec(memory_space=pltpu.SMEM)]
        + [pl.BlockSpec((per_quad, rows, A), ahead)] * len(sources)
        + [
            pl.BlockSpec((per_quad, tmpl2, A), lambda i: (jnp.maximum(i - 1, 0), 0, 0)),
            pl.BlockSpec((per_quad, chunks, lag_total, lanes), ahead_lags),
            pl.BlockSpec((per_quad, chunks, lag_total, lanes), ahead_lags),
        ],
        out_specs=pl.BlockSpec((segs, 2 * lag_total, tmpl2 // 2), lambda i: (0, 0, 0)),
        out_shape=jax.ShapeDtypeStruct((segs, 2 * lag_total, tmpl2 // 2), jnp.float32),
        scratch_shapes=[
            pltpu.VMEM((2, 2 * segs * lag_total, tmpl2 // 2), jnp.float32),
            pltpu.VMEM((per_quad, 2 * segs * lag_total, A), jnp.bfloat16),
            pltpu.VMEM((per_quad, 2 * segs * lag_total, A), jnp.bfloat16),
        ],
        compiler_params=pltpu.CompilerParams(vmem_limit_bytes=60 * 2**20),
        cost_estimate=pl.CostEstimate(
            flops=4 * segs * lag_total * tmpl2 * blocks * A,
            bytes_accessed=blocks * A * (tmpl2 * 2 + segs * 4),
            transcendentals=0,
        ),
        name="lag_products",
    )(place, *sources, laid, lag_cos, lag_sin)


def block_rows(data):
    segs, parts, blocks, _ = data.shape
    return data.transpose(2, 1, 0, 3).reshape(blocks, parts * segs, A)


def spread(data):
    moved = [lax.ppermute(data, "tmpl", [(n, n ^ bit) for n in range(4)]) for bit in (1, 2, 3)]
    return (data, *moved)


def layout_kernel(cut_ref, t_ref, *refs):
    out_ref = refs[-1]
    tmpl, _, rows, _ = t_ref.shape
    first_row = pl.program_id(0) * rows + cut_ref[cut_ref.shape[0] - 1]
    first_tmpl = pl.program_id(1) * tmpl
    row_ids = lax.broadcasted_iota(jnp.int32, (rows, 128), 0) + first_row
    batch = 16

    @pl.loop(0, tmpl // batch)
    def _(group):
        some = pl.ds(pl.multiple_of(group * batch, batch), batch)
        keeps = [row_ids < cut_ref[first_tmpl + group * batch + n] for n in range(batch)]
        for part in range(2):
            for chunk in range(A // 128):
                lanes = slice(chunk * 128, (chunk + 1) * 128)
                value = t_ref[some, part, :, lanes].astype(jnp.float32)
                value = jnp.stack([jnp.where(keeps[n], value[n], 0.0) for n in range(batch)], axis=0)
                value = jnp.swapaxes(value, 0, 1).astype(jnp.bfloat16)
                for row in range(rows):
                    out_ref[row, part, some, lanes] = value[row]


def lay_out(templates, cuts, piece, pieces, laid):
    tmpl, _, blocks, _ = templates.shape
    rows = min(16, blocks)
    steps = blocks // rows // pieces
    batch = min(64, tmpl)
    shape = (blocks, 2, tmpl, A)
    first = piece * steps
    info = jnp.concatenate([cuts, jnp.full((1,), first * rows, jnp.int32)])
    earlier = () if laid is None else (laid,)
    return pl.pallas_call(
        layout_kernel,
        grid=(steps, tmpl // batch),
        in_specs=[
            pl.BlockSpec(memory_space=pltpu.SMEM),
            pl.BlockSpec((batch, 2, rows, A), lambda i, j: (j, 0, i + first, 0)),
        ]
        + [pl.BlockSpec(memory_space=pl.ANY)] * len(earlier),
        out_specs=pl.BlockSpec((rows, 2, batch, A), lambda i, j: (i + first, 0, j, 0)),
        out_shape=jax.ShapeDtypeStruct(shape, jnp.bfloat16),
        input_output_aliases={2: 0} if earlier else {},
        compiler_params=pltpu.CompilerParams(vmem_limit_bytes=40 * 2**20),
        cost_estimate=pl.CostEstimate(
            flops=0, bytes_accessed=8 * tmpl * 2 * blocks * A // pieces, transcendentals=0
        ),
        name="lay_out",
    )(info, templates, *earlier)


def general_transform(strain, psd):
    freq_count = lax.axis_size("freq")
    freq_index = lax.axis_index("freq")
    seg_local = strain.shape[0]
    step_time = B // freq_count
    highest = lax.Precision.HIGHEST
    first_cos, first_sin = cos_sin_table(
        jnp.arange(A, dtype=jnp.int32), jnp.arange(A, dtype=jnp.int32), A
    )
    table = jnp.concatenate([first_cos, -first_sin], axis=0)
    time_ids = freq_index * step_time + jnp.arange(step_time, dtype=jnp.int32)
    twist_cos, twist_sin = cos_sin_table(jnp.arange(A, dtype=jnp.int32), time_ids, LEN)
    slab_blocks = strain.reshape(seg_local, A // freq_count, B)
    both_parts = jnp.einsum(
        "kn,snb->skb",
        table,
        lax.all_to_all(slab_blocks, "freq", split_axis=2, concat_axis=1, tiled=True),
        precision=highest,
    )
    real_part = both_parts[:, :A]
    imag_part = both_parts[:, A:]
    second_cos, second_sin = cos_sin_table(
        jnp.arange(B, dtype=jnp.int32), jnp.arange(NB, dtype=jnp.int32), B
    )
    rotation = jnp.concatenate(
        [
            jnp.concatenate([second_cos, -second_sin], axis=1),
            jnp.concatenate([second_sin, second_cos], axis=1),
        ],
        axis=0,
    )
    amplitude = jnp.sqrt(LEN * psd)
    real_in = lax.all_to_all(
        real_part * twist_cos + imag_part * twist_sin, "freq", split_axis=1, concat_axis=2, tiled=True
    )
    imag_in = lax.all_to_all(
        imag_part * twist_cos - real_part * twist_sin, "freq", split_axis=1, concat_axis=2, tiled=True
    )
    joined = jnp.concatenate([real_in, imag_in], axis=2)
    both_out = jnp.einsum("spc,cm->smp", joined, rotation, precision=highest)
    both_out = both_out.reshape(joined.shape[0], 2, NB, joined.shape[1])
    whitened = (both_out / amplitude).astype(jnp.bfloat16)
    return lax.all_to_all(whitened, "freq", split_axis=2, concat_axis=3, tiled=True)


def exchange(sent):
    return lax.all_to_all(sent, "freq", split_axis=0, concat_axis=0, tiled=True)


def pack_strain(strain, freq_count):
    seg_local = strain.shape[0]
    sent = (strain * STRAIN_SCALE).astype(jnp.float16)
    sent = sent.reshape(seg_local, A // freq_count, freq_count, B // freq_count)
    return sent.transpose(2, 0, 1, 3)


def pack_coefs(received, table):
    freq_count, seg_local, _, width = received.shape
    coefs = first_section(received.astype(jnp.float32) * (1.0 / STRAIN_SCALE), table)
    sent = (coefs * COEF_SCALE).astype(jnp.float16)
    return sent.reshape(freq_count, seg_local // freq_count, A, width)


def whiten(received, tables, white, white_far):
    return second_section(received.astype(jnp.float32) * (1.0 / COEF_SCALE), tables, white, white_far)


def on_device(strain, psd, templates, cutoffs, lags):
    freq_count = lax.axis_size("freq")
    freq_index = lax.axis_index("freq")
    seg_local = strain.shape[0]
    tmpl_local = templates.shape[0]
    blocks_here = templates.shape[2]
    first_block = freq_index * blocks_here
    block_ids = first_block + jnp.arange(blocks_here, dtype=jnp.int32)
    cuts = cutoffs - first_block
    tied = lax.optimization_barrier

    block_cos, block_sin = cos_sin_table(block_ids, lags % B, B)
    position = jnp.arange(A, dtype=jnp.int32).reshape(A // 128, 1, 128)
    place = lags[None, :, None] * position % LEN
    place_angle = place.astype(jnp.float32) * (two_pi / LEN)
    place_cos = jnp.cos(place_angle)[None]
    place_sin = jnp.sin(place_angle)[None]
    block_cos = block_cos[:, None, :, None]
    block_sin = block_sin[:, None, :, None]
    lag_cos = block_cos * place_cos - block_sin * place_sin
    lag_sin = block_sin * place_cos + block_cos * place_sin

    sliced = (
        lax.axis_size("tmpl") == 4
        and seg_local == 2 * freq_count == 16
        and (NB // freq_count) % 32 == 0
        and B // freq_count == 128
    )
    if not sliced:
        laid = lay_out(templates, cuts, 0, 1, None)
        laid = laid.reshape(blocks_here, 2 * tmpl_local, A)
        data = lax.all_gather(general_transform(strain, psd), "tmpl", axis=0, tiled=True)
        origin = jnp.zeros((1,), jnp.int32)
        sums = []
        for start in range(0, data.shape[0], 16):
            sources = [block_rows(data[n : n + 4]) for n in range(start, start + 16, 4)]
            sums.append(lag_products(sources, origin, laid, lag_cos, lag_sin))
        sums = jnp.concatenate(sums, axis=0)
        return lax.psum_scatter(sums, "freq", scatter_dimension=0, tiled=True)

    order = mirror_table()
    psd_all = lax.all_gather(psd, "freq", axis=1, tiled=True)
    psd_far = jnp.dot(psd_all[:, HALF:], order.T, precision=lax.Precision.HIGHEST)
    white = lax.rsqrt(LEN * psd_all[:, :HALF])
    white_far = lax.rsqrt(LEN * psd_far)
    first = first_table()
    second = (twist_tables(), second_tables(), order.astype(ml_dtypes.bfloat16))

    seg_out = seg_local * lax.axis_size("tmpl") // freq_count
    by_owner = strain.reshape(seg_local // seg_out, 2, seg_out // 2, strain.shape[1])
    strain_a, strain_b = (
        pack_strain(by_owner[:, group].reshape(seg_local // 2, strain.shape[1]), freq_count)
        for group in range(2)
    )
    time_a = exchange(strain_a)
    laid = lay_out(templates, cuts, 0, 2, None)
    time_a, laid, strain_b = tied((time_a, laid, strain_b))
    coefs_a = pack_coefs(time_a, first)
    parts_a = exchange(coefs_a)
    parts_a, strain_b, white, white_far, lag_cos, lag_sin = tied(
        (parts_a, strain_b, white, white_far, lag_cos, lag_sin)
    )
    time_b = exchange(strain_b)
    white_a = whiten(parts_a, second, white, white_far)
    time_b, white_a = tied((time_b, white_a))
    data_a = exchange(white_a)
    coefs_b = pack_coefs(time_b, first)
    laid = lay_out(templates, cuts, 1, 2, laid)
    data_a, coefs_b, laid = tied((data_a, coefs_b, laid))
    parts_b = exchange(coefs_b)
    laid = laid.reshape(blocks_here, 2 * tmpl_local, A)
    place = lax.axis_index("tmpl").astype(jnp.int32).reshape(1)

    def halves(data):
        data = data.reshape(2, 2, 2, 2, blocks_here, A)
        return [block_rows(data[:, n].reshape(4, 2, blocks_here, A)) for n in range(2)]

    def products(part):
        return lag_products(part, place, laid, lag_cos, lag_sin)

    def collect(sums):
        return lax.psum_scatter(sums, "freq", scatter_dimension=0, tiled=True)

    def collect_late(sums):
        shares = exchange(sums.reshape(freq_count, 2, 2 * lags.shape[0], tmpl_local))
        return jnp.sum(shares, axis=0)

    first_a, second_a = halves(data_a)
    first_a = spread(first_a)
    parts_b, first_a, second_a = tied((parts_b, first_a, second_a))
    second_a = spread(second_a)
    data_b = exchange(whiten(parts_b, second, white, white_far))
    sums_a1 = products(first_a)
    data_b, second_a, sums_a1 = tied((data_b, second_a, sums_a1))
    first_b, second_b = halves(data_b)
    first_b = spread(first_b)
    out_a1 = collect(sums_a1)
    sums_a2 = products(second_a)
    first_b, second_b, sums_a2 = tied((first_b, second_b, sums_a2))
    second_b = spread(second_b)
    out_a2 = collect(sums_a2)
    sums_b1 = products(first_b)
    second_b, sums_b1 = tied((second_b, sums_b1))
    out_b1 = collect(sums_b1)
    sums_b2 = products(second_b)
    out_a1, out_a2, sums_b2 = tied((out_a1, out_a2, sums_b2))
    out_b2 = collect_late(sums_b2)
    return jnp.concatenate([out_a1, out_a2, out_b1, out_b2], axis=0)


def solution(mesh):
    placed = (P("tmpl", "freq"), P(None, "freq"), P("tmpl", None, "freq", None), P("tmpl"), P())
    return jax.shard_map(
        on_device, mesh=mesh, in_specs=placed, out_specs=P("freq", None, "tmpl"), check_vma=False
    )
```
